512 devices in a mesh: passage: 32 (over x, y), sub: 16 (over z, core).
Axes of the slice: x: 4, y: 8, z: 8, core: 2. Of those that a mesh axis runs over, the one named last changes fastest.
Arguments:
- block_vectors: float32 [32, 131072], P(None, ('passage', 'sub')), may hold values from -75 to 75
- stiffness: float32 [131072], P(('passage', 'sub')), may hold values from 2 to 8
- mass_diag: float32 [131072], P(('passage', 'sub')), may hold values from 0.5 to 2
- kblocks: float32 [1024, 4, 128, 128], P(('passage', 'sub')), may hold values from -0.25 to 0.25
- block_cols: int32 [1024, 4], P(('passage', 'sub')), may hold values from 0 to 5
- slot_node: int32 [524288], P(('passage', 'sub')), may hold values from 0 to 255
- slot_owner: int32 [524288, 1], P(('passage', 'sub')), may hold values from 0 to 15; in each aligned block of 1024 rows (0 to 1023, 1024 to 2047, ...) at most 128 rows name the same one
- slot_cell: int32 [524288], P(('passage', 'sub')), may hold values from 0 to 8191
- slot_weight: float32 [524288], P(('passage', 'sub')), may hold values from 0.5 to 4
- live_slots: int32 [512], P(('passage', 'sub')), may hold values from 768 to 1024, as said below
Outputs:
- residual: float32 [32, 131072], P(None, ('passage', 'sub'))
- gram_stiff: float32 [64, 64], replicated
- gram_plain: float32 [64, 64], replicated
The draws below stay inside these ranges and needn't reach their ends.
Inputs may be any that keep to these rules, and one draw needn't show every extreme that they name: `slot_owner`: per device at most 128 slots name the same owner, and some device reaches 128 for some owner. `live_slots`: some device has all 1024 slots live.
All inputs are finite; a program needn't handle non-finite values.
Results may differ from the reference program's by a relative error of at most 0.00019.
Values sent between devices are 32-bit elements; how exact they have to be, the bound alone decides.
A program may use at most 64 MiB of HBM per device.

```python
import math
import jax
import jax.numpy as jnp
import numpy as np
from jax import lax

M = 32
BS = 128
NB = 4
RB = 2
NI = 1024
CX = 8
CY = 8
CZ = 128
NSD = 256
NSG = 131072
NI_ALL = 524288
CAP = 128
N_PASSAGE = 32
N_SUB = 16


def draw_block_vectors(key, part):
    key_base, key_scale = jax.random.split(key, 2)
    mode_scale = 0.5 * jnp.exp(jax.random.uniform(key_scale, (M, 1), jnp.float32, 0.0, math.log(10.0)))
    rising = jnp.exp(math.log(3.0) * jnp.arange(NSG, dtype=jnp.float32) / NSG)[None, :]
    base = jnp.clip(jax.random.normal(key_base, (M, NSG), jnp.float32), -5.0, 5.0)
    return (base * mode_scale * rising).astype(jnp.float32)


def draw_live_slots(key, part):
    devices_all = NSG // NSD
    key_counts, key_choice = jax.random.split(key)
    drawn_counts = jax.random.randint(key_counts, (devices_all,), 3 * NI // 4, NI + 1)
    chosen_one = jax.random.randint(key_choice, (), 0, devices_all)
    return jnp.where(jnp.arange(devices_all) == chosen_one, NI, drawn_counts).astype(jnp.int32)


def place_ends(values, own_key, low, top_value):
    extent = values.shape
    place = [jax.random.randint(jax.random.fold_in(own_key, axis), (), 0, extent[axis]) for axis in range(len(extent))]
    values = values.at[tuple(place)].set(low)
    longest = extent.index(max(extent))
    place[longest] = (place[longest] + 1) % extent[longest]
    return values.at[tuple(place)].set(top_value)


def block_scale(own_key, dims, cuts, smallest, high):
    def one(dim, shards_of):
        heights = jax.random.uniform(jax.random.fold_in(jax.random.fold_in(own_key, 6), dim), (shards_of,), jnp.float32, smallest / len(cuts), high / len(cuts))
        return jnp.repeat(jnp.exp(heights), dims[dim] // shards_of).reshape((-1,) + (1,) * (len(dims) - dim - 1))

    gain = one(*cuts[0])
    for cut in cuts[1:]:
        gain = gain * one(*cut)
    return gain


def assign_block(key, own, number, rows, count, top, limit, slope):
    sequence = jax.random.permutation(key, count)
    crowded, usual = portions_of(count, rows * top, limit, slope, True), portions_of(count, rows * top, limit, slope, False)
    places = jnp.arange(count)

    def named(lengths, rotation):
        used = int((lengths > 0).sum())
        fixed = max(1, used // 4)
        moved = fixed + (places - fixed + rotation * (used - fixed)) % max(1, count - fixed)
        return jnp.zeros((count,), jnp.int32).at[sequence[jnp.where(places < fixed, places, moved)]].set(jnp.asarray(lengths, jnp.int32))

    lengths = jnp.where(number % 4 == 0, named(crowded, number // 4), named(usual, number - number // 4 - 1))
    mixed = jax.random.permutation(jax.random.fold_in(own, 3), count)
    donor, taker = mixed[0:count // 2 * 2:2], mixed[1:count // 2 * 2:2]
    room = jnp.minimum(lengths[donor] - 1, limit - lengths[taker]) // 2
    room = jnp.where((donor == sequence[0]) | (taker == sequence[0]) | (lengths[taker] == 0), 0, jnp.maximum(room, 0))
    moved = jax.random.randint(jax.random.fold_in(own, 4), (count // 2,), 0, 1 << 20) % (room + 1)
    lengths = lengths.at[donor].add(-moved).at[taker].add(moved)
    items = jnp.searchsorted(jnp.cumsum(lengths), jnp.arange(rows * top), side="right").astype(jnp.int32)
    listing = items.reshape(top, rows).T
    listing = listing[jax.random.permutation(jax.random.fold_in(own, 1), rows)]
    rotation = jax.random.randint(jax.random.fold_in(own, 2), (rows, 1), 0, top)
    return jnp.take_along_axis(listing, (jnp.arange(top)[None, :] + rotation) % top, axis=1)


def portions_of(amount, total, limit, skew, full):
    weights = [(1 << 20) // math.isqrt(standing ** skew) + 1 for standing in range(1, amount + 1)]
    largest = limit if full else min(limit, max(-(-total // amount), total * weights[0] // sum(weights)))
    least = 1 if total - largest >= amount - 1 else 0
    holding, rest = [largest] + [least] * (amount - 1), total - largest - least * (amount - 1)
    while rest > 0:
        candidates = [i for i in range(1, amount) if holding[i] < largest] or [i for i in range(1, amount) if holding[i] < limit]
        mass, left = sum([weights[i] for i in candidates]), rest
        for i in candidates:
            more = min(limit - holding[i], max(1, left * weights[i] // mass), rest)
            holding[i] = holding[i] + more
            rest = rest - more
    return np.array(holding)


def centred(key, shape, deviation, most, cuts=(), kind=jnp.bfloat16):
    array = jax.random.normal(key, shape, jnp.float32) * deviation
    if len(cuts) > 0:
        array = block_scale(key, shape, cuts, -0.22, 0.18) * array
    return jnp.clip(array, min=-most, max=most).astype(kind)


def setup_inputs(seed: int = 0) -> dict:
    keys = jax.random.split(jax.random.key(seed), 11)
    block_vectors = draw_block_vectors(jax.random.fold_in(keys[10], 71), 0)
    stiffness = jnp.clip(jnp.exp(math.log(8.0) - 1.3862944 * jax.random.uniform(keys[1], (NSG,), jnp.float32) ** block_scale(keys[1], (NSG,), ((0, 512),), -0.2, 0.2)), 2.0, 8.0)
    mass_diag = jnp.clip(jnp.exp(math.log(2.0) - 1.3862944 * jax.random.uniform(keys[2], (NSG,), jnp.float32) ** block_scale(keys[2], (NSG,), ((0, 512),), -0.2, 0.2)), 0.5, 2.0)
    kblocks = centred(keys[3], (RB * N_PASSAGE * N_SUB, NB, BS, BS), (NB * BS) ** -0.5, 0.25, ((0, 512),), jnp.float32)
    block_cols = place_ends(jax.random.randint(keys[4], (RB * N_PASSAGE * N_SUB, NB), 0, 3 * RB), jax.random.fold_in(keys[4], 1), 0, (3 * RB) - 1).astype(jnp.int32)
    slot_node = place_ends(jax.random.randint(keys[5], (NI_ALL,), 0, NSD), jax.random.fold_in(keys[5], 1), 0, NSD - 1).astype(jnp.int32)
    slot_owner_keys = jax.random.split(jax.random.fold_in(keys[6], 1), NI_ALL // NI)
    slot_owner_turns = jax.random.permutation(jax.random.fold_in(keys[6], 3), NI_ALL // NI)
    slot_owner = jax.vmap(lambda own, number: assign_block(jax.random.fold_in(keys[6], 2), own, number, NI, N_SUB, 1, CAP, 2))(slot_owner_keys, slot_owner_turns).reshape((NI_ALL, 1))
    slot_cell = place_ends(jax.random.randint(keys[7], (NI_ALL,), 0, CX * CY * CZ), jax.random.fold_in(keys[7], 1), 0, (CX * CY * CZ) - 1).astype(jnp.int32)
    slot_weight = jnp.clip(jnp.exp(math.log(4.0) - 2.0794415 * jax.random.uniform(keys[8], (NI_ALL,), jnp.float32) ** block_scale(keys[8], (NI_ALL,), ((0, 512),), -0.2, 0.2)), 0.5, 4.0)
    live_slots = draw_live_slots(jax.random.fold_in(keys[10], 71), 0)
    return {"block_vectors": block_vectors, "stiffness": stiffness, "mass_diag": mass_diag, "kblocks": kblocks, "block_cols": block_cols, "slot_node": slot_node, "slot_owner": slot_owner, "slot_cell": slot_cell, "slot_weight": slot_weight, "live_slots": live_slots}


center_weight = 15.0
lower_bound = 1.0 / 15.0
upper_bound = 17.0 / 15.0
middle = (upper_bound + lower_bound) / 2.0
radius = (upper_bound - lower_bound) / 2.0
sigma_ratio = middle / radius
first_rho = 1.0 / sigma_ratio
second_rho = 1.0 / (2.0 * sigma_ratio - first_rho)
third_rho = 1.0 / (2.0 * sigma_ratio - second_rho)


def laplace_inner(padded):
    rows_one = padded.shape[1] - 2
    rows_two = padded.shape[2] - 2
    depth = padded.shape[3]
    zpadded = jnp.pad(padded, ((0, 0), (0, 0), (0, 0), (1, 1)))
    neighbours = jnp.zeros((padded.shape[0], rows_one, rows_two, depth), jnp.float32)
    for offset_one in range(3):
        for offset_two in range(3):
            for offset_three in range(3):
                distance = abs(offset_one - 1) + abs(offset_two - 1) + abs(offset_three - 1)
                if distance == 0:
                    continue
                weight = 0.5 ** (distance - 1)
                neighbours = neighbours + weight * zpadded[:, offset_one:offset_one + rows_one, offset_two:offset_two + rows_two, offset_three:offset_three + depth]
    return center_weight * padded[:, 1:-1, 1:-1, :] - neighbours


def extend_field(field):
    looped = jnp.concatenate([field[-1:], field, field[:1]], axis=0)
    return jnp.pad(looped, ((0, 0), (1, 1), (0, 0)))[None]


def chebyshev(source):
    first = source / (center_weight * middle)
    resid = source - laplace_inner(extend_field(first))[0]
    second_step = second_rho * first_rho * first + (2.0 * second_rho / radius) * (resid / center_weight)
    second = first + second_step
    resid = source - laplace_inner(extend_field(second))[0]
    third_step = third_rho * second_rho * second_step + (2.0 * third_rho / radius) * (resid / center_weight)
    return second + third_step


def apply_stiffness(field, block_cols, kblocks, stiffness):
    width = field.shape[0]
    total_blocks = block_cols.shape[0]
    blocks = field.reshape(width, total_blocks, BS)
    row_ids = jnp.arange(total_blocks, dtype=jnp.int32)[:, None]
    device = row_ids // RB
    sub_pos = device % N_SUB
    offset = block_cols // RB - 1
    valid = (sub_pos + offset >= 0) & (sub_pos + offset < N_SUB)
    source = jnp.where(valid, device * RB + block_cols - RB, 0).astype(jnp.int32)
    window = blocks[:, source] * valid[None, :, :, None].astype(jnp.float32)
    mixed = jnp.einsum("mrnb,rnbk->mrk", window, kblocks, precision=lax.Precision.HIGHEST)
    return stiffness[None, :] * field + mixed.reshape(width, -1)


def inner(left, right):
    return lax.dot_general(left, right, (((1,), (1,)), ((), ())), precision=lax.Precision.HIGHEST, preferred_element_type=jnp.float32)


def reference(block_vectors, stiffness, mass_diag, kblocks, block_cols, slot_node, slot_owner, slot_cell, slot_weight, live_slots):
    total = block_vectors.shape[1]
    slot_ids = jnp.arange(slot_node.shape[0], dtype=jnp.int32)
    device = slot_ids // NI
    passage = device // N_SUB
    live = (slot_ids % NI < live_slots[device]).astype(jnp.float32)
    scaled = slot_weight * live
    column = (device * (RB * BS) + slot_node).astype(jnp.int32)
    cell_one = slot_cell // (CY * CZ)
    cell_two = (slot_cell // CZ) % CY
    cell_three = slot_cell % CZ
    flat = (((passage * CX + cell_one) * (CY * N_SUB) + slot_owner[:, 0] * CY + cell_two) * CZ + cell_three).astype(jnp.int32)
    cells_all = CX * N_PASSAGE * CY * N_SUB * CZ

    def added_force(mode_row):
        source = jnp.zeros((cells_all,), jnp.float32).at[flat].add(mode_row[column] * scaled)
        press = chebyshev(source.reshape(CX * N_PASSAGE, CY * N_SUB, CZ)).reshape(-1)
        return jnp.zeros((total,), jnp.float32).at[column].add(press[flat] * scaled)

    stiff_image = apply_stiffness(block_vectors, block_cols, kblocks, stiffness)
    mass_image = mass_diag[None, :] * block_vectors + lax.map(added_force, block_vectors)
    theta = jnp.sum(block_vectors * stiff_image, axis=1) / jnp.sum(block_vectors * mass_image, axis=1)
    residual = stiff_image - theta[:, None] * mass_image
    stiff_resid = apply_stiffness(residual, block_cols, kblocks, stiffness)
    search = jnp.concatenate([block_vectors, residual], axis=0)
    image = jnp.concatenate([stiff_image, stiff_resid], axis=0)
    gram_stiff = inner(search, image) / total
    gram_plain = inner(search, search) / total
    return residual, gram_stiff, gram_plain
```

```python
import functools

import jax
import jax.numpy as jnp
from jax import lax
from jax.experimental import pallas as pl
from jax.experimental.pallas import tpu as pltpu
from jax.sharding import PartitionSpec as P

MESH = pl.DeviceIdType.MESH
F32 = jnp.float32
BF16 = jnp.bfloat16
I32 = jnp.int32

M = 32
CX = 8
CY = 8
CZ = 128
CAP = 128
NSD = 256

center_weight = 15.0
lower_bound = 1.0 / 15.0
upper_bound = 17.0 / 15.0
middle = (upper_bound + lower_bound) / 2.0
radius = (upper_bound - lower_bound) / 2.0
sigma_ratio = middle / radius
first_rho = 1.0 / sigma_ratio
second_rho = 1.0 / (2.0 * sigma_ratio - first_rho)
third_rho = 1.0 / (2.0 * sigma_ratio - second_rho)
FIRST = 1.0 / (center_weight * middle)
GAIN_TWO = 2.0 * second_rho / radius / center_weight
GAIN_THREE = 2.0 * third_rho / radius / center_weight
STEP_ONE = second_rho * first_rho * FIRST + GAIN_TWO * (1.0 - 17.0 * FIRST)
STEP_T = GAIN_TWO * 2.0 * FIRST
ALPHA = FIRST + STEP_ONE + third_rho * second_rho * STEP_ONE + GAIN_THREE * (1.0 - 17.0 * (FIRST + STEP_ONE))
BETA = STEP_T + third_rho * second_rho * STEP_T + GAIN_THREE * (2.0 * (FIRST + STEP_ONE) - 17.0 * STEP_T)
GAMMA = GAIN_THREE * 2.0 * STEP_T


def iota(shape, dim):
    return lax.broadcasted_iota(I32, shape, dim)


def nn(left, right):
    return jnp.dot(left, right, preferred_element_type=F32)


def nt(left, right):
    return lax.dot_general(left, right, (((1,), (1,)), ((), ())), preferred_element_type=F32)


def two(x):
    high = x.astype(BF16)
    return high, (x - high.astype(F32)).astype(BF16)


def three(x):
    high, rest = x.astype(BF16), None
    rest = x - high.astype(F32)
    middle_part = rest.astype(BF16)
    return high, middle_part, (rest - middle_part.astype(F32)).astype(BF16)


def kernel(
    n_passage,
    n_sub,
    v_ref,
    stiff_ref,
    mass_ref,
    kb_ref,
    cols_ref,
    node_ref,
    owner_ref,
    cell_ref,
    weight_ref,
    live_ref,
    resid_ref,
    gs_ref,
    gp_ref,
    win_v,
    win_s,
    win_w,
    kbh,
    kbl,
    mt,
    mt_in,
    n2,
    out,
    inc,
    rhot,
    s,
    xl,
    xr,
    pp,
    qq,
    ysl,
    ysr,
    yl,
    yr,
    fp,
    ret,
    back,
    gbuf,
    grecv,
    part,
    precv,
    gfull,
    nb_send,
    nb_recv,
    mt_send,
    mt_recv,
    a_send,
    a_recv,
    x_send,
    x_recv,
    y_send,
    y_recv,
    b_send,
    b_recv,
    g_send,
    g_recv,
    p_send,
    p_recv,
    f_send,
    f_recv,
):
    chips = n_sub // 2
    ni = node_ref.shape[0] * 128
    nc = node_ref.shape[0]
    rows = 128 // n_sub
    myp = lax.axis_index("passage")
    me = lax.axis_index("sub")
    chip = me // 2
    left_p = lax.rem(myp + n_passage - 1, n_passage)
    right_p = lax.rem(myp + 1, n_passage)
    has_left = me > 0
    has_right = me < n_sub - 1

    def sub_copy(src, dst, send, recv, peer):
        return pltpu.make_async_remote_copy(
            src_ref=src, dst_ref=dst, send_sem=send, recv_sem=recv,
            device_id={"sub": peer}, device_id_type=MESH,
        )

    def passage_copy(src, dst, send, recv, peer):
        return pltpu.make_async_remote_copy(
            src_ref=src, dst_ref=dst, send_sem=send, recv_sem=recv,
            device_id={"passage": peer}, device_id_type=MESH,
        )

    for win in (win_v, win_s, win_w):
        win[0:2] = jnp.zeros((2, M, 128), F32)
        win[4:6] = jnp.zeros((2, M, 128), F32)

    @pl.when(jnp.logical_not(has_left))
    def _():
        yl[...] = jnp.zeros_like(yl)

    @pl.when(jnp.logical_not(has_right))
    def _():
        yr[...] = jnp.zeros_like(yr)

    barrier = pltpu.get_barrier_semaphore()

    def greet_sub(i, carry):
        pl.semaphore_signal(barrier, inc=1, device_id={"sub": lax.rem(me + i, n_sub)}, device_id_type=MESH)
        return carry

    def greet_passage(i, carry):
        pl.semaphore_signal(barrier, inc=1, device_id={"passage": lax.rem(myp + i, n_passage)}, device_id_type=MESH)
        return carry

    lax.fori_loop(1, n_sub, greet_sub, 0)
    lax.fori_loop(1, n_passage, greet_passage, 0)

    v = v_ref[...]
    win_v[2] = v[:, :128]
    win_v[3] = v[:, 128:]

    owner = owner_ref[...]
    lane_of_slot = iota((1, ni), 1)

    def flat(x):
        return jnp.concatenate([x[c : c + 1, :] for c in range(nc)], axis=1)

    group = iota((n_sub, 128), 0)
    hot = [(owner[c : c + 1, :] == group).astype(F32) for c in range(nc)]
    upper = (iota((128, 128), 0) < iota((128, 128), 1)).astype(F32).astype(BF16)
    before = nn(jnp.concatenate(hot, axis=0).astype(BF16), upper)
    ahead = jnp.zeros((n_sub, 1), F32)
    ranks = []
    for c in range(nc):
        ranks.append(jnp.sum(hot[c] * (before[c * n_sub : (c + 1) * n_sub] + ahead), axis=0, keepdims=True))
        ahead = ahead + jnp.sum(hot[c], axis=1, keepdims=True)
    rank = jnp.concatenate(ranks, axis=1).astype(I32)
    rank_hot = (iota((CAP, ni), 0) == rank).astype(F32).astype(BF16)
    node = flat(node_ref[...]).astype(F32)
    cell = flat(cell_ref[...])
    weight = jnp.where(lane_of_slot < live_ref[0], flat(weight_ref[...]), 0.0)
    w0, w1, w2 = three(weight)
    which = iota((8, ni), 0)
    meta = jnp.zeros((8, ni), F32)
    for row, values in enumerate(
        (((cell >> 7) << 7).astype(F32), (cell & 127).astype(F32), node, w0.astype(F32), w1.astype(F32), w2.astype(F32))
    ):
        meta = jnp.where(which == row, values, meta)
    owner_row = flat(owner)
    lhs = jnp.concatenate([jnp.where(owner_row == g, meta, 0.0) for g in range(n_sub)], axis=0).astype(BF16)
    placed = nt(lhs, rank_hot)
    for g in range(n_sub):
        mt[g] = placed[g * 8 : (g + 1) * 8]

    pl.semaphore_wait(barrier, n_sub - 1 + n_passage - 1)

    def exchange(win, k):
        to_right = sub_copy(win.at[pl.ds(2, 2)], win.at[pl.ds(0, 2)], nb_send.at[k, 0], nb_recv.at[k, 0], me + 1)
        to_left = sub_copy(win.at[pl.ds(2, 2)], win.at[pl.ds(4, 2)], nb_send.at[k, 1], nb_recv.at[k, 1], me - 1)

        def start():
            pl.when(has_right)(to_right.start)
            pl.when(has_left)(to_left.start)

        def arrive():
            pl.when(has_left)(to_right.wait_recv)
            pl.when(has_right)(to_left.wait_recv)

        def sent():
            pl.when(has_right)(to_right.wait_send)
            pl.when(has_left)(to_left.wait_send)

        return start, arrive, sent

    v_start, v_arrive, v_sent = exchange(win_v, 0)
    s_start, s_arrive, s_sent = exchange(win_s, 1)
    w_start, w_arrive, w_sent = exchange(win_w, 2)

    def meta_copy(peer, slot):
        return sub_copy(mt.at[peer], mt_in.at[slot], mt_send.at[peer], mt_recv.at[slot], peer)

    def out_copy(peer, slot):
        return sub_copy(out.at[peer], inc.at[slot], a_send.at[peer], a_recv.at[slot], peer)

    def back_copy(peer, slot):
        return sub_copy(ret.at[peer], back.at[slot], b_send.at[peer], b_recv.at[slot], peer)

    def gram_copy(peer, slot):
        return sub_copy(gbuf.at[peer], grecv.at[slot], g_send.at[peer], g_recv.at[slot], peer)

    def full_copy(peer, slot):
        return sub_copy(part.at[1], gfull.at[slot], f_send.at[peer], f_recv.at[slot], peer)

    def part_copy(peer, slot):
        return passage_copy(part.at[0], precv.at[slot], p_send.at[peer], p_recv.at[slot], peer)

    def each_sub(act):
        def step(i, carry):
            act(lax.rem(me + i, n_sub))
            return carry

        lax.fori_loop(1, n_sub, step, 0)

    def each_passage(act):
        def step(i, carry):
            act(lax.rem(myp + i, n_passage))
            return carry

        lax.fori_loop(1, n_passage, step, 0)

    each_sub(lambda peer: meta_copy(peer, me).start())
    v_start()

    v3 = jnp.concatenate(three(v), axis=0)
    node_of = iota((NSD, 128), 0)

    def weight_row(g):
        return mt[g, 3:4, :] + mt[g, 4:5, :] + mt[g, 5:6, :]

    def send_step(t, carry):
        there = lax.rem(chip + 1 + t, chips)
        parts = [(node_of == mt[2 * there + core, 2:3, :].astype(I32)).astype(F32) for core in range(2)]
        one_hot = jnp.concatenate(parts, axis=1).astype(BF16)
        n2[there] = one_hot
        picked = nn(v3, one_hot)
        picked = picked[0:M] + picked[M : 2 * M] + picked[2 * M :]
        for core in range(2):
            g = 2 * there + core
            out[g] = picked[:, core * 128 : (core + 1) * 128] * weight_row(g)
            pl.when(g != me)(out_copy(g, me).start)
        return carry

    lax.fori_loop(0, chips, send_step, 0)
    inc[me] = out[me]
    mt_in[me] = mt[me]

    for r in range(2):
        kb = kb_ref[r]
        high, low = two(kb)
        kbh[r] = high
        kbl[r] = low

    stiff = stiff_ref[...]

    def apply(win, own):
        mixed = []
        for r in range(2):
            blocks = jnp.concatenate([win[cols_ref[r, n]] for n in range(4)], axis=1)
            high, low = two(blocks)
            both = nn(jnp.concatenate([high, low], axis=0), kbh[r])
            mixed.append(both[:M] + both[M:] + nn(high, kbl[r]))
        return stiff * own + jnp.concatenate(mixed, axis=1)

    v_arrive()
    image = apply(win_v, v)
    win_s[2] = image[:, :128]
    win_s[3] = image[:, 128:]
    s_start()

    s[...] = jnp.zeros_like(s)
    place = iota((512, 256), 0)

    def rows_of(there):
        high = jnp.concatenate([mt_in[2 * there + core, 0:1, :] for core in range(2)], axis=1).astype(I32)
        low = jnp.concatenate([mt_in[2 * there + core, 1:2, :] for core in range(2)], axis=1).astype(I32)
        return high >> 9, (high & 511) + low

    def take_step(t, carry):
        there = lax.rem(chip + chips - 1 - t + chips, chips)
        for core in range(2):
            j = 2 * there + core

            @pl.when(j != me)
            def _():
                meta_copy(j, j).wait_recv()
                out_copy(j, j).wait_recv()

        row, column = rows_of(there)
        one_hot = (place == column).astype(F32).astype(BF16)
        rhot[there] = one_hot
        values = jnp.concatenate([inc[2 * there], inc[2 * there + 1]], axis=1)
        high, low = two(values)
        for half in range(2):
            terms = []
            for k in range(8):
                mask = jnp.broadcast_to((row == half * 8 + k).astype(F32), (M, 256)).astype(BF16)
                terms.append(high * mask)
                terms.append(low * mask)
            product = nt(jnp.concatenate(terms, axis=0), one_hot)
            for k in range(8):
                term = product[k * 64 : k * 64 + 32] + product[k * 64 + 32 : k * 64 + 64]
                for q in range(4):
                    a, b = half * 4 + k // 2, (k % 2) * 4 + q
                    s[a, b] += term[:, q * 128 : (q + 1) * 128]
        return carry

    lax.fori_loop(0, chips, take_step, 0)

    x_right = passage_copy(s.at[pl.ds(6, 2)], xl, x_send.at[0], x_recv.at[0], right_p)
    x_left = passage_copy(s.at[pl.ds(0, 2)], xr, x_send.at[1], x_recv.at[1], left_p)
    x_right.start()
    x_left.start()

    s_arrive()
    image_image = apply(win_s, image)

    lane = iota((M, 128), 1)
    inner_low = (lane > 0).astype(F32) * 0.5
    inner_high = (lane < 127).astype(F32) * 0.5

    def along(x):
        return x + pltpu.roll(x, 1, 1) * inner_low + pltpu.roll(x, 127, 1) * inner_high

    def layer(a, b):
        if a < 0:
            return xl[a + 2, b]
        if a >= CX:
            return xr[a - CX, b]
        return s[a, b]

    def filters(layers):
        def step(b, carry):
            for a in layers:
                near = layer(a - 1, b) + layer(a + 1, b)
                mine = layer(a, b)
                far = layer(a - 2, b) + layer(a + 2, b)
                pp[a, b] = BETA * along(mine + 0.5 * near)
                qq[a, b] = GAMMA * along(along(1.5 * mine + near + 0.25 * far))
            return carry

        lax.fori_loop(0, CY, step, 0)

    filters((2, 3, 4, 5))
    x_right.wait_recv()
    x_left.wait_recv()
    filters((0, 1, 6, 7))

    def edge_step(a, carry):
        ysr[0, a] = 0.5 * pp[a, 7] + 0.25 * qq[a, 6] + qq[a, 7]
        ysr[1, a] = 0.25 * qq[a, 7]
        ysl[0, a] = 0.5 * pp[a, 0] + 0.25 * qq[a, 1] + qq[a, 0]
        ysl[1, a] = 0.25 * qq[a, 0]
        return carry

    lax.fori_loop(0, CX, edge_step, 0)
    y_right = sub_copy(ysr, yl, y_send.at[0], y_recv.at[0], me + 1)
    y_left = sub_copy(ysl, yr, y_send.at[1], y_recv.at[1], me - 1)
    pl.when(has_right)(y_right.start)
    pl.when(has_left)(y_left.start)
    pl.when(has_left)(y_right.wait_recv)
    pl.when(has_right)(y_left.wait_recv)
    end_left = jnp.where(has_left, 1.5, 1.25).astype(F32)
    end_right = jnp.where(has_right, 1.5, 1.25).astype(F32)

    def press_step(a, carry):
        p = [pp[a, b] for b in range(CY)]
        q = [qq[a, b] for b in range(CY)]
        for b in range(CY):
            near_p = [p[k] for k in (b - 1, b + 1) if 0 <= k < CY]
            near_q = [q[k] for k in (b - 1, b + 1) if 0 <= k < CY]
            far_q = [q[k] for k in (b - 2, b + 2) if 0 <= k < CY]
            centre = end_left if b == 0 else end_right if b == CY - 1 else 1.5
            total = ALPHA * s[a, b] + p[b] + 0.5 * sum(near_p) + centre * q[b] + sum(near_q) + 0.25 * sum(far_q)
            if b < 2:
                total = total + yl[b, a]
            if b >= CY - 2:
                total = total + yr[CY - 1 - b, a]
            high, low = two(total)
            fp[0, 2 * a + b // 4, :, (b % 4) * 128 : (b % 4 + 1) * 128] = high
            fp[1, 2 * a + b // 4, :, (b % 4) * 128 : (b % 4 + 1) * 128] = low
        return carry

    lax.fori_loop(0, CX, press_step, 0)

    def give_step(t, carry):
        there = lax.rem(chip + 1 + t, chips)
        row, _ = rows_of(there)
        one_hot = rhot[there]
        total = jnp.zeros((M, 256), F32)
        for half in range(2):
            product = nn(fp[0, half * 8 : half * 8 + 8].reshape(8 * M, 512), one_hot) + nn(
                fp[1, half * 8 : half * 8 + 8].reshape(8 * M, 512), one_hot
            )
            for k in range(8):
                total = total + jnp.where(row == half * 8 + k, product[k * M : (k + 1) * M], 0.0)
        for core in range(2):
            j = 2 * there + core
            ret[j] = total[:, core * 128 : (core + 1) * 128]
            pl.when(j != me)(back_copy(j, me).start)
        return carry

    lax.fori_loop(0, chips, give_step, 0)
    back[me] = ret[me]

    def force_step(t, total):
        there = lax.rem(chip + chips - 1 - t + chips, chips)
        for core in range(2):
            j = 2 * there + core

            @pl.when(j != me)
            def _():
                back_copy(j, j).wait_recv()

        forces = jnp.concatenate([back[2 * there + core] * weight_row(2 * there + core) for core in range(2)], axis=1)
        product = nt(jnp.concatenate(three(forces), axis=0), n2[there])
        return total + product[0:M] + product[M : 2 * M] + product[2 * M :]

    massed = lax.fori_loop(0, chips, force_step, mass_ref[...] * v)
    win_w[2] = massed[:, :128]
    win_w[3] = massed[:, 128:]
    w_start()
    w_arrive()
    image_massed = apply(win_w, massed)

    x_high, x_low = two(jnp.concatenate([v, image, massed], axis=0))
    z_high, z_low = two(
        jnp.concatenate([image, massed, image_image, image_massed, v, jnp.zeros((96, NSD), F32)], axis=0)
    )
    x_both = jnp.concatenate([x_high, x_low], axis=0)
    product = nt(x_both, z_high) + nt(x_both, z_low)
    product = product[:96] + product[96:]
    third = jnp.where(lane < M, product[0:32, 128:], product[64:96, :128])
    gram = jnp.concatenate([product[0:64, :128], third, jnp.zeros((32, 128), F32)], axis=0)
    for g in range(n_sub):
        gbuf[g] = gram[g * rows : (g + 1) * rows]
    each_sub(lambda peer: gram_copy(peer, me).start())
    grecv[me] = gbuf[me]
    each_sub(lambda peer: gram_copy(peer, peer).wait_recv())
    part[0] = lax.fori_loop(1, n_sub, lambda g, total: total + grecv[g], grecv[0])
    each_passage(lambda peer: part_copy(peer, myp).start())
    precv[myp] = part[0]
    each_passage(lambda peer: part_copy(peer, peer).wait_recv())
    part[1] = lax.fori_loop(1, n_passage, lambda g, total: total + precv[g], precv[0])
    each_sub(lambda peer: full_copy(peer, me).start())
    gfull[me] = part[1]
    each_sub(lambda peer: full_copy(peer, peer).wait_recv())

    whole = jnp.concatenate([gfull[g] for g in range(n_sub)], axis=0)
    turned = whole.T
    scale = 1.0 / (NSD * n_sub * n_passage)
    row_of = iota((M, 128), 0)

    def moved(x, blocks):
        return pltpu.roll(x, (128 - 32 * blocks) % 128, 1)

    top, mid, bottom = whole[0:32], whole[32:64], whole[64:96]
    numer = jnp.where(lane == row_of, top, 0.0)
    denom = jnp.where(lane == row_of, moved(top, 1), 0.0)
    theta = jnp.sum(numer, axis=1, keepdims=True) / jnp.sum(denom, axis=1, keepdims=True)
    theta_row = jnp.sum(jnp.where(lane == row_of, theta, 0.0), axis=0, keepdims=True)
    resid_ref[...] = image - theta * massed
    mass_stiff = moved(turned[32:64], 1)
    plain_vr = top - moved(top, 1) * theta_row
    plain_rv = turned[0:32] - theta * turned[32:64]
    stiff_rs = mid - theta * mass_stiff
    plain_rr = stiff_rs - moved(mid, 1) * theta_row + theta * theta_row * moved(bottom, 1)
    stiff_vr = moved(top, 2) - moved(top, 3) * theta_row
    stiff_rr = (
        moved(mid, 2) - theta * moved(bottom, 2) - moved(mid, 3) * theta_row + theta * theta_row * moved(bottom, 3)
    )

    def side(first, second):
        return (jnp.where(lane < M, first, pltpu.roll(second, 32, 1)) * scale)[:, : 2 * M]

    gs_ref[0:M, :] = side(top, stiff_vr)
    gs_ref[M:, :] = side(stiff_rs, stiff_rr)
    gp_ref[0:M, :] = side(bottom, plain_vr)
    gp_ref[M:, :] = side(plain_rv, plain_rr)

    each_sub(lambda peer: meta_copy(peer, me).wait_send())
    each_sub(lambda peer: out_copy(peer, me).wait_send())
    each_sub(lambda peer: back_copy(peer, me).wait_send())
    each_sub(lambda peer: gram_copy(peer, me).wait_send())
    each_sub(lambda peer: full_copy(peer, me).wait_send())
    each_passage(lambda peer: part_copy(peer, myp).wait_send())
    x_right.wait_send()
    x_left.wait_send()
    pl.when(has_right)(y_right.wait_send)
    pl.when(has_left)(y_left.wait_send)
    v_sent()
    s_sent()
    w_sent()


def body(
    n_passage,
    n_sub,
    block_vectors,
    stiffness,
    mass_diag,
    kblocks,
    block_cols,
    slot_node,
    slot_owner,
    slot_cell,
    slot_weight,
    live_slots,
):
    nc = slot_node.shape[0] // 128
    chips = n_sub // 2
    rows = 128 // n_sub
    vmem = pl.BlockSpec(memory_space=pltpu.VMEM)
    smem = pl.BlockSpec(memory_space=pltpu.SMEM)
    dma = pltpu.SemaphoreType.DMA
    layers = (2, CY, M, CZ)
    return pl.pallas_call(
        functools.partial(kernel, n_passage, n_sub),
        out_shape=(
            jax.ShapeDtypeStruct((M, NSD), F32),
            jax.ShapeDtypeStruct((2 * M, 2 * M), F32),
            jax.ShapeDtypeStruct((2 * M, 2 * M), F32),
        ),
        in_specs=[vmem, vmem, vmem, vmem, smem, vmem, vmem, vmem, vmem, smem],
        out_specs=(vmem, vmem, vmem),
        scratch_shapes=[
            pltpu.VMEM((6, M, 128), F32),
            pltpu.VMEM((6, M, 128), F32),
            pltpu.VMEM((6, M, 128), F32),
            pltpu.VMEM((2, 512, 128), BF16),
            pltpu.VMEM((2, 512, 128), BF16),
            pltpu.VMEM((n_sub, 8, 128), F32),
            pltpu.VMEM((n_sub, 8, 128), F32),
            pltpu.VMEM((chips, NSD, 256), BF16),
            pltpu.VMEM((n_sub, M, CAP), F32),
            pltpu.VMEM((n_sub, M, CAP), F32),
            pltpu.VMEM((chips, 512, 256), BF16),
            pltpu.VMEM((CX, CY, M, CZ), F32),
            pltpu.VMEM(layers, F32),
            pltpu.VMEM(layers, F32),
            pltpu.VMEM((CX, CY, M, CZ), F32),
            pltpu.VMEM((CX, CY, M, CZ), F32),
            pltpu.VMEM(layers, F32),
            pltpu.VMEM(layers, F32),
            pltpu.VMEM(layers, F32),
            pltpu.VMEM(layers, F32),
            pltpu.VMEM((2, 16, M, 512), BF16),
            pltpu.VMEM((n_sub, M, CAP), F32),
            pltpu.VMEM((n_sub, M, CAP), F32),
            pltpu.VMEM((n_sub, rows, 128), F32),
            pltpu.VMEM((n_sub, rows, 128), F32),
            pltpu.VMEM((2, rows, 128), F32),
            pltpu.VMEM((n_passage, rows, 128), F32),
            pltpu.VMEM((n_sub, rows, 128), F32),
            dma((3, 2)),
            dma((3, 2)),
            dma((n_sub,)),
            dma((n_sub,)),
            dma((n_sub,)),
            dma((n_sub,)),
            dma((2,)),
            dma((2,)),
            dma((2,)),
            dma((2,)),
            dma((n_sub,)),
            dma((n_sub,)),
            dma((n_sub,)),
            dma((n_sub,)),
            dma((n_passage,)),
            dma((n_passage,)),
            dma((n_sub,)),
            dma((n_sub,)),
        ],
        compiler_params=pltpu.CompilerParams(
            collective_id=0, has_side_effects=True, vmem_limit_bytes=48 * 1024 * 1024
        ),
    )(
        block_vectors,
        stiffness.reshape(1, NSD),
        mass_diag.reshape(1, NSD),
        kblocks.reshape(2, 512, 128),
        block_cols,
        slot_node.reshape(nc, 128),
        slot_owner.reshape(nc, 128),
        slot_cell.reshape(nc, 128),
        slot_weight.reshape(nc, 128),
        live_slots,
    )


def solution(mesh):
    return jax.shard_map(
        functools.partial(body, mesh.shape["passage"], mesh.shape["sub"]),
        mesh=mesh,
        in_specs=(
            P(None, ("passage", "sub")),
            P(("passage", "sub")),
            P(("passage", "sub")),
            P(("passage", "sub"), None, None, None),
            P(("passage", "sub"), None),
            P(("passage", "sub")),
            P(("passage", "sub"), None),
            P(("passage", "sub")),
            P(("passage", "sub")),
            P(("passage", "sub")),
        ),
        out_specs=(P(None, ("passage", "sub")), P(), P()),
        check_vma=False,
    )
```

```python
import functools

import jax
import jax.numpy as jnp
from jax import lax
from jax.experimental import pallas as pl
from jax.experimental.pallas import tpu as pltpu
from jax.sharding import PartitionSpec as P

MESH = pl.DeviceIdType.MESH
F32 = jnp.float32
BF16 = jnp.bfloat16
I32 = jnp.int32

M = 32
CX = 8
CY = 8
CZ = 128
CAP = 128
NSD = 256
CHUNKS = 2
MC = M // CHUNKS

center_weight = 15.0
lower_bound = 1.0 / 15.0
upper_bound = 17.0 / 15.0
middle = (upper_bound + lower_bound) / 2.0
radius = (upper_bound - lower_bound) / 2.0
sigma_ratio = middle / radius
first_rho = 1.0 / sigma_ratio
second_rho = 1.0 / (2.0 * sigma_ratio - first_rho)
third_rho = 1.0 / (2.0 * sigma_ratio - second_rho)
FIRST = 1.0 / (center_weight * middle)
GAIN_TWO = 2.0 * second_rho / radius / center_weight
GAIN_THREE = 2.0 * third_rho / radius / center_weight
STEP_ONE = second_rho * first_rho * FIRST + GAIN_TWO * (1.0 - 17.0 * FIRST)
STEP_T = GAIN_TWO * 2.0 * FIRST
ALPHA = FIRST + STEP_ONE + third_rho * second_rho * STEP_ONE + GAIN_THREE * (1.0 - 17.0 * (FIRST + STEP_ONE))
BETA = STEP_T + third_rho * second_rho * STEP_T + GAIN_THREE * (2.0 * (FIRST + STEP_ONE) - 17.0 * STEP_T)
GAMMA = GAIN_THREE * 2.0 * STEP_T


def iota(shape, dim):
    return lax.broadcasted_iota(I32, shape, dim)


def nn(left, right):
    return jnp.dot(left, right, preferred_element_type=F32)


def nt(left, right):
    return lax.dot_general(left, right, (((1,), (1,)), ((), ())), preferred_element_type=F32)


def two(x):
    high = x.astype(BF16)
    return high, (x - high.astype(F32)).astype(BF16)


def three(x):
    high, rest = x.astype(BF16), None
    rest = x - high.astype(F32)
    middle_part = rest.astype(BF16)
    return high, middle_part, (rest - middle_part.astype(F32)).astype(BF16)


def kernel(
    n_passage,
    n_sub,
    v_hbm,
    stiff_hbm,
    mass_hbm,
    kb_hbm,
    cols_hbm,
    node_hbm,
    owner_hbm,
    cell_hbm,
    weight_hbm,
    live_hbm,
    resid_ref,
    gs_ref,
    gp_ref,
    v_ref,
    stiff_ref,
    mass_ref,
    kb_ref,
    cols_ref,
    node_ref,
    owner_ref,
    cell_ref,
    weight_ref,
    live_ref,
    in_sem,
    win_v,
    win_s,
    win_w,
    kbh,
    kbl,
    mt,
    n2,
    out,
    inc,
    rhot,
    s,
    xl,
    xr,
    pp,
    qq,
    ysl,
    ysr,
    yl,
    yr,
    fp,
    ret,
    back,
    gbuf,
    grecv,
    part,
    precv,
    gfull,
    nb_send,
    nb_recv,
    a_send,
    a_recv,
    x_send,
    x_recv,
    y_send,
    y_recv,
    b_send,
    b_recv,
    g_send,
    g_recv,
    p_send,
    p_recv,
    f_send,
    f_recv,
):
    chips = n_sub // 2
    ni = node_ref.shape[0] * 128
    nc = node_ref.shape[0]
    rows = 128 // n_sub
    myp = lax.axis_index("passage")
    me = lax.axis_index("sub")
    chip = me // 2
    left_p = lax.rem(myp + n_passage - 1, n_passage)
    right_p = lax.rem(myp + 1, n_passage)
    has_left = me > 0
    has_right = me < n_sub - 1

    def sub_copy(src, dst, send, recv, peer):
        return pltpu.make_async_remote_copy(
            src_ref=src, dst_ref=dst, send_sem=send, recv_sem=recv,
            device_id={"sub": peer}, device_id_type=MESH,
        )

    def passage_copy(src, dst, send, recv, peer):
        return pltpu.make_async_remote_copy(
            src_ref=src, dst_ref=dst, send_sem=send, recv_sem=recv,
            device_id={"passage": peer}, device_id_type=MESH,
        )

    arguments = (
        (node_hbm, node_ref),
        (owner_hbm, owner_ref),
        (cell_hbm, cell_ref),
        (weight_hbm, weight_ref),
        (live_hbm, live_ref),
        (v_hbm, v_ref),
        (kb_hbm, kb_ref),
        (stiff_hbm, stiff_ref),
        (mass_hbm, mass_ref),
        (cols_hbm, cols_ref),
    )
    loads = [pltpu.make_async_copy(src, dst, in_sem.at[k]) for k, (src, dst) in enumerate(arguments)]
    for load in loads:
        load.start()

    for win in (win_v, win_s, win_w):
        win[0:2] = jnp.zeros((2, M, 128), F32)
        win[4:6] = jnp.zeros((2, M, 128), F32)

    @pl.when(jnp.logical_not(has_left))
    def _():
        yl[...] = jnp.zeros_like(yl)

    @pl.when(jnp.logical_not(has_right))
    def _():
        yr[...] = jnp.zeros_like(yr)

    barrier = pltpu.get_barrier_semaphore()

    def greet_sub(i, carry):
        pl.semaphore_signal(barrier, inc=1, device_id={"sub": lax.rem(me + i, n_sub)}, device_id_type=MESH)
        return carry

    def greet_passage(i, carry):
        pl.semaphore_signal(barrier, inc=1, device_id={"passage": lax.rem(myp + i, n_passage)}, device_id_type=MESH)
        return carry

    lax.fori_loop(1, n_sub, greet_sub, 0)
    lax.fori_loop(1, n_passage, greet_passage, 0)

    for load in loads[:5]:
        load.wait()

    owner = owner_ref[...]
    lane_of_slot = iota((1, ni), 1)

    def flat(x):
        return jnp.concatenate([x[c : c + 1, :] for c in range(nc)], axis=1)

    group = iota((n_sub, 128), 0)
    hot = [(owner[c : c + 1, :] == group).astype(F32) for c in range(nc)]
    upper = (iota((128, 128), 0) < iota((128, 128), 1)).astype(F32).astype(BF16)
    before = nn(jnp.concatenate(hot, axis=0).astype(BF16), upper)
    ahead = jnp.zeros((n_sub, 1), F32)
    ranks = []
    for c in range(nc):
        ranks.append(jnp.sum(hot[c] * (before[c * n_sub : (c + 1) * n_sub] + ahead), axis=0, keepdims=True))
        ahead = ahead + jnp.sum(hot[c], axis=1, keepdims=True)
    rank = jnp.concatenate(ranks, axis=1).astype(I32)
    rank_hot = (iota((CAP, ni), 0) == rank).astype(F32).astype(BF16)
    node = flat(node_ref[...]).astype(F32)
    cell = flat(cell_ref[...])
    weight = jnp.where(lane_of_slot < live_ref[0], flat(weight_ref[...]), 0.0)
    w0, w1, w2 = three(weight)
    which = iota((8, ni), 0)
    meta = jnp.zeros((8, ni), F32)
    for row, values in enumerate(
        (((cell >> 7) << 7).astype(F32), (cell & 127).astype(F32), node, w0.astype(F32), w1.astype(F32), w2.astype(F32))
    ):
        meta = jnp.where(which == row, values, meta)
    owner_row = flat(owner)
    lhs = jnp.concatenate([jnp.where(owner_row == g, meta, 0.0) for g in range(n_sub)], axis=0).astype(BF16)
    placed = nt(lhs, rank_hot)
    for g in range(n_sub):
        mt[g] = placed[g * 8 : (g + 1) * 8]
    for load in loads[5:]:
        load.wait()
    v = v_ref[...]
    win_v[2] = v[:, :128]
    win_v[3] = v[:, 128:]

    pl.semaphore_wait(barrier, n_sub - 1 + n_passage - 1)

    def exchange(win, k):
        to_right = sub_copy(win.at[pl.ds(2, 2)], win.at[pl.ds(0, 2)], nb_send.at[k, 0], nb_recv.at[k, 0], me + 1)
        to_left = sub_copy(win.at[pl.ds(2, 2)], win.at[pl.ds(4, 2)], nb_send.at[k, 1], nb_recv.at[k, 1], me - 1)

        def start():
            pl.when(has_right)(to_right.start)
            pl.when(has_left)(to_left.start)

        def arrive():
            pl.when(has_left)(to_right.wait_recv)
            pl.when(has_right)(to_left.wait_recv)

        def sent():
            pl.when(has_right)(to_right.wait_send)
            pl.when(has_left)(to_left.wait_send)

        return start, arrive, sent

    v_start, v_arrive, v_sent = exchange(win_v, 0)
    s_start, s_arrive, s_sent = exchange(win_s, 1)
    w_start, w_arrive, w_sent = exchange(win_w, 2)

    def out_copy(c, peer, slot):
        sent_rows = pl.ds(0, MC + 8 if c == 0 else MC)
        return sub_copy(
            out.at[c, peer, sent_rows], inc.at[c, slot, sent_rows], a_send.at[c, peer], a_recv.at[c, slot], peer
        )

    def back_copy(c, peer, slot):
        return sub_copy(ret.at[c, peer], back.at[c, slot], b_send.at[c, peer], b_recv.at[c, slot], peer)

    def gram_copy(peer, slot):
        return sub_copy(gbuf.at[peer], grecv.at[slot], g_send.at[peer], g_recv.at[slot], peer)

    def full_copy(peer, slot):
        return sub_copy(part.at[1], gfull.at[slot], f_send.at[peer], f_recv.at[slot], peer)

    def part_copy(peer, slot):
        return passage_copy(part.at[0], precv.at[slot], p_send.at[peer], p_recv.at[slot], peer)

    def each_sub(act):
        def step(i, carry):
            act(lax.rem(me + i, n_sub))
            return carry

        lax.fori_loop(1, n_sub, step, 0)

    def each_passage(act):
        def step(i, carry):
            act(lax.rem(myp + i, n_passage))
            return carry

        lax.fori_loop(1, n_passage, step, 0)

    v_start()
    departures = [v_sent]

    v3 = jnp.concatenate(three(v), axis=0)
    node_of = iota((NSD, 128), 0)

    def weight_row(g):
        return mt[g, 3:4, :] + mt[g, 4:5, :] + mt[g, 5:6, :]

    def send_step(t, carry):
        there = lax.rem(chip + 1 + t, chips)
        parts = [(node_of == mt[2 * there + core, 2:3, :].astype(I32)).astype(F32) for core in range(2)]
        one_hot = jnp.concatenate(parts, axis=1).astype(BF16)
        n2[there] = one_hot
        picked = nn(v3, one_hot)
        picked = picked[0:M] + picked[M : 2 * M] + picked[2 * M :]
        for core in range(2):
            g = 2 * there + core
            values = picked[:, core * 128 : (core + 1) * 128] * weight_row(g)
            for c in range(CHUNKS):
                out[c, g, 0:MC, :] = values[c * MC : (c + 1) * MC]
            out[0, g, MC : MC + 8, :] = mt[g]
            pl.when(g != me)(out_copy(0, g, me).start)
        return carry

    lax.fori_loop(0, chips, send_step, 0)
    for c in range(1, CHUNKS):
        each_sub(lambda peer, c=c: out_copy(c, peer, me).start())
    for c in range(CHUNKS):
        departures.append(lambda c=c: each_sub(lambda peer: out_copy(c, peer, me).wait_send()))
        inc[c, me] = out[c, me]

    for r in range(2):
        kb = kb_ref[r]
        high, low = two(kb)
        kbh[r] = high
        kbl[r] = low

    stiff = stiff_ref[...]

    def apply(win, own):
        mixed = []
        for r in range(2):
            blocks = jnp.concatenate([win[cols_ref[r, n]] for n in range(4)], axis=1)
            high, low = two(blocks)
            both = nn(jnp.concatenate([high, low], axis=0), kbh[r])
            mixed.append(both[:M] + both[M:] + nn(high, kbl[r]))
        return stiff * own + jnp.concatenate(mixed, axis=1)

    v_arrive()
    image = apply(win_v, v)
    win_s[2] = image[:, :128]
    win_s[3] = image[:, 128:]
    s_start()
    departures.append(s_sent)

    place = iota((512, 256), 0)

    def rows_of(there):
        high = jnp.concatenate([inc[0, 2 * there + k, MC : MC + 1, :] for k in range(2)], axis=1).astype(I32)
        low = jnp.concatenate([inc[0, 2 * there + k, MC + 1 : MC + 2, :] for k in range(2)], axis=1).astype(I32)
        return high >> 9, (high & 511) + low

    def each_source(there, act):
        for core in range(2):
            j = 2 * there + core
            pl.when(j != me)(functools.partial(act, j))

    def take(c):
        s[c] = jnp.zeros((CX, CY, MC, CZ), F32)

        def step(t, carry):
            there = lax.rem(chip + 2 * chips - 1 - t, chips)
            each_source(there, lambda j: out_copy(c, j, j).wait_recv())
            row, column = rows_of(there)
            if c == 0:
                one_hot = (place == column).astype(F32).astype(BF16)
                rhot[there] = one_hot
            else:
                one_hot = rhot[there]
            values = jnp.concatenate([inc[c, 2 * there, 0:MC, :], inc[c, 2 * there + 1, 0:MC, :]], axis=1)
            high, low = two(values)
            terms = []
            for k in range(16):
                mask = jnp.broadcast_to((row == k).astype(F32), (MC, 256)).astype(BF16)
                terms.append(high * mask)
                terms.append(low * mask)
            product = nt(jnp.concatenate(terms, axis=0), one_hot)
            for k in range(16):
                term = product[2 * k * MC : (2 * k + 1) * MC] + product[(2 * k + 1) * MC : (2 * k + 2) * MC]
                for q in range(4):
                    s[c, k // 2, (k % 2) * 4 + q] += term[:, q * 128 : (q + 1) * 128]
            return carry

        lax.fori_loop(0, chips, step, 0)

    x_right = [
        passage_copy(s.at[c, pl.ds(6, 2)], xl.at[c], x_send.at[c, 0], x_recv.at[c, 0], right_p) for c in range(CHUNKS)
    ]
    x_left = [
        passage_copy(s.at[c, pl.ds(0, 2)], xr.at[c], x_send.at[c, 1], x_recv.at[c, 1], left_p) for c in range(CHUNKS)
    ]
    for c in range(CHUNKS):
        take(c)
        x_right[c].start()
        x_left[c].start()
        departures += [x_right[c].wait_send, x_left[c].wait_send]

    s_arrive()
    image_image = apply(win_s, image)

    lane = iota((M, 128), 1)
    chunk_lane = iota((MC, 128), 1)
    inner_low = (chunk_lane > 0).astype(F32) * 0.5
    inner_high = (chunk_lane < 127).astype(F32) * 0.5

    def along(x):
        return x + pltpu.roll(x, 1, 1) * inner_low + pltpu.roll(x, 127, 1) * inner_high

    def filters(c, layers):
        def layer(a, b):
            if a < 0:
                return xl[c, a + 2, b]
            if a >= CX:
                return xr[c, a - CX, b]
            return s[c, a, b]

        def step(b, carry):
            for a in layers:
                near = layer(a - 1, b) + layer(a + 1, b)
                mine = layer(a, b)
                far = layer(a - 2, b) + layer(a + 2, b)
                pp[c, a, b] = BETA * along(mine + 0.5 * near)
                qq[c, a, b] = GAMMA * along(along(1.5 * mine + near + 0.25 * far))
            return carry

        lax.fori_loop(0, CY, step, 0)

    y_right = [sub_copy(ysr.at[c], yl.at[c], y_send.at[c, 0], y_recv.at[c, 0], me + 1) for c in range(CHUNKS)]
    y_left = [sub_copy(ysl.at[c], yr.at[c], y_send.at[c, 1], y_recv.at[c, 1], me - 1) for c in range(CHUNKS)]
    for c in range(CHUNKS):
        filters(c, (2, 3, 4, 5))
        x_right[c].wait_recv()
        x_left[c].wait_recv()
        filters(c, (0, 1, 6, 7))

        def edge_step(a, carry):
            ysr[c, 0, a] = 0.5 * pp[c, a, 7] + 0.25 * qq[c, a, 6] + qq[c, a, 7]
            ysr[c, 1, a] = 0.25 * qq[c, a, 7]
            ysl[c, 0, a] = 0.5 * pp[c, a, 0] + 0.25 * qq[c, a, 1] + qq[c, a, 0]
            ysl[c, 1, a] = 0.25 * qq[c, a, 0]
            return carry

        lax.fori_loop(0, CX, edge_step, 0)
        pl.when(has_right)(y_right[c].start)
        pl.when(has_left)(y_left[c].start)
        departures.append(lambda c=c: pl.when(has_right)(y_right[c].wait_send))
        departures.append(lambda c=c: pl.when(has_left)(y_left[c].wait_send))

    end_left = jnp.where(has_left, 1.5, 1.25).astype(F32)
    end_right = jnp.where(has_right, 1.5, 1.25).astype(F32)

    def press(c):
        def step(a, carry):
            p = [pp[c, a, b] for b in range(CY)]
            q = [qq[c, a, b] for b in range(CY)]
            for b in range(CY):
                near_p = [p[k] for k in (b - 1, b + 1) if 0 <= k < CY]
                near_q = [q[k] for k in (b - 1, b + 1) if 0 <= k < CY]
                far_q = [q[k] for k in (b - 2, b + 2) if 0 <= k < CY]
                centre = end_left if b == 0 else end_right if b == CY - 1 else 1.5
                total = ALPHA * s[c, a, b] + p[b] + 0.5 * sum(near_p) + centre * q[b] + sum(near_q) + 0.25 * sum(far_q)
                if b < 2:
                    total = total + yl[c, b, a]
                if b >= CY - 2:
                    total = total + yr[c, CY - 1 - b, a]
                high, low = two(total)
                fp[0, 2 * a + b // 4, :, (b % 4) * 128 : (b % 4 + 1) * 128] = high
                fp[1, 2 * a + b // 4, :, (b % 4) * 128 : (b % 4 + 1) * 128] = low
            return carry

        lax.fori_loop(0, CX, step, 0)

    def give(c):
        def step(t, carry):
            there = lax.rem(chip + 1 + t, chips)
            row, _ = rows_of(there)
            product = nn(fp[...].reshape(32 * MC, 512), rhot[there])
            total = jnp.zeros((MC, 256), F32)
            for k in range(16):
                both = product[k * MC : (k + 1) * MC] + product[(16 + k) * MC : (17 + k) * MC]
                total = total + jnp.where(row == k, both, 0.0)
            for core in range(2):
                ret[c, 2 * there + core] = total[:, core * 128 : (core + 1) * 128]
            each_source(there, lambda j: back_copy(c, j, me).start())
            return carry

        lax.fori_loop(0, chips, step, 0)
        back[c, me] = ret[c, me]

    for c in range(CHUNKS):
        pl.when(has_left)(y_right[c].wait_recv)
        pl.when(has_right)(y_left[c].wait_recv)
        press(c)
        give(c)
        departures.append(lambda c=c: each_sub(lambda peer: back_copy(c, peer, me).wait_send()))

    def forces(c):
        def step(t, total):
            there = lax.rem(chip + 2 * chips - 1 - t, chips)
            each_source(there, lambda j: back_copy(c, j, j).wait_recv())
            force = jnp.concatenate([back[c, 2 * there + k] * weight_row(2 * there + k) for k in range(2)], axis=1)
            product = nt(jnp.concatenate(three(force), axis=0), n2[there])
            return total + product[0:MC] + product[MC : 2 * MC] + product[2 * MC :]

        return lax.fori_loop(0, chips, step, mass_ref[...] * v[c * MC : (c + 1) * MC])

    massed = jnp.concatenate([forces(c) for c in range(CHUNKS)], axis=0)
    win_w[2] = massed[:, :128]
    win_w[3] = massed[:, 128:]
    w_start()
    departures.append(w_sent)
    w_arrive()
    image_massed = apply(win_w, massed)

    x_high, x_low = two(jnp.concatenate([v, image, massed], axis=0))
    z_high, z_low = two(
        jnp.concatenate([image, massed, image_image, image_massed, v, jnp.zeros((96, NSD), F32)], axis=0)
    )
    x_both = jnp.concatenate([x_high, x_low], axis=0)
    product = nt(x_both, z_high) + nt(x_both, z_low)
    product = product[:96] + product[96:]
    third = jnp.where(lane < M, product[0:32, 128:], product[64:96, :128])
    gram = jnp.concatenate([product[0:64, :128], third, jnp.zeros((32, 128), F32)], axis=0)
    for g in range(n_sub):
        gbuf[g] = gram[g * rows : (g + 1) * rows]
    each_sub(lambda peer: gram_copy(peer, me).start())
    departures.append(lambda: each_sub(lambda peer: gram_copy(peer, me).wait_send()))
    grecv[me] = gbuf[me]
    each_sub(lambda peer: gram_copy(peer, peer).wait_recv())
    part[0] = lax.fori_loop(1, n_sub, lambda g, total: total + grecv[g], grecv[0])
    each_passage(lambda peer: part_copy(peer, myp).start())
    departures.append(lambda: each_passage(lambda peer: part_copy(peer, myp).wait_send()))
    precv[myp] = part[0]
    each_passage(lambda peer: part_copy(peer, peer).wait_recv())
    part[1] = lax.fori_loop(1, n_passage, lambda g, total: total + precv[g], precv[0])
    each_sub(lambda peer: full_copy(peer, me).start())
    departures.append(lambda: each_sub(lambda peer: full_copy(peer, me).wait_send()))
    gfull[me] = part[1]
    each_sub(lambda peer: full_copy(peer, peer).wait_recv())

    whole = jnp.concatenate([gfull[g] for g in range(n_sub)], axis=0)
    turned = whole.T
    scale = 1.0 / (NSD * n_sub * n_passage)
    row_of = iota((M, 128), 0)

    def moved(x, blocks):
        return pltpu.roll(x, (128 - 32 * blocks) % 128, 1)

    top, mid, bottom = whole[0:32], whole[32:64], whole[64:96]
    numer = jnp.where(lane == row_of, top, 0.0)
    denom = jnp.where(lane == row_of, moved(top, 1), 0.0)
    theta = jnp.sum(numer, axis=1, keepdims=True) / jnp.sum(denom, axis=1, keepdims=True)
    theta_row = jnp.sum(jnp.where(lane == row_of, theta, 0.0), axis=0, keepdims=True)
    resid_ref[...] = image - theta * massed
    mass_stiff = moved(turned[32:64], 1)
    plain_vr = top - moved(top, 1) * theta_row
    plain_rv = turned[0:32] - theta * turned[32:64]
    stiff_rs = mid - theta * mass_stiff
    plain_rr = stiff_rs - moved(mid, 1) * theta_row + theta * theta_row * moved(bottom, 1)
    stiff_vr = moved(top, 2) - moved(top, 3) * theta_row
    stiff_rr = (
        moved(mid, 2) - theta * moved(bottom, 2) - moved(mid, 3) * theta_row + theta * theta_row * moved(bottom, 3)
    )

    def side(first, second):
        return (jnp.where(lane < M, first, pltpu.roll(second, 32, 1)) * scale)[:, : 2 * M]

    gs_ref[0:M, :] = side(top, stiff_vr)
    gs_ref[M:, :] = side(stiff_rs, stiff_rr)
    gp_ref[0:M, :] = side(bottom, plain_vr)
    gp_ref[M:, :] = side(plain_rv, plain_rr)

    for sent in departures:
        sent()


def body(
    n_passage,
    n_sub,
    block_vectors,
    stiffness,
    mass_diag,
    kblocks,
    block_cols,
    slot_node,
    slot_owner,
    slot_cell,
    slot_weight,
    live_slots,
):
    nc = slot_node.shape[0] // 128
    chips = n_sub // 2
    rows = 128 // n_sub
    vmem = pl.BlockSpec(memory_space=pltpu.VMEM)
    hbm = pl.BlockSpec(memory_space=pltpu.HBM)
    dma = pltpu.SemaphoreType.DMA
    layers = pltpu.VMEM((CHUNKS, 2, CY, MC, CZ), F32)
    cells = pltpu.VMEM((CHUNKS, CX, CY, MC, CZ), F32)
    return pl.pallas_call(
        functools.partial(kernel, n_passage, n_sub),
        out_shape=(
            jax.ShapeDtypeStruct((M, NSD), F32),
            jax.ShapeDtypeStruct((2 * M, 2 * M), F32),
            jax.ShapeDtypeStruct((2 * M, 2 * M), F32),
        ),
        in_specs=[hbm] * 10,
        out_specs=(vmem, vmem, vmem),
        scratch_shapes=[
            pltpu.VMEM((M, NSD), F32),
            pltpu.VMEM((1, NSD), F32),
            pltpu.VMEM((1, NSD), F32),
            pltpu.VMEM((2, 512, 128), F32),
            pltpu.SMEM((2, 4), I32),
            pltpu.VMEM((nc, 128), I32),
            pltpu.VMEM((nc, 128), I32),
            pltpu.VMEM((nc, 128), I32),
            pltpu.VMEM((nc, 128), F32),
            pltpu.SMEM((1,), I32),
            dma((10,)),
            pltpu.VMEM((6, M, 128), F32),
            pltpu.VMEM((6, M, 128), F32),
            pltpu.VMEM((6, M, 128), F32),
            pltpu.VMEM((2, 512, 128), BF16),
            pltpu.VMEM((2, 512, 128), BF16),
            pltpu.VMEM((n_sub, 8, 128), F32),
            pltpu.VMEM((chips, NSD, 256), BF16),
            pltpu.VMEM((CHUNKS, n_sub, MC + 8, CAP), F32),
            pltpu.VMEM((CHUNKS, n_sub, MC + 8, CAP), F32),
            pltpu.VMEM((chips, 512, 256), BF16),
            cells,
            layers,
            layers,
            cells,
            cells,
            layers,
            layers,
            layers,
            layers,
            pltpu.VMEM((2, 16, MC, 512), BF16),
            pltpu.VMEM((CHUNKS, n_sub, MC, CAP), F32),
            pltpu.VMEM((CHUNKS, n_sub, MC, CAP), F32),
            pltpu.VMEM((n_sub, rows, 128), F32),
            pltpu.VMEM((n_sub, rows, 128), F32),
            pltpu.VMEM((2, rows, 128), F32),
            pltpu.VMEM((n_passage, rows, 128), F32),
            pltpu.VMEM((n_sub, rows, 128), F32),
            dma((3, 2)),
            dma((3, 2)),
            dma((CHUNKS, n_sub)),
            dma((CHUNKS, n_sub)),
            dma((CHUNKS, 2)),
            dma((CHUNKS, 2)),
            dma((CHUNKS, 2)),
            dma((CHUNKS, 2)),
            dma((CHUNKS, n_sub)),
            dma((CHUNKS, n_sub)),
            dma((n_sub,)),
            dma((n_sub,)),
            dma((n_passage,)),
            dma((n_passage,)),
            dma((n_sub,)),
            dma((n_sub,)),
        ],
        compiler_params=pltpu.CompilerParams(
            collective_id=0, has_side_effects=True, vmem_limit_bytes=60 * 1024 * 1024
        ),
    )(
        block_vectors,
        stiffness.reshape(1, NSD),
        mass_diag.reshape(1, NSD),
        kblocks.reshape(2, 512, 128),
        block_cols,
        slot_node.reshape(nc, 128),
        slot_owner.reshape(nc, 128),
        slot_cell.reshape(nc, 128),
        slot_weight.reshape(nc, 128),
        live_slots,
    )


def solution(mesh):
    return jax.shard_map(
        functools.partial(body, mesh.shape["passage"], mesh.shape["sub"]),
        mesh=mesh,
        in_specs=(
            P(None, ("passage", "sub")),
            P(("passage", "sub")),
            P(("passage", "sub")),
            P(("passage", "sub"), None, None, None),
            P(("passage", "sub"), None),
            P(("passage", "sub")),
            P(("passage", "sub"), None),
            P(("passage", "sub")),
            P(("passage", "sub")),
            P(("passage", "sub")),
        ),
        out_specs=(P(None, ("passage", "sub")), P(), P()),
        check_vma=False,
    )
```

```python
import functools

import jax
import jax.numpy as jnp
from jax import lax
from jax.experimental import pallas as pl
from jax.experimental.pallas import tpu as pltpu
from jax.sharding import PartitionSpec as P

MESH = pl.DeviceIdType.MESH
F32 = jnp.float32
BF16 = jnp.bfloat16
I32 = jnp.int32

M = 32
CX = 8
CY = 8
CZ = 128
CAP = 128
NSD = 256
CHUNKS = 2
MC = M // CHUNKS

center_weight = 15.0
lower_bound = 1.0 / 15.0
upper_bound = 17.0 / 15.0
middle = (upper_bound + lower_bound) / 2.0
radius = (upper_bound - lower_bound) / 2.0
sigma_ratio = middle / radius
first_rho = 1.0 / sigma_ratio
second_rho = 1.0 / (2.0 * sigma_ratio - first_rho)
third_rho = 1.0 / (2.0 * sigma_ratio - second_rho)
FIRST = 1.0 / (center_weight * middle)
GAIN_TWO = 2.0 * second_rho / radius / center_weight
GAIN_THREE = 2.0 * third_rho / radius / center_weight
STEP_ONE = second_rho * first_rho * FIRST + GAIN_TWO * (1.0 - 17.0 * FIRST)
STEP_T = GAIN_TWO * 2.0 * FIRST
ALPHA = FIRST + STEP_ONE + third_rho * second_rho * STEP_ONE + GAIN_THREE * (1.0 - 17.0 * (FIRST + STEP_ONE))
BETA = STEP_T + third_rho * second_rho * STEP_T + GAIN_THREE * (2.0 * (FIRST + STEP_ONE) - 17.0 * STEP_T)
GAMMA = GAIN_THREE * 2.0 * STEP_T


def iota(shape, dim):
    return lax.broadcasted_iota(I32, shape, dim)


def nn(left, right):
    return jnp.dot(left, right, preferred_element_type=F32)


def nt(left, right):
    return lax.dot_general(left, right, (((1,), (1,)), ((), ())), preferred_element_type=F32)


def two(x):
    high = x.astype(BF16)
    return high, (x - high.astype(F32)).astype(BF16)


def three(x):
    high, rest = x.astype(BF16), None
    rest = x - high.astype(F32)
    middle_part = rest.astype(BF16)
    return high, middle_part, (rest - middle_part.astype(F32)).astype(BF16)


def kernel(
    n_passage,
    n_sub,
    v_hbm,
    stiff_hbm,
    mass_hbm,
    kb_hbm,
    cols_hbm,
    node_hbm,
    owner_hbm,
    cell_hbm,
    weight_hbm,
    live_hbm,
    resid_ref,
    gs_ref,
    gp_ref,
    v_ref,
    stiff_ref,
    mass_ref,
    kb_ref,
    cols_ref,
    node_ref,
    owner_ref,
    cell_ref,
    weight_ref,
    live_ref,
    in_sem,
    win_v,
    win_s,
    win_w,
    kbh,
    kbl,
    mt,
    n2,
    out,
    inc,
    rhot,
    s,
    xl,
    xr,
    pp,
    qq,
    ysl,
    ysr,
    yl,
    yr,
    fp,
    ret,
    back,
    gbuf,
    grecv,
    part,
    precv,
    gfull,
    whole,
    nb_send,
    nb_recv,
    a_send,
    a_recv,
    x_send,
    x_recv,
    y_send,
    y_recv,
    b_send,
    b_recv,
    g_send,
    g_recv,
    p_send,
    p_recv,
    f_send,
    f_recv,
):
    chips = n_sub // 2
    ni = node_ref.shape[0] * 128
    nc = node_ref.shape[0]
    rows = 3 * M // n_sub
    myp = lax.axis_index("passage")
    me = lax.axis_index("sub")
    chip = me // 2
    left_p = lax.rem(myp + n_passage - 1, n_passage)
    right_p = lax.rem(myp + 1, n_passage)
    has_left = me > 0
    has_right = me < n_sub - 1

    def sub_copy(src, dst, send, recv, peer):
        return pltpu.make_async_remote_copy(
            src_ref=src, dst_ref=dst, send_sem=send, recv_sem=recv,
            device_id={"sub": peer}, device_id_type=MESH,
        )

    def passage_copy(src, dst, send, recv, peer):
        return pltpu.make_async_remote_copy(
            src_ref=src, dst_ref=dst, send_sem=send, recv_sem=recv,
            device_id={"passage": peer}, device_id_type=MESH,
        )

    arguments = (
        (node_hbm, node_ref),
        (owner_hbm, owner_ref),
        (cell_hbm, cell_ref),
        (weight_hbm, weight_ref),
        (live_hbm, live_ref),
        (v_hbm, v_ref),
        (kb_hbm, kb_ref),
        (stiff_hbm, stiff_ref),
        (mass_hbm, mass_ref),
        (cols_hbm, cols_ref),
    )
    loads = [pltpu.make_async_copy(src, dst, in_sem.at[k]) for k, (src, dst) in enumerate(arguments)]
    for load in loads:
        load.start()

    for win in (win_v, win_s, win_w):
        win[0:2] = jnp.zeros((2, M, 128), F32)
        win[4:6] = jnp.zeros((2, M, 128), F32)

    @pl.when(jnp.logical_not(has_left))
    def _():
        yl[...] = jnp.zeros_like(yl)

    @pl.when(jnp.logical_not(has_right))
    def _():
        yr[...] = jnp.zeros_like(yr)

    barrier = pltpu.get_barrier_semaphore()

    def greet_sub(i, carry):
        pl.semaphore_signal(barrier, inc=1, device_id={"sub": lax.rem(me + i, n_sub)}, device_id_type=MESH)
        return carry

    def greet_passage(i, carry):
        pl.semaphore_signal(barrier, inc=1, device_id={"passage": lax.rem(myp + i, n_passage)}, device_id_type=MESH)
        return carry

    lax.fori_loop(1, n_sub, greet_sub, 0)
    lax.fori_loop(1, n_passage, greet_passage, 0)

    for load in loads[:5]:
        load.wait()

    owner = owner_ref[...]
    lane_of_slot = iota((1, ni), 1)

    def flat(x):
        return jnp.concatenate([x[c : c + 1, :] for c in range(nc)], axis=1)

    group = iota((n_sub, 128), 0)
    hot = [(owner[c : c + 1, :] == group).astype(F32) for c in range(nc)]
    upper = (iota((128, 128), 0) < iota((128, 128), 1)).astype(F32).astype(BF16)
    before = nn(jnp.concatenate(hot, axis=0).astype(BF16), upper)
    ahead = jnp.zeros((n_sub, 1), F32)
    ranks = []
    for c in range(nc):
        ranks.append(jnp.sum(hot[c] * (before[c * n_sub : (c + 1) * n_sub] + ahead), axis=0, keepdims=True))
        ahead = ahead + jnp.sum(hot[c], axis=1, keepdims=True)
    rank = jnp.concatenate(ranks, axis=1).astype(I32)
    rank_hot = (iota((CAP, ni), 0) == rank).astype(F32).astype(BF16)
    node = flat(node_ref[...]).astype(F32)
    cell = flat(cell_ref[...])
    weight = jnp.where(lane_of_slot < live_ref[0], flat(weight_ref[...]), 0.0)
    w0, w1, w2 = three(weight)
    which = iota((8, ni), 0)
    meta = jnp.zeros((8, ni), F32)
    for row, values in enumerate(
        (((cell >> 7) << 7).astype(F32), (cell & 127).astype(F32), node, w0.astype(F32), w1.astype(F32), w2.astype(F32))
    ):
        meta = jnp.where(which == row, values, meta)
    owner_row = flat(owner)
    lhs = jnp.concatenate([jnp.where(owner_row == g, meta, 0.0) for g in range(n_sub)], axis=0).astype(BF16)
    placed = nt(lhs, rank_hot)
    for g in range(n_sub):
        mt[g] = placed[g * 8 : (g + 1) * 8]
    for load in loads[5:]:
        load.wait()
    v = v_ref[...]
    win_v[2] = v[:, :128]
    win_v[3] = v[:, 128:]

    pl.semaphore_wait(barrier, n_sub - 1 + n_passage - 1)

    def exchange(win, k):
        to_right = sub_copy(win.at[pl.ds(2, 2)], win.at[pl.ds(0, 2)], nb_send.at[k, 0], nb_recv.at[k, 0], me + 1)
        to_left = sub_copy(win.at[pl.ds(2, 2)], win.at[pl.ds(4, 2)], nb_send.at[k, 1], nb_recv.at[k, 1], me - 1)

        def start():
            pl.when(has_right)(to_right.start)
            pl.when(has_left)(to_left.start)

        def arrive():
            pl.when(has_left)(to_right.wait_recv)
            pl.when(has_right)(to_left.wait_recv)

        def sent():
            pl.when(has_right)(to_right.wait_send)
            pl.when(has_left)(to_left.wait_send)

        return start, arrive, sent

    v_start, v_arrive, v_sent = exchange(win_v, 0)
    s_start, s_arrive, s_sent = exchange(win_s, 1)
    w_start, w_arrive, w_sent = exchange(win_w, 2)

    def out_copy(c, peer, slot):
        sent_rows = pl.ds(0, MC + 2 if c == 0 else MC)
        return sub_copy(
            out.at[c, peer, sent_rows], inc.at[c, slot, sent_rows], a_send.at[c, peer], a_recv.at[c, slot], peer
        )

    def back_copy(c, peer, slot):
        return sub_copy(ret.at[c, peer], back.at[c, slot], b_send.at[c, peer], b_recv.at[c, slot], peer)

    kept = pl.ds(0, rows)

    def gram_copy(peer, slot):
        return sub_copy(gbuf.at[peer, kept], grecv.at[slot, kept], g_send.at[peer], g_recv.at[slot], peer)

    def full_copy(peer, slot):
        return sub_copy(part.at[1, kept], gfull.at[slot, kept], f_send.at[peer], f_recv.at[slot], peer)

    def part_copy(peer, slot):
        return passage_copy(part.at[0, kept], precv.at[slot, kept], p_send.at[peer], p_recv.at[slot], peer)

    def far_first(k, count):
        half = (k + 1) // 2
        return count // 2 + jnp.where(lax.rem(k, 2) == 1, -half, half)

    def each_sub(act):
        def step(k, carry):
            act(lax.rem(me + far_first(k, n_sub), n_sub))
            return carry

        lax.fori_loop(0, n_sub - 1, step, 0)

    def each_passage(act):
        def step(k, carry):
            act(lax.rem(myp + far_first(k, n_passage), n_passage))
            return carry

        lax.fori_loop(0, n_passage - 1, step, 0)

    def chip_to(t):
        return lax.rem(chip + far_first(t, chips), chips)

    def chip_from(t):
        return lax.rem(chip + chips - far_first(t, chips), chips)

    v_start()
    departures = [v_sent]

    v3 = jnp.concatenate(three(v), axis=0)
    node_of = iota((NSD, 128), 0)

    def weight_row(g):
        return mt[g, 3:4, :] + mt[g, 4:5, :] + mt[g, 5:6, :]

    def send_step(t, carry):
        there = chip_to(t)
        parts = [(node_of == mt[2 * there + core, 2:3, :].astype(I32)).astype(F32) for core in range(2)]
        one_hot = jnp.concatenate(parts, axis=1).astype(BF16)
        n2[there] = one_hot
        picked = nn(v3, one_hot)
        picked = picked[0:M] + picked[M : 2 * M] + picked[2 * M :]
        for core in range(2):
            g = 2 * there + core
            values = picked[:, core * 128 : (core + 1) * 128] * weight_row(g)
            for c in range(CHUNKS):
                out[c, g, 0:MC, :] = values[c * MC : (c + 1) * MC]
            out[0, g, MC : MC + 2, :] = mt[g, 0:2, :]
            pl.when(g != me)(out_copy(0, g, me).start)
        return carry

    lax.fori_loop(0, chips, send_step, 0)
    for c in range(1, CHUNKS):
        each_sub(lambda peer, c=c: out_copy(c, peer, me).start())
    for c in range(CHUNKS):
        departures.append(lambda c=c: each_sub(lambda peer: out_copy(c, peer, me).wait_send()))
        own = MC + 2 if c == 0 else MC
        inc[c, me, 0:own] = out[c, me, 0:own]

    for r in range(2):
        kb = kb_ref[r]
        high, low = two(kb)
        kbh[r] = high
        kbl[r] = low

    stiff = stiff_ref[...]

    def apply(win, own):
        mixed = []
        for r in range(2):
            blocks = jnp.concatenate([win[cols_ref[r, n]] for n in range(4)], axis=1)
            high, low = two(blocks)
            both = nn(jnp.concatenate([high, low], axis=0), kbh[r])
            mixed.append(both[:M] + both[M:] + nn(high, kbl[r]))
        return stiff * own + jnp.concatenate(mixed, axis=1)

    v_arrive()
    image = apply(win_v, v)
    win_s[2] = image[:, :128]
    win_s[3] = image[:, 128:]
    s_start()
    departures.append(s_sent)

    place = iota((512, 256), 0)

    def rows_of(there):
        high = jnp.concatenate([inc[0, 2 * there + k, MC : MC + 1, :] for k in range(2)], axis=1).astype(I32)
        low = jnp.concatenate([inc[0, 2 * there + k, MC + 1 : MC + 2, :] for k in range(2)], axis=1).astype(I32)
        return high >> 9, (high & 511) + low

    def each_source(there, act):
        for core in range(2):
            j = 2 * there + core
            pl.when(j != me)(functools.partial(act, j))

    def take(c, first, layers):
        span = range(2 * layers[0], 2 * layers[0] + 4), range(2 * layers[1], 2 * layers[1] + 4)
        places = [k for part_of in span for k in part_of]
        for a in layers:
            s[c, a : a + 2] = jnp.zeros((2, CY, MC, CZ), F32)

        def step(t, carry):
            there = chip_from(t)
            if first:
                each_source(there, lambda j: out_copy(c, j, j).wait_recv())
            row, column = rows_of(there)
            if first and c == 0:
                one_hot = (place == column).astype(F32).astype(BF16)
                rhot[there] = one_hot
            else:
                one_hot = rhot[there]
            values = jnp.concatenate([inc[c, 2 * there, 0:MC, :], inc[c, 2 * there + 1, 0:MC, :]], axis=1)
            high, low = two(values)
            terms = []
            for k in places:
                mask = jnp.broadcast_to((row == k).astype(F32), (MC, 256)).astype(BF16)
                terms.append(high * mask)
                terms.append(low * mask)
            product = nt(jnp.concatenate(terms, axis=0), one_hot)
            for n, k in enumerate(places):
                term = product[2 * n * MC : (2 * n + 1) * MC] + product[(2 * n + 1) * MC : (2 * n + 2) * MC]
                for q in range(4):
                    s[c, k // 2, (k % 2) * 4 + q] += term[:, q * 128 : (q + 1) * 128]
            return carry

        lax.fori_loop(0, chips, step, 0)

    x_right = [
        passage_copy(s.at[c, pl.ds(6, 2)], xl.at[c], x_send.at[c, 0], x_recv.at[c, 0], right_p) for c in range(CHUNKS)
    ]
    x_left = [
        passage_copy(s.at[c, pl.ds(0, 2)], xr.at[c], x_send.at[c, 1], x_recv.at[c, 1], left_p) for c in range(CHUNKS)
    ]
    for c in range(CHUNKS):
        take(c, True, (0, 6))
        x_right[c].start()
        x_left[c].start()
        take(c, False, (2, 4))
        departures += [x_right[c].wait_send, x_left[c].wait_send]

    s_arrive()
    image_image = apply(win_s, image)

    lane = iota((M, 128), 1)
    chunk_lane = iota((MC, 128), 1)
    inner_low = (chunk_lane > 0).astype(F32) * 0.5
    inner_high = (chunk_lane < 127).astype(F32) * 0.5

    def along(x):
        return x + pltpu.roll(x, 1, 1) * inner_low + pltpu.roll(x, 127, 1) * inner_high

    def filters(c, layers):
        def layer(a, b):
            if a < 0:
                return xl[c, a + 2, b]
            if a >= CX:
                return xr[c, a - CX, b]
            return s[c, a, b]

        def step(b, carry):
            for a in layers:
                near = layer(a - 1, b) + layer(a + 1, b)
                mine = layer(a, b)
                far = layer(a - 2, b) + layer(a + 2, b)
                pp[c, a, b] = BETA * along(mine + 0.5 * near)
                qq[c, a, b] = GAMMA * along(along(1.5 * mine + near + 0.25 * far))
            return carry

        lax.fori_loop(0, CY, step, 0)

    y_right = [sub_copy(ysr.at[c], yl.at[c], y_send.at[c, 0], y_recv.at[c, 0], me + 1) for c in range(CHUNKS)]
    y_left = [sub_copy(ysl.at[c], yr.at[c], y_send.at[c, 1], y_recv.at[c, 1], me - 1) for c in range(CHUNKS)]
    for c in range(CHUNKS):
        filters(c, (2, 3, 4, 5))
        x_right[c].wait_recv()
        x_left[c].wait_recv()
        filters(c, (0, 1, 6, 7))

        def edge_step(a, carry):
            ysr[c, 0, a] = 0.5 * pp[c, a, 7] + 0.25 * qq[c, a, 6] + qq[c, a, 7]
            ysr[c, 1, a] = 0.25 * qq[c, a, 7]
            ysl[c, 0, a] = 0.5 * pp[c, a, 0] + 0.25 * qq[c, a, 1] + qq[c, a, 0]
            ysl[c, 1, a] = 0.25 * qq[c, a, 0]
            return carry

        lax.fori_loop(0, CX, edge_step, 0)
        pl.when(has_right)(y_right[c].start)
        pl.when(has_left)(y_left[c].start)
        departures.append(lambda c=c: pl.when(has_right)(y_right[c].wait_send))
        departures.append(lambda c=c: pl.when(has_left)(y_left[c].wait_send))

    end_left = jnp.where(has_left, 1.5, 1.25).astype(F32)
    end_right = jnp.where(has_right, 1.5, 1.25).astype(F32)

    def press(c):
        def step(a, carry):
            p = [pp[c, a, b] for b in range(CY)]
            q = [qq[c, a, b] for b in range(CY)]
            for b in range(CY):
                near_p = [p[k] for k in (b - 1, b + 1) if 0 <= k < CY]
                near_q = [q[k] for k in (b - 1, b + 1) if 0 <= k < CY]
                far_q = [q[k] for k in (b - 2, b + 2) if 0 <= k < CY]
                centre = end_left if b == 0 else end_right if b == CY - 1 else 1.5
                total = ALPHA * s[c, a, b] + p[b] + 0.5 * sum(near_p) + centre * q[b] + sum(near_q) + 0.25 * sum(far_q)
                if b < 2:
                    total = total + yl[c, b, a]
                if b >= CY - 2:
                    total = total + yr[c, CY - 1 - b, a]
                high, low = two(total)
                fp[0, 2 * a + b // 4, :, (b % 4) * 128 : (b % 4 + 1) * 128] = high
                fp[1, 2 * a + b // 4, :, (b % 4) * 128 : (b % 4 + 1) * 128] = low
            return carry

        lax.fori_loop(0, CX, step, 0)

    def give(c):
        def step(t, carry):
            there = chip_to(t)
            row, _ = rows_of(there)
            product = nn(fp[...].reshape(32 * MC, 512), rhot[there])
            total = jnp.zeros((MC, 256), F32)
            for k in range(16):
                both = product[k * MC : (k + 1) * MC] + product[(16 + k) * MC : (17 + k) * MC]
                total = total + jnp.where(row == k, both, 0.0)
            for core in range(2):
                ret[c, 2 * there + core] = total[:, core * 128 : (core + 1) * 128]
            each_source(there, lambda j: back_copy(c, j, me).start())
            return carry

        lax.fori_loop(0, chips, step, 0)
        back[c, me] = ret[c, me]

    for c in range(CHUNKS):
        pl.when(has_left)(y_right[c].wait_recv)
        pl.when(has_right)(y_left[c].wait_recv)
        press(c)
        give(c)
        departures.append(lambda c=c: each_sub(lambda peer: back_copy(c, peer, me).wait_send()))

    def forces(c):
        def step(t, total):
            there = chip_from(t)
            each_source(there, lambda j: back_copy(c, j, j).wait_recv())
            force = jnp.concatenate([back[c, 2 * there + k] * weight_row(2 * there + k) for k in range(2)], axis=1)
            product = nt(jnp.concatenate(three(force), axis=0), n2[there])
            return total + product[0:MC] + product[MC : 2 * MC] + product[2 * MC :]

        return lax.fori_loop(0, chips, step, mass_ref[...] * v[c * MC : (c + 1) * MC])

    massed = jnp.concatenate([forces(c) for c in range(CHUNKS)], axis=0)
    win_w[2] = massed[:, :128]
    win_w[3] = massed[:, 128:]
    w_start()
    departures.append(w_sent)
    w_arrive()
    image_massed = apply(win_w, massed)

    x_high, x_low = two(jnp.concatenate([v, image, massed], axis=0))
    z_high, z_low = two(
        jnp.concatenate([image, massed, image_image, image_massed, v, jnp.zeros((96, NSD), F32)], axis=0)
    )
    x_both = jnp.concatenate([x_high, x_low], axis=0)
    product = nt(x_both, z_high) + nt(x_both, z_low)
    product = product[:96] + product[96:]
    third = jnp.where(lane < M, product[0:32, 128:], product[64:96, :128])
    whole[0:64, :] = product[0:64, :128]
    whole[64:96, :] = third
    whole[96:128, :] = jnp.zeros((32, 128), F32)
    for g in range(n_sub):
        gbuf[g, 0:rows, :] = whole[g * rows : (g + 1) * rows, :]
    each_sub(lambda peer: gram_copy(peer, me).start())
    departures.append(lambda: each_sub(lambda peer: gram_copy(peer, me).wait_send()))
    grecv[me, 0:rows] = gbuf[me, 0:rows]
    each_sub(lambda peer: gram_copy(peer, peer).wait_recv())
    part[0, 0:rows] = lax.fori_loop(1, n_sub, lambda g, total: total + grecv[g, 0:rows], grecv[0, 0:rows])
    each_passage(lambda peer: part_copy(peer, myp).start())
    departures.append(lambda: each_passage(lambda peer: part_copy(peer, myp).wait_send()))
    precv[myp, 0:rows] = part[0, 0:rows]
    each_passage(lambda peer: part_copy(peer, peer).wait_recv())
    part[1, 0:rows] = lax.fori_loop(1, n_passage, lambda g, total: total + precv[g, 0:rows], precv[0, 0:rows])
    each_sub(lambda peer: full_copy(peer, me).start())
    departures.append(lambda: each_sub(lambda peer: full_copy(peer, me).wait_send()))
    gfull[me, 0:rows] = part[1, 0:rows]
    each_sub(lambda peer: full_copy(peer, peer).wait_recv())

    for g in range(n_sub):
        whole[g * rows : (g + 1) * rows, :] = gfull[g, 0:rows, :]
    turned = whole[...].T
    scale = 1.0 / (NSD * n_sub * n_passage)
    row_of = iota((M, 128), 0)

    def moved(x, blocks):
        return pltpu.roll(x, (128 - 32 * blocks) % 128, 1)

    top, mid, bottom = whole[0:32], whole[32:64], whole[64:96]
    numer = jnp.where(lane == row_of, top, 0.0)
    denom = jnp.where(lane == row_of, moved(top, 1), 0.0)
    theta = jnp.sum(numer, axis=1, keepdims=True) / jnp.sum(denom, axis=1, keepdims=True)
    theta_row = jnp.sum(jnp.where(lane == row_of, theta, 0.0), axis=0, keepdims=True)
    resid_ref[...] = image - theta * massed
    mass_stiff = moved(turned[32:64], 1)
    plain_vr = top - moved(top, 1) * theta_row
    plain_rv = turned[0:32] - theta * turned[32:64]
    stiff_rs = mid - theta * mass_stiff
    plain_rr = stiff_rs - moved(mid, 1) * theta_row + theta * theta_row * moved(bottom, 1)
    stiff_vr = moved(top, 2) - moved(top, 3) * theta_row
    stiff_rr = (
        moved(mid, 2) - theta * moved(bottom, 2) - moved(mid, 3) * theta_row + theta * theta_row * moved(bottom, 3)
    )

    def side(first, second):
        return (jnp.where(lane < M, first, pltpu.roll(second, 32, 1)) * scale)[:, : 2 * M]

    gs_ref[0:M, :] = side(top, stiff_vr)
    gs_ref[M:, :] = side(stiff_rs, stiff_rr)
    gp_ref[0:M, :] = side(bottom, plain_vr)
    gp_ref[M:, :] = side(plain_rv, plain_rr)

    for sent in departures:
        sent()


def hand_out(a, b, c, a_out, b_out, c_out, sem):
    copies = [
        pltpu.make_async_copy(src, dst, sem.at[k]) for k, (src, dst) in enumerate(((a, a_out), (b, b_out), (c, c_out)))
    ]
    for copy in copies:
        copy.start()
    for copy in copies:
        copy.wait()


def body(
    n_passage,
    n_sub,
    block_vectors,
    stiffness,
    mass_diag,
    kblocks,
    block_cols,
    slot_node,
    slot_owner,
    slot_cell,
    slot_weight,
    live_slots,
):
    nc = slot_node.shape[0] // 128
    chips = n_sub // 2
    rows = -(-3 * M // n_sub // 8) * 8
    shapes = (
        jax.ShapeDtypeStruct((M, NSD), F32),
        jax.ShapeDtypeStruct((2 * M, 2 * M), F32),
        jax.ShapeDtypeStruct((2 * M, 2 * M), F32),
    )
    vmem = pl.BlockSpec(memory_space=pltpu.VMEM)
    hbm = pl.BlockSpec(memory_space=pltpu.HBM)
    dma = pltpu.SemaphoreType.DMA
    layers = pltpu.VMEM((CHUNKS, 2, CY, MC, CZ), F32)
    cells = pltpu.VMEM((CHUNKS, CX, CY, MC, CZ), F32)
    outs = pl.pallas_call(
        functools.partial(kernel, n_passage, n_sub),
        out_shape=shapes,
        in_specs=[hbm] * 10,
        out_specs=(vmem, vmem, vmem),
        scratch_shapes=[
            pltpu.VMEM((M, NSD), F32),
            pltpu.VMEM((1, NSD), F32),
            pltpu.VMEM((1, NSD), F32),
            pltpu.VMEM((2, 512, 128), F32),
            pltpu.SMEM((2, 4), I32),
            pltpu.VMEM((nc, 128), I32),
            pltpu.VMEM((nc, 128), I32),
            pltpu.VMEM((nc, 128), I32),
            pltpu.VMEM((nc, 128), F32),
            pltpu.SMEM((1,), I32),
            dma((10,)),
            pltpu.VMEM((6, M, 128), F32),
            pltpu.VMEM((6, M, 128), F32),
            pltpu.VMEM((6, M, 128), F32),
            pltpu.VMEM((2, 512, 128), BF16),
            pltpu.VMEM((2, 512, 128), BF16),
            pltpu.VMEM((n_sub, 8, 128), F32),
            pltpu.VMEM((chips, NSD, 256), BF16),
            pltpu.VMEM((CHUNKS, n_sub, MC + 8, CAP), F32),
            pltpu.VMEM((CHUNKS, n_sub, MC + 8, CAP), F32),
            pltpu.VMEM((chips, 512, 256), BF16),
            cells,
            layers,
            layers,
            cells,
            cells,
            layers,
            layers,
            layers,
            layers,
            pltpu.VMEM((2, 16, MC, 512), BF16),
            pltpu.VMEM((CHUNKS, n_sub, MC, CAP), F32),
            pltpu.VMEM((CHUNKS, n_sub, MC, CAP), F32),
            pltpu.VMEM((n_sub, rows, 128), F32),
            pltpu.VMEM((n_sub, rows, 128), F32),
            pltpu.VMEM((2, rows, 128), F32),
            pltpu.VMEM((n_passage, rows, 128), F32),
            pltpu.VMEM((n_sub, rows, 128), F32),
            pltpu.VMEM((128, 128), F32),
            dma((3, 2)),
            dma((3, 2)),
            dma((CHUNKS, n_sub)),
            dma((CHUNKS, n_sub)),
            dma((CHUNKS, 2)),
            dma((CHUNKS, 2)),
            dma((CHUNKS, 2)),
            dma((CHUNKS, 2)),
            dma((CHUNKS, n_sub)),
            dma((CHUNKS, n_sub)),
            dma((n_sub,)),
            dma((n_sub,)),
            dma((n_passage,)),
            dma((n_passage,)),
            dma((n_sub,)),
            dma((n_sub,)),
        ],
        compiler_params=pltpu.CompilerParams(
            collective_id=0, has_side_effects=True, vmem_limit_bytes=60 * 1024 * 1024
        ),
    )(
        block_vectors,
        stiffness.reshape(1, NSD),
        mass_diag.reshape(1, NSD),
        kblocks.reshape(2, 512, 128),
        block_cols,
        slot_node.reshape(nc, 128),
        slot_owner.reshape(nc, 128),
        slot_cell.reshape(nc, 128),
        slot_weight.reshape(nc, 128),
        live_slots,
    )
    return pl.pallas_call(
        hand_out,
        out_shape=shapes,
        in_specs=[pl.BlockSpec(memory_space=pl.ANY)] * 3,
        out_specs=(hbm, hbm, hbm),
        scratch_shapes=[dma((3,))],
    )(*outs)


def solution(mesh):
    return jax.shard_map(
        functools.partial(body, mesh.shape["passage"], mesh.shape["sub"]),
        mesh=mesh,
        in_specs=(
            P(None, ("passage", "sub")),
            P(("passage", "sub")),
            P(("passage", "sub")),
            P(("passage", "sub"), None, None, None),
            P(("passage", "sub"), None),
            P(("passage", "sub")),
            P(("passage", "sub"), None),
            P(("passage", "sub")),
            P(("passage", "sub")),
            P(("passage", "sub")),
        ),
        out_specs=(P(None, ("passage", "sub")), P(), P()),
        check_vma=False,
    )
```

```python
import functools

import jax
import jax.numpy as jnp
from jax import lax
from jax.experimental import pallas as pl
from jax.experimental.pallas import tpu as pltpu
from jax.sharding import PartitionSpec as P

MESH = pl.DeviceIdType.MESH
F32 = jnp.float32
BF16 = jnp.bfloat16
I32 = jnp.int32

M = 32
CX = 8
CY = 8
CZ = 128
CAP = 128
NSD = 256
CHUNKS = 2
MC = M // CHUNKS

center_weight = 15.0
lower_bound = 1.0 / 15.0
upper_bound = 17.0 / 15.0
middle = (upper_bound + lower_bound) / 2.0
radius = (upper_bound - lower_bound) / 2.0
sigma_ratio = middle / radius
first_rho = 1.0 / sigma_ratio
second_rho = 1.0 / (2.0 * sigma_ratio - first_rho)
third_rho = 1.0 / (2.0 * sigma_ratio - second_rho)
FIRST = 1.0 / (center_weight * middle)
GAIN_TWO = 2.0 * second_rho / radius / center_weight
GAIN_THREE = 2.0 * third_rho / radius / center_weight
STEP_ONE = second_rho * first_rho * FIRST + GAIN_TWO * (1.0 - 17.0 * FIRST)
STEP_T = GAIN_TWO * 2.0 * FIRST
ALPHA = FIRST + STEP_ONE + third_rho * second_rho * STEP_ONE + GAIN_THREE * (1.0 - 17.0 * (FIRST + STEP_ONE))
BETA = STEP_T + third_rho * second_rho * STEP_T + GAIN_THREE * (2.0 * (FIRST + STEP_ONE) - 17.0 * STEP_T)
GAMMA = GAIN_THREE * 2.0 * STEP_T


def iota(shape, dim):
    return lax.broadcasted_iota(I32, shape, dim)


def nn(left, right):
    return jnp.dot(left, right, preferred_element_type=F32)


def nt(left, right):
    return lax.dot_general(left, right, (((1,), (1,)), ((), ())), preferred_element_type=F32)


def two(x):
    high = x.astype(BF16)
    return high, (x - high.astype(F32)).astype(BF16)


def three(x):
    high, rest = x.astype(BF16), None
    rest = x - high.astype(F32)
    middle_part = rest.astype(BF16)
    return high, middle_part, (rest - middle_part.astype(F32)).astype(BF16)


def kernel(
    n_passage,
    n_sub,
    v_hbm,
    stiff_hbm,
    mass_hbm,
    kb_hbm,
    cols_hbm,
    node_hbm,
    owner_hbm,
    cell_hbm,
    weight_hbm,
    live_hbm,
    resid_ref,
    gs_ref,
    gp_ref,
    v_ref,
    stiff_ref,
    mass_ref,
    kb_ref,
    cols_ref,
    node_ref,
    owner_ref,
    cell_ref,
    weight_ref,
    live_ref,
    in_sem,
    win_v,
    win_s,
    win_w,
    kbh,
    kbl,
    mt,
    n2,
    out,
    inc,
    rhot,
    rowf,
    s,
    xl,
    xr,
    pp,
    qq,
    ysl,
    ysr,
    yl,
    yr,
    fp,
    ret,
    back,
    gbuf,
    grecv,
    part,
    precv,
    gfull,
    whole,
    nb_send,
    nb_recv,
    a_send,
    a_recv,
    x_send,
    x_recv,
    y_send,
    y_recv,
    b_send,
    b_recv,
    g_send,
    g_recv,
    p_send,
    p_recv,
    f_send,
    f_recv,
):
    chips = n_sub // 2
    ni = node_ref.shape[0] * 128
    nc = node_ref.shape[0]
    rows = 3 * M // n_sub
    myp = lax.axis_index("passage")
    me = lax.axis_index("sub")
    chip = me // 2
    left_p = lax.rem(myp + n_passage - 1, n_passage)
    right_p = lax.rem(myp + 1, n_passage)
    has_left = me > 0
    has_right = me < n_sub - 1

    def sub_copy(src, dst, send, recv, peer):
        return pltpu.make_async_remote_copy(
            src_ref=src, dst_ref=dst, send_sem=send, recv_sem=recv,
            device_id={"sub": peer}, device_id_type=MESH,
        )

    def passage_copy(src, dst, send, recv, peer):
        return pltpu.make_async_remote_copy(
            src_ref=src, dst_ref=dst, send_sem=send, recv_sem=recv,
            device_id={"passage": peer}, device_id_type=MESH,
        )

    arguments = (
        (node_hbm, node_ref),
        (owner_hbm, owner_ref),
        (cell_hbm, cell_ref),
        (weight_hbm, weight_ref),
        (live_hbm, live_ref),
        (v_hbm, v_ref),
        (kb_hbm, kb_ref),
        (stiff_hbm, stiff_ref),
        (mass_hbm, mass_ref),
        (cols_hbm, cols_ref),
    )
    loads = [pltpu.make_async_copy(src, dst, in_sem.at[k]) for k, (src, dst) in enumerate(arguments)]
    for load in loads:
        load.start()

    for win in (win_v, win_s, win_w):
        win[0:2] = jnp.zeros((2, M, 128), F32)
        win[4:6] = jnp.zeros((2, M, 128), F32)

    @pl.when(jnp.logical_not(has_left))
    def _():
        yl[...] = jnp.zeros_like(yl)

    @pl.when(jnp.logical_not(has_right))
    def _():
        yr[...] = jnp.zeros_like(yr)

    barrier = pltpu.get_barrier_semaphore()

    def greet_sub(i, carry):
        pl.semaphore_signal(barrier, inc=1, device_id={"sub": lax.rem(me + i, n_sub)}, device_id_type=MESH)
        return carry

    def greet_passage(i, carry):
        pl.semaphore_signal(barrier, inc=1, device_id={"passage": lax.rem(myp + i, n_passage)}, device_id_type=MESH)
        return carry

    lax.fori_loop(1, n_sub, greet_sub, 0)
    lax.fori_loop(1, n_passage, greet_passage, 0)

    for load in loads[:5]:
        load.wait()

    owner = owner_ref[...]
    lane_of_slot = iota((1, ni), 1)

    def flat(x):
        return jnp.concatenate([x[c : c + 1, :] for c in range(nc)], axis=1)

    group = iota((n_sub, 128), 0)
    hot = [(owner[c : c + 1, :] == group).astype(F32) for c in range(nc)]
    upper = (iota((128, 128), 0) < iota((128, 128), 1)).astype(F32).astype(BF16)
    before = nn(jnp.concatenate(hot, axis=0).astype(BF16), upper)
    ahead = jnp.zeros((n_sub, 1), F32)
    ranks = []
    for c in range(nc):
        ranks.append(jnp.sum(hot[c] * (before[c * n_sub : (c + 1) * n_sub] + ahead), axis=0, keepdims=True))
        ahead = ahead + jnp.sum(hot[c], axis=1, keepdims=True)
    rank = jnp.concatenate(ranks, axis=1).astype(I32)
    rank_hot = (iota((CAP, ni), 0) == rank).astype(F32).astype(BF16)
    node = flat(node_ref[...]).astype(F32)
    cell = flat(cell_ref[...])
    weight = jnp.where(lane_of_slot < live_ref[0], flat(weight_ref[...]), 0.0)
    w0, w1, w2 = three(weight)
    which = iota((8, ni), 0)
    meta = jnp.zeros((8, ni), F32)
    for row, values in enumerate(
        (((cell >> 7) << 7).astype(F32), (cell & 127).astype(F32), node, w0.astype(F32), w1.astype(F32), w2.astype(F32))
    ):
        meta = jnp.where(which == row, values, meta)
    owner_row = flat(owner)
    lhs = jnp.concatenate([jnp.where(owner_row == g, meta, 0.0) for g in range(n_sub)], axis=0).astype(BF16)
    placed = nt(lhs, rank_hot)
    for g in range(n_sub):
        mt[g] = placed[g * 8 : (g + 1) * 8]
    for load in loads[5:]:
        load.wait()
    v = v_ref[...]
    win_v[2] = v[:, :128]
    win_v[3] = v[:, 128:]

    pl.semaphore_wait(barrier, n_sub - 1 + n_passage - 1)

    def exchange(win, k):
        to_right = sub_copy(win.at[pl.ds(2, 2)], win.at[pl.ds(0, 2)], nb_send.at[k, 0], nb_recv.at[k, 0], me + 1)
        to_left = sub_copy(win.at[pl.ds(2, 2)], win.at[pl.ds(4, 2)], nb_send.at[k, 1], nb_recv.at[k, 1], me - 1)

        def start():
            pl.when(has_right)(to_right.start)
            pl.when(has_left)(to_left.start)

        def arrive():
            pl.when(has_left)(to_right.wait_recv)
            pl.when(has_right)(to_left.wait_recv)

        def sent():
            pl.when(has_right)(to_right.wait_send)
            pl.when(has_left)(to_left.wait_send)

        return start, arrive, sent

    v_start, v_arrive, v_sent = exchange(win_v, 0)
    s_start, s_arrive, s_sent = exchange(win_s, 1)
    w_start, w_arrive, w_sent = exchange(win_w, 2)

    def out_copy(c, peer, slot):
        sent_rows = pl.ds(0, MC + 2 if c == 0 else MC)
        return sub_copy(
            out.at[c, peer, sent_rows], inc.at[c, slot, sent_rows], a_send.at[c, peer], a_recv.at[c, slot], peer
        )

    def back_copy(c, peer, slot):
        return sub_copy(ret.at[c, peer], back.at[c, slot], b_send.at[c, peer], b_recv.at[c, slot], peer)

    kept = pl.ds(0, rows)

    def gram_copy(peer, slot):
        return sub_copy(gbuf.at[peer, kept], grecv.at[slot, kept], g_send.at[peer], g_recv.at[slot], peer)

    def full_copy(peer, slot):
        return sub_copy(part.at[1, kept], gfull.at[slot, kept], f_send.at[peer], f_recv.at[slot], peer)

    def part_copy(peer, slot):
        return passage_copy(part.at[0, kept], precv.at[slot, kept], p_send.at[peer], p_recv.at[slot], peer)

    def far_first(k, count):
        half = (k + 1) // 2
        if isinstance(k, int):
            return count // 2 + (-half if k % 2 else half)
        return count // 2 + jnp.where(lax.rem(k, 2) == 1, -half, half)

    def each_sub(act):
        def step(k, carry):
            act(lax.rem(me + far_first(k, n_sub), n_sub))
            return carry

        lax.fori_loop(0, n_sub - 1, step, 0)

    def each_passage(act):
        def step(k, carry):
            act(lax.rem(myp + far_first(k, n_passage), n_passage))
            return carry

        lax.fori_loop(0, n_passage - 1, step, 0)

    def chip_to(t):
        return lax.rem(chip + far_first(t, chips), chips)

    v_start()
    departures = [v_sent]

    v3 = jnp.concatenate(three(v), axis=0)
    node_of = iota((NSD, 128), 0)

    def weight_row(g):
        return mt[g, 3:4, :] + mt[g, 4:5, :] + mt[g, 5:6, :]

    def send_step(t, carry):
        there = chip_to(t)
        parts = [(node_of == mt[2 * there + core, 2:3, :].astype(I32)).astype(F32) for core in range(2)]
        one_hot = jnp.concatenate(parts, axis=1).astype(BF16)
        n2[there] = one_hot
        picked = nn(v3, one_hot)
        picked = picked[0:M] + picked[M : 2 * M] + picked[2 * M :]
        for core in range(2):
            g = 2 * there + core
            values = picked[:, core * 128 : (core + 1) * 128] * weight_row(g)
            for c in range(CHUNKS):
                out[c, g, 0:MC, :] = values[c * MC : (c + 1) * MC]
            out[0, g, MC : MC + 2, :] = mt[g, 0:2, :]
            pl.when(g != me)(out_copy(0, g, me).start)
        return carry

    lax.fori_loop(0, chips, send_step, 0)
    inc[0, me, 0 : MC + 2] = out[0, me, 0 : MC + 2]

    for r in range(2):
        kb = kb_ref[r]
        high, low = two(kb)
        kbh[r] = high
        kbl[r] = low

    stiff = stiff_ref[...]

    def apply(win, own):
        mixed = []
        for r in range(2):
            blocks = jnp.concatenate([win[cols_ref[r, n]] for n in range(4)], axis=1)
            high, low = two(blocks)
            both = nn(jnp.concatenate([high, low], axis=0), kbh[r])
            mixed.append(both[:M] + both[M:] + nn(high, kbl[r]))
        return stiff * own + jnp.concatenate(mixed, axis=1)

    v_arrive()
    image = apply(win_v, v)
    win_s[2] = image[:, :128]
    win_s[3] = image[:, 128:]
    s_start()
    departures.append(s_sent)
    for c in range(1, CHUNKS):
        each_sub(lambda peer: out_copy(c - 1, peer, me).wait_send())
        each_sub(lambda peer: out_copy(c, peer, me).start())
        inc[c, me, 0:MC] = out[c, me, 0:MC]
    departures.append(lambda: each_sub(lambda peer: out_copy(CHUNKS - 1, peer, me).wait_send()))

    place = iota((512, 256), 0)

    def rows_of(there):
        high = jnp.concatenate([inc[0, 2 * there + k, MC : MC + 1, :] for k in range(2)], axis=1).astype(I32)
        low = jnp.concatenate([inc[0, 2 * there + k, MC + 1 : MC + 2, :] for k in range(2)], axis=1).astype(I32)
        return high >> 9, (high & 511) + low

    def each_source(there, act):
        for core in range(2):
            j = 2 * there + core
            pl.when(j != me)(functools.partial(act, j))

    def take(c):
        each_sub(lambda peer: out_copy(c, peer, peer).wait_recv())
        if c == 0:

            def mark(there, carry):
                row, column = rows_of(there)
                rhot[there] = (place == column).astype(F32).astype(BF16)
                rowf[there] = jnp.broadcast_to(row, (8, 256))
                return carry

            lax.fori_loop(0, chips, mark, 0)
        one_hot = jnp.concatenate([rhot[k] for k in range(chips)], axis=1)
        row = jnp.concatenate([rowf[k, 0:1, :] for k in range(chips)], axis=1)
        high, low = two(jnp.concatenate([inc[c, k, 0:MC, :] for k in range(n_sub)], axis=1))
        highs, lows = [], []
        for k in range(16):
            mask = jnp.broadcast_to((row == k).astype(F32), (MC, n_sub * CAP)).astype(BF16)
            highs.append(high * mask)
            lows.append(low * mask)
        terms = jnp.concatenate([jnp.concatenate(highs, axis=0), jnp.concatenate(lows, axis=0)], axis=1)
        product = nt(terms, jnp.concatenate([one_hot, one_hot], axis=1))
        for k in range(16):
            for q in range(4):
                s[c, k // 2, (k % 2) * 4 + q] = product[k * MC : (k + 1) * MC, q * 128 : (q + 1) * 128]

    x_right = [
        passage_copy(s.at[c, pl.ds(6, 2)], xl.at[c], x_send.at[c, 0], x_recv.at[c, 0], right_p) for c in range(CHUNKS)
    ]
    x_left = [
        passage_copy(s.at[c, pl.ds(0, 2)], xr.at[c], x_send.at[c, 1], x_recv.at[c, 1], left_p) for c in range(CHUNKS)
    ]
    for c in range(CHUNKS):
        take(c)
        x_right[c].start()
        x_left[c].start()
        departures += [x_right[c].wait_send, x_left[c].wait_send]

    s_arrive()
    image_image = apply(win_s, image)

    lane = iota((M, 128), 1)
    apart = jnp.abs(iota((128, 128), 0) - iota((128, 128), 1))
    at_end = (iota((128, 128), 0) == 0) | (iota((128, 128), 0) == 127)
    once = jnp.where(apart == 0, 1.0, jnp.where(apart == 1, 0.5, 0.0))
    middle_weight = jnp.where(at_end, 1.25, 1.5)
    twice = jnp.where(apart == 0, middle_weight, jnp.where(apart == 1, 1.0, jnp.where(apart == 2, 0.25, 0.0)))
    once = jnp.concatenate([once, once], axis=0).astype(BF16)
    twice = jnp.concatenate([twice, twice], axis=0).astype(BF16)

    def filters(c, layers):
        def layer(a, b):
            if a < 0:
                return xl[c, a + 2, b]
            if a >= CX:
                return xr[c, a - CX, b]
            return s[c, a, b]

        ps, qs = [], []
        for a in layers:
            for b in range(CY):
                near = layer(a - 1, b) + layer(a + 1, b)
                mine = layer(a, b)
                far = layer(a - 2, b) + layer(a + 2, b)
                ps.append(jnp.concatenate(two(mine + 0.5 * near), axis=1))
                qs.append(jnp.concatenate(two(1.5 * mine + near + 0.25 * far), axis=1))
        p = BETA * nn(jnp.concatenate(ps, axis=0), once)
        q = GAMMA * nn(jnp.concatenate(qs, axis=0), twice)
        for n, a in enumerate(layers):
            for b in range(CY):
                at = (n * CY + b) * MC
                pp[c, a, b] = p[at : at + MC]
                qq[c, a, b] = q[at : at + MC]

    y_right = [sub_copy(ysr.at[c], yl.at[c], y_send.at[c, 0], y_recv.at[c, 0], me + 1) for c in range(CHUNKS)]
    y_left = [sub_copy(ysl.at[c], yr.at[c], y_send.at[c, 1], y_recv.at[c, 1], me - 1) for c in range(CHUNKS)]
    for c in range(CHUNKS):
        filters(c, (2, 3, 4, 5))
        x_right[c].wait_recv()
        x_left[c].wait_recv()
        filters(c, (0, 1, 6, 7))

        for a in range(CX):
            ysr[c, 0, a] = 0.5 * pp[c, a, 7] + 0.25 * qq[c, a, 6] + qq[c, a, 7]
            ysr[c, 1, a] = 0.25 * qq[c, a, 7]
            ysl[c, 0, a] = 0.5 * pp[c, a, 0] + 0.25 * qq[c, a, 1] + qq[c, a, 0]
            ysl[c, 1, a] = 0.25 * qq[c, a, 0]
        pl.when(has_right)(y_right[c].start)
        pl.when(has_left)(y_left[c].start)
        departures.append(lambda c=c: pl.when(has_right)(y_right[c].wait_send))
        departures.append(lambda c=c: pl.when(has_left)(y_left[c].wait_send))

    end_left = jnp.where(has_left, 1.5, 1.25).astype(F32)
    end_right = jnp.where(has_right, 1.5, 1.25).astype(F32)

    def press(c):
        def step(a, carry):
            p = [pp[c, a, b] for b in range(CY)]
            q = [qq[c, a, b] for b in range(CY)]
            for b in range(CY):
                near_p = [p[k] for k in (b - 1, b + 1) if 0 <= k < CY]
                near_q = [q[k] for k in (b - 1, b + 1) if 0 <= k < CY]
                far_q = [q[k] for k in (b - 2, b + 2) if 0 <= k < CY]
                centre = end_left if b == 0 else end_right if b == CY - 1 else 1.5
                total = ALPHA * s[c, a, b] + p[b] + 0.5 * sum(near_p) + centre * q[b] + sum(near_q) + 0.25 * sum(far_q)
                if b < 2:
                    total = total + yl[c, b, a]
                if b >= CY - 2:
                    total = total + yr[c, CY - 1 - b, a]
                high, low = two(total)
                fp[2 * a + b // 4, :, (b % 4) * 128 : (b % 4 + 1) * 128] = high
                fp[2 * a + b // 4, :, 512 + (b % 4) * 128 : 512 + (b % 4 + 1) * 128] = low
            return carry

        lax.fori_loop(0, CX, step, 0)

    def give(c):
        fields = fp[...].reshape(16 * MC, 1024)
        for times in (range(chips // 2), range(chips // 2, chips)):
            one_hot = jnp.concatenate([rhot[chip_to(t)] for t in times], axis=1)
            row = jnp.concatenate([rowf[chip_to(t), 0:1, :] for t in times], axis=1)
            product = nn(fields, jnp.concatenate([one_hot, one_hot], axis=0))
            total = jnp.where(row == 0, product[0:MC], 0.0)
            for k in range(1, 16):
                total = jnp.where(row == k, product[k * MC : (k + 1) * MC], total)
            for n, t in enumerate(times):
                for core in range(2):
                    at = (2 * n + core) * 128
                    ret[c, 2 * chip_to(t) + core] = total[:, at : at + 128]
            for t in times:
                each_source(chip_to(t), lambda j: back_copy(c, j, me).start())
        back[c, me] = ret[c, me]

    for c in range(CHUNKS):
        pl.when(has_left)(y_right[c].wait_recv)
        pl.when(has_right)(y_left[c].wait_recv)
        press(c)
        give(c)
        departures.append(lambda c=c: each_sub(lambda peer: back_copy(c, peer, me).wait_send()))

    def forces(c):
        each_sub(lambda peer: back_copy(c, peer, peer).wait_recv())
        force = jnp.concatenate([back[c, k] * weight_row(k) for k in range(n_sub)], axis=1)
        product = nt(jnp.concatenate(three(force), axis=0), jnp.concatenate([n2[k] for k in range(chips)], axis=1))
        product = product[0:MC] + product[MC : 2 * MC] + product[2 * MC :]
        return mass_ref[...] * v[c * MC : (c + 1) * MC] + product

    massed = jnp.concatenate([forces(c) for c in range(CHUNKS)], axis=0)
    win_w[2] = massed[:, :128]
    win_w[3] = massed[:, 128:]
    w_start()
    departures.append(w_sent)
    w_arrive()
    image_massed = apply(win_w, massed)

    x_high, x_low = two(jnp.concatenate([v, image, massed], axis=0))
    z_high, z_low = two(
        jnp.concatenate([image, massed, image_image, image_massed, v, jnp.zeros((96, NSD), F32)], axis=0)
    )
    x_both = jnp.concatenate([x_high, x_low], axis=0)
    product = nt(x_both, z_high) + nt(x_both, z_low)
    product = product[:96] + product[96:]
    third = jnp.where(lane < M, product[0:32, 128:], product[64:96, :128])
    whole[0:64, :] = product[0:64, :128]
    whole[64:96, :] = third
    whole[96:128, :] = jnp.zeros((32, 128), F32)
    for g in range(n_sub):
        gbuf[g, 0:rows, :] = whole[g * rows : (g + 1) * rows, :]
    each_sub(lambda peer: gram_copy(peer, me).start())
    departures.append(lambda: each_sub(lambda peer: gram_copy(peer, me).wait_send()))
    grecv[me, 0:rows] = gbuf[me, 0:rows]
    each_sub(lambda peer: gram_copy(peer, peer).wait_recv())
    part[0, 0:rows] = lax.fori_loop(1, n_sub, lambda g, total: total + grecv[g, 0:rows], grecv[0, 0:rows])
    each_passage(lambda peer: part_copy(peer, myp).start())
    departures.append(lambda: each_passage(lambda peer: part_copy(peer, myp).wait_send()))
    precv[myp, 0:rows] = part[0, 0:rows]
    each_passage(lambda peer: part_copy(peer, peer).wait_recv())
    part[1, 0:rows] = lax.fori_loop(1, n_passage, lambda g, total: total + precv[g, 0:rows], precv[0, 0:rows])
    each_sub(lambda peer: full_copy(peer, me).start())
    departures.append(lambda: each_sub(lambda peer: full_copy(peer, me).wait_send()))
    gfull[me, 0:rows] = part[1, 0:rows]
    each_sub(lambda peer: full_copy(peer, peer).wait_recv())

    for g in range(n_sub):
        whole[g * rows : (g + 1) * rows, :] = gfull[g, 0:rows, :]
    turned = whole[...].T
    scale = 1.0 / (NSD * n_sub * n_passage)
    row_of = iota((M, 128), 0)

    def moved(x, blocks):
        return pltpu.roll(x, (128 - 32 * blocks) % 128, 1)

    top, mid, bottom = whole[0:32], whole[32:64], whole[64:96]
    numer = jnp.where(lane == row_of, top, 0.0)
    denom = jnp.where(lane == row_of, moved(top, 1), 0.0)
    theta = jnp.sum(numer, axis=1, keepdims=True) / jnp.sum(denom, axis=1, keepdims=True)
    theta_row = jnp.sum(jnp.where(lane == row_of, theta, 0.0), axis=0, keepdims=True)
    resid_ref[...] = image - theta * massed
    mass_stiff = moved(turned[32:64], 1)
    plain_vr = top - moved(top, 1) * theta_row
    plain_rv = turned[0:32] - theta * turned[32:64]
    stiff_rs = mid - theta * mass_stiff
    plain_rr = stiff_rs - moved(mid, 1) * theta_row + theta * theta_row * moved(bottom, 1)
    stiff_vr = moved(top, 2) - moved(top, 3) * theta_row
    stiff_rr = (
        moved(mid, 2) - theta * moved(bottom, 2) - moved(mid, 3) * theta_row + theta * theta_row * moved(bottom, 3)
    )

    def side(first, second):
        return (jnp.where(lane < M, first, pltpu.roll(second, 32, 1)) * scale)[:, : 2 * M]

    gs_ref[0:M, :] = side(top, stiff_vr)
    gs_ref[M:, :] = side(stiff_rs, stiff_rr)
    gp_ref[0:M, :] = side(bottom, plain_vr)
    gp_ref[M:, :] = side(plain_rv, plain_rr)

    for sent in departures:
        sent()


def body(
    n_passage,
    n_sub,
    block_vectors,
    stiffness,
    mass_diag,
    kblocks,
    block_cols,
    slot_node,
    slot_owner,
    slot_cell,
    slot_weight,
    live_slots,
):
    nc = slot_node.shape[0] // 128
    chips = n_sub // 2
    rows = -(-3 * M // n_sub // 8) * 8
    shapes = (
        jax.ShapeDtypeStruct((M, NSD), F32),
        jax.ShapeDtypeStruct((2 * M, 2 * M), F32),
        jax.ShapeDtypeStruct((2 * M, 2 * M), F32),
    )
    vmem = pl.BlockSpec(memory_space=pltpu.VMEM)
    hbm = pl.BlockSpec(memory_space=pltpu.HBM)
    dma = pltpu.SemaphoreType.DMA
    layers = pltpu.VMEM((CHUNKS, 2, CY, MC, CZ), F32)
    cells = pltpu.VMEM((CHUNKS, CX, CY, MC, CZ), F32)
    return pl.pallas_call(
        functools.partial(kernel, n_passage, n_sub),
        out_shape=shapes,
        in_specs=[hbm] * 10,
        out_specs=(vmem, vmem, vmem),
        scratch_shapes=[
            pltpu.VMEM((M, NSD), F32),
            pltpu.VMEM((1, NSD), F32),
            pltpu.VMEM((1, NSD), F32),
            pltpu.VMEM((2, 512, 128), F32),
            pltpu.SMEM((2, 4), I32),
            pltpu.VMEM((nc, 128), I32),
            pltpu.VMEM((nc, 128), I32),
            pltpu.VMEM((nc, 128), I32),
            pltpu.VMEM((nc, 128), F32),
            pltpu.SMEM((1,), I32),
            dma((10,)),
            pltpu.VMEM((6, M, 128), F32),
            pltpu.VMEM((6, M, 128), F32),
            pltpu.VMEM((6, M, 128), F32),
            pltpu.VMEM((2, 512, 128), BF16),
            pltpu.VMEM((2, 512, 128), BF16),
            pltpu.VMEM((n_sub, 8, 128), F32),
            pltpu.VMEM((chips, NSD, 256), BF16),
            pltpu.VMEM((CHUNKS, n_sub, MC + 8, CAP), F32),
            pltpu.VMEM((CHUNKS, n_sub, MC + 8, CAP), F32),
            pltpu.VMEM((chips, 512, 256), BF16),
            pltpu.VMEM((chips, 8, 256), I32),
            cells,
            layers,
            layers,
            cells,
            cells,
            layers,
            layers,
            layers,
            layers,
            pltpu.VMEM((16, MC, 1024), BF16),
            pltpu.VMEM((CHUNKS, n_sub, MC, CAP), F32),
            pltpu.VMEM((CHUNKS, n_sub, MC, CAP), F32),
            pltpu.VMEM((n_sub, rows, 128), F32),
            pltpu.VMEM((n_sub, rows, 128), F32),
            pltpu.VMEM((2, rows, 128), F32),
            pltpu.VMEM((n_passage, rows, 128), F32),
            pltpu.VMEM((n_sub, rows, 128), F32),
            pltpu.VMEM((128, 128), F32),
            dma((3, 2)),
            dma((3, 2)),
            dma((CHUNKS, n_sub)),
            dma((CHUNKS, n_sub)),
            dma((CHUNKS, 2)),
            dma((CHUNKS, 2)),
            dma((CHUNKS, 2)),
            dma((CHUNKS, 2)),
            dma((CHUNKS, n_sub)),
            dma((CHUNKS, n_sub)),
            dma((n_sub,)),
            dma((n_sub,)),
            dma((n_passage,)),
            dma((n_passage,)),
            dma((n_sub,)),
            dma((n_sub,)),
        ],
        compiler_params=pltpu.CompilerParams(
            collective_id=0, has_side_effects=True, vmem_limit_bytes=60 * 1024 * 1024
        ),
    )(
        block_vectors,
        stiffness.reshape(1, NSD),
        mass_diag.reshape(1, NSD),
        kblocks.reshape(2, 512, 128),
        block_cols,
        slot_node.reshape(nc, 128),
        slot_owner.reshape(nc, 128),
        slot_cell.reshape(nc, 128),
        slot_weight.reshape(nc, 128),
        live_slots,
    )


def solution(mesh):
    return jax.shard_map(
        functools.partial(body, mesh.shape["passage"], mesh.shape["sub"]),
        mesh=mesh,
        in_specs=(
            P(None, ("passage", "sub")),
            P(("passage", "sub")),
            P(("passage", "sub")),
            P(("passage", "sub"), None, None, None),
            P(("passage", "sub"), None),
            P(("passage", "sub")),
            P(("passage", "sub"), None),
            P(("passage", "sub")),
            P(("passage", "sub")),
            P(("passage", "sub")),
        ),
        out_specs=(P(None, ("passage", "sub")), P(), P()),
        check_vma=False,
    )
```

```python
import functools

import jax
import jax.numpy as jnp
from jax import lax
from jax.experimental import pallas as pl
from jax.experimental.pallas import tpu as pltpu
from jax.sharding import PartitionSpec as P

MESH = pl.DeviceIdType.MESH
F32 = jnp.float32
BF16 = jnp.bfloat16
I32 = jnp.int32

M = 32
CX = 8
CY = 8
CZ = 128
CAP = 128
NSD = 256
CHUNKS = 2
MC = M // CHUNKS

center_weight = 15.0
lower_bound = 1.0 / 15.0
upper_bound = 17.0 / 15.0
middle = (upper_bound + lower_bound) / 2.0
radius = (upper_bound - lower_bound) / 2.0
sigma_ratio = middle / radius
first_rho = 1.0 / sigma_ratio
second_rho = 1.0 / (2.0 * sigma_ratio - first_rho)
third_rho = 1.0 / (2.0 * sigma_ratio - second_rho)
FIRST = 1.0 / (center_weight * middle)
GAIN_TWO = 2.0 * second_rho / radius / center_weight
GAIN_THREE = 2.0 * third_rho / radius / center_weight
STEP_ONE = second_rho * first_rho * FIRST + GAIN_TWO * (1.0 - 17.0 * FIRST)
STEP_T = GAIN_TWO * 2.0 * FIRST
ALPHA = FIRST + STEP_ONE + third_rho * second_rho * STEP_ONE + GAIN_THREE * (1.0 - 17.0 * (FIRST + STEP_ONE))
BETA = STEP_T + third_rho * second_rho * STEP_T + GAIN_THREE * (2.0 * (FIRST + STEP_ONE) - 17.0 * STEP_T)
GAMMA = GAIN_THREE * 2.0 * STEP_T


def iota(shape, dim):
    return lax.broadcasted_iota(I32, shape, dim)


def nn(left, right):
    return jnp.dot(left, right, preferred_element_type=F32)


def nt(left, right):
    return lax.dot_general(left, right, (((1,), (1,)), ((), ())), preferred_element_type=F32)


def two(x):
    high = x.astype(BF16)
    return high, (x - high.astype(F32)).astype(BF16)


def three(x):
    high, rest = x.astype(BF16), None
    rest = x - high.astype(F32)
    middle_part = rest.astype(BF16)
    return high, middle_part, (rest - middle_part.astype(F32)).astype(BF16)


def kernel(
    n_passage,
    n_sub,
    v_hbm,
    stiff_hbm,
    mass_hbm,
    kb_hbm,
    cols_hbm,
    node_hbm,
    owner_hbm,
    cell_hbm,
    weight_hbm,
    live_hbm,
    resid_ref,
    gs_ref,
    gp_ref,
    v_ref,
    stiff_ref,
    mass_ref,
    kb_ref,
    cols_ref,
    node_ref,
    owner_ref,
    cell_ref,
    weight_ref,
    live_ref,
    in_sem,
    win_v,
    win_s,
    win_w,
    kbh,
    kbl,
    mt,
    n2,
    out,
    inc,
    rhot,
    rowf,
    s,
    xl,
    xr,
    pp,
    qq,
    ysl,
    ysr,
    yl,
    yr,
    fp,
    ret,
    back,
    gbuf,
    grecv,
    part,
    precv,
    gfull,
    whole,
    nb_send,
    nb_recv,
    a_send,
    a_recv,
    x_send,
    x_recv,
    y_send,
    y_recv,
    b_send,
    b_recv,
    g_send,
    g_recv,
    p_send,
    p_recv,
    f_send,
    f_recv,
):
    chips = n_sub // 2
    ni = node_ref.shape[0] * 128
    nc = node_ref.shape[0]
    rows = 3 * M // n_sub
    myp = lax.axis_index("passage")
    me = lax.axis_index("sub")
    chip = me // 2
    left_p = lax.rem(myp + n_passage - 1, n_passage)
    right_p = lax.rem(myp + 1, n_passage)
    has_left = me > 0
    has_right = me < n_sub - 1

    def sub_copy(src, dst, send, recv, peer):
        return pltpu.make_async_remote_copy(
            src_ref=src, dst_ref=dst, send_sem=send, recv_sem=recv,
            device_id={"sub": peer}, device_id_type=MESH,
        )

    def passage_copy(src, dst, send, recv, peer):
        return pltpu.make_async_remote_copy(
            src_ref=src, dst_ref=dst, send_sem=send, recv_sem=recv,
            device_id={"passage": peer}, device_id_type=MESH,
        )

    arguments = (
        (node_hbm, node_ref),
        (owner_hbm, owner_ref),
        (cell_hbm, cell_ref),
        (weight_hbm, weight_ref),
        (live_hbm, live_ref),
        (v_hbm, v_ref),
        (kb_hbm, kb_ref),
        (stiff_hbm, stiff_ref),
        (mass_hbm, mass_ref),
        (cols_hbm, cols_ref),
    )
    loads = [pltpu.make_async_copy(src, dst, in_sem.at[k]) for k, (src, dst) in enumerate(arguments)]
    for load in loads:
        load.start()

    for win in (win_v, win_s, win_w):
        win[0:2] = jnp.zeros((2, M, 128), F32)
        win[4:6] = jnp.zeros((2, M, 128), F32)

    @pl.when(jnp.logical_not(has_left))
    def _():
        yl[...] = jnp.zeros_like(yl)

    @pl.when(jnp.logical_not(has_right))
    def _():
        yr[...] = jnp.zeros_like(yr)

    barrier = pltpu.get_barrier_semaphore()

    def greet_sub(i):
        pl.semaphore_signal(barrier, inc=1, device_id={"sub": lax.rem(me + i, n_sub)}, device_id_type=MESH)

    def greet_passage(i):
        pl.semaphore_signal(barrier, inc=1, device_id={"passage": lax.rem(myp + i, n_passage)}, device_id_type=MESH)

    for i in range(1, n_sub):
        greet_sub(i)
    for i in range(1, n_passage):
        greet_passage(i)

    for load in loads[:5]:
        load.wait()

    owner = owner_ref[...]
    lane_of_slot = iota((1, ni), 1)

    def flat(x):
        return jnp.concatenate([x[c : c + 1, :] for c in range(nc)], axis=1)

    group = iota((n_sub, 128), 0)
    hot = [(owner[c : c + 1, :] == group).astype(F32) for c in range(nc)]
    upper = (iota((128, 128), 0) < iota((128, 128), 1)).astype(F32).astype(BF16)
    before = nn(jnp.concatenate(hot, axis=0).astype(BF16), upper)
    ahead = jnp.zeros((n_sub, 1), F32)
    ranks = []
    for c in range(nc):
        ranks.append(jnp.sum(hot[c] * (before[c * n_sub : (c + 1) * n_sub] + ahead), axis=0, keepdims=True))
        ahead = ahead + jnp.sum(hot[c], axis=1, keepdims=True)
    rank = jnp.concatenate(ranks, axis=1).astype(I32)
    rank_hot = (iota((CAP, ni), 0) == rank).astype(F32).astype(BF16)
    node = flat(node_ref[...]).astype(F32)
    cell = flat(cell_ref[...])
    weight = jnp.where(lane_of_slot < live_ref[0], flat(weight_ref[...]), 0.0)
    w0, w1, w2 = three(weight)
    which = iota((8, ni), 0)
    meta = jnp.zeros((8, ni), F32)
    for row, values in enumerate(
        (((cell >> 7) << 7).astype(F32), (cell & 127).astype(F32), node, w0.astype(F32), w1.astype(F32), w2.astype(F32))
    ):
        meta = jnp.where(which == row, values, meta)
    owner_row = flat(owner)
    lhs = jnp.concatenate([jnp.where(owner_row == g, meta, 0.0) for g in range(n_sub)], axis=0).astype(BF16)
    placed = nt(lhs, rank_hot)
    for g in range(n_sub):
        mt[g] = placed[g * 8 : (g + 1) * 8]
    for load in loads[5:]:
        load.wait()
    v = v_ref[...]
    win_v[2] = v[:, :128]
    win_v[3] = v[:, 128:]

    pl.semaphore_wait(barrier, n_sub - 1 + n_passage - 1)

    def exchange(win, k):
        to_right = sub_copy(win.at[pl.ds(2, 2)], win.at[pl.ds(0, 2)], nb_send.at[k, 0], nb_recv.at[k, 0], me + 1)
        to_left = sub_copy(win.at[pl.ds(2, 2)], win.at[pl.ds(4, 2)], nb_send.at[k, 1], nb_recv.at[k, 1], me - 1)

        def start():
            pl.when(has_right)(to_right.start)
            pl.when(has_left)(to_left.start)

        def arrive():
            pl.when(has_left)(to_right.wait_recv)
            pl.when(has_right)(to_left.wait_recv)

        def sent():
            pl.when(has_right)(to_right.wait_send)
            pl.when(has_left)(to_left.wait_send)

        return start, arrive, sent

    v_start, v_arrive, v_sent = exchange(win_v, 0)
    s_start, s_arrive, s_sent = exchange(win_s, 1)
    w_start, w_arrive, w_sent = exchange(win_w, 2)

    def out_copy(c, peer, slot):
        sent_rows = pl.ds(0, MC + 2 if c == 0 else MC)
        return sub_copy(
            out.at[c, peer, sent_rows], inc.at[c, slot, sent_rows], a_send.at[c, peer], a_recv.at[c, slot], peer
        )

    def back_copy(c, peer, slot):
        return sub_copy(ret.at[c, peer], back.at[c, slot], b_send.at[c, peer], b_recv.at[c, slot], peer)

    kept = pl.ds(0, rows)

    def gram_copy(peer, slot):
        return sub_copy(gbuf.at[peer, kept], grecv.at[slot, kept], g_send.at[peer], g_recv.at[slot], peer)

    def full_copy(peer, slot):
        return sub_copy(part.at[1, kept], gfull.at[slot, kept], f_send.at[peer], f_recv.at[slot], peer)

    def part_copy(peer, slot):
        return passage_copy(part.at[0, kept], precv.at[slot, kept], p_send.at[peer], p_recv.at[slot], peer)

    def far_first(k, count):
        half = (k + 1) // 2
        return count // 2 + (-half if k % 2 else half)

    def each_sub(act):
        for k in range(n_sub - 1):
            act(lax.rem(me + far_first(k, n_sub), n_sub))

    def each_passage(act):
        for k in range(n_passage - 1):
            act(lax.rem(myp + far_first(k, n_passage), n_passage))

    def chip_to(t):
        return lax.rem(chip + far_first(t, chips), chips)

    v_start()
    departures = [v_sent]

    v3 = jnp.concatenate(three(v), axis=0)
    node_of = iota((NSD, 128), 0)

    def weight_row(g):
        return mt[g, 3:4, :] + mt[g, 4:5, :] + mt[g, 5:6, :]

    def send_step(t):
        there = chip_to(t)
        parts = [(node_of == mt[2 * there + core, 2:3, :].astype(I32)).astype(F32) for core in range(2)]
        one_hot = jnp.concatenate(parts, axis=1).astype(BF16)
        n2[there] = one_hot
        picked = nn(v3, one_hot)
        picked = picked[0:M] + picked[M : 2 * M] + picked[2 * M :]
        for core in range(2):
            g = 2 * there + core
            values = picked[:, core * 128 : (core + 1) * 128] * weight_row(g)
            for c in range(CHUNKS):
                out[c, g, 0:MC, :] = values[c * MC : (c + 1) * MC]
            out[0, g, MC : MC + 2, :] = mt[g, 0:2, :]
            pl.when(g != me)(out_copy(0, g, me).start)

    for t in range(chips):
        send_step(t)
    inc[0, me, 0 : MC + 2] = out[0, me, 0 : MC + 2]

    for r in range(2):
        kb = kb_ref[r]
        high, low = two(kb)
        kbh[r] = high
        kbl[r] = low

    stiff = stiff_ref[...]

    def apply(win, own):
        mixed = []
        for r in range(2):
            blocks = jnp.concatenate([win[cols_ref[r, n]] for n in range(4)], axis=1)
            high, low = two(blocks)
            both = nn(jnp.concatenate([high, low], axis=0), kbh[r])
            mixed.append(both[:M] + both[M:] + nn(high, kbl[r]))
        return stiff * own + jnp.concatenate(mixed, axis=1)

    v_arrive()
    image = apply(win_v, v)
    win_s[2] = image[:, :128]
    win_s[3] = image[:, 128:]
    s_start()
    departures.append(s_sent)
    for c in range(1, CHUNKS):
        each_sub(lambda peer: out_copy(c - 1, peer, me).wait_send())
        each_sub(lambda peer: out_copy(c, peer, me).start())
        inc[c, me, 0:MC] = out[c, me, 0:MC]
    departures.append(lambda: each_sub(lambda peer: out_copy(CHUNKS - 1, peer, me).wait_send()))

    place = iota((512, 256), 0)

    def rows_of(there):
        high = jnp.concatenate([inc[0, 2 * there + k, MC : MC + 1, :] for k in range(2)], axis=1).astype(I32)
        low = jnp.concatenate([inc[0, 2 * there + k, MC + 1 : MC + 2, :] for k in range(2)], axis=1).astype(I32)
        return high >> 9, (high & 511) + low

    def each_source(there, act):
        for core in range(2):
            j = 2 * there + core
            pl.when(j != me)(functools.partial(act, j))

    def take(c):
        each_sub(lambda peer: out_copy(c, peer, peer).wait_recv())
        if c == 0:

            for there in range(chips):
                row, column = rows_of(there)
                rhot[there] = (place == column).astype(F32).astype(BF16)
                rowf[there] = jnp.broadcast_to(row, (8, 256))
        one_hot = jnp.concatenate([rhot[k] for k in range(chips)], axis=1)
        row = jnp.concatenate([rowf[k, 0:1, :] for k in range(chips)], axis=1)
        high, low = two(jnp.concatenate([inc[c, k, 0:MC, :] for k in range(n_sub)], axis=1))
        highs, lows = [], []
        for k in range(16):
            mask = jnp.broadcast_to((row == k).astype(F32), (MC, n_sub * CAP)).astype(BF16)
            highs.append(high * mask)
            lows.append(low * mask)
        terms = jnp.concatenate([jnp.concatenate(highs, axis=0), jnp.concatenate(lows, axis=0)], axis=1)
        product = nt(terms, jnp.concatenate([one_hot, one_hot], axis=1))
        for k in range(16):
            for q in range(4):
                s[c, k // 2, (k % 2) * 4 + q] = product[k * MC : (k + 1) * MC, q * 128 : (q + 1) * 128]

    x_right = [
        passage_copy(s.at[c, pl.ds(6, 2)], xl.at[c], x_send.at[c, 0], x_recv.at[c, 0], right_p) for c in range(CHUNKS)
    ]
    x_left = [
        passage_copy(s.at[c, pl.ds(0, 2)], xr.at[c], x_send.at[c, 1], x_recv.at[c, 1], left_p) for c in range(CHUNKS)
    ]
    for c in range(CHUNKS):
        take(c)
        x_right[c].start()
        x_left[c].start()
        departures += [x_right[c].wait_send, x_left[c].wait_send]

    s_arrive()
    image_image = apply(win_s, image)

    lane = iota((M, 128), 1)
    apart = jnp.abs(iota((128, 128), 0) - iota((128, 128), 1))
    at_end = (iota((128, 128), 0) == 0) | (iota((128, 128), 0) == 127)
    once = jnp.where(apart == 0, 1.0, jnp.where(apart == 1, 0.5, 0.0))
    middle_weight = jnp.where(at_end, 1.25, 1.5)
    twice = jnp.where(apart == 0, middle_weight, jnp.where(apart == 1, 1.0, jnp.where(apart == 2, 0.25, 0.0)))
    once = jnp.concatenate([once, once], axis=0).astype(BF16)
    twice = jnp.concatenate([twice, twice], axis=0).astype(BF16)

    def filters(c, layers):
        def layer(a, b):
            if a < 0:
                return xl[c, a + 2, b]
            if a >= CX:
                return xr[c, a - CX, b]
            return s[c, a, b]

        ps, qs = [], []
        for a in layers:
            for b in range(CY):
                near = layer(a - 1, b) + layer(a + 1, b)
                mine = layer(a, b)
                far = layer(a - 2, b) + layer(a + 2, b)
                ps.append(jnp.concatenate(two(mine + 0.5 * near), axis=1))
                qs.append(jnp.concatenate(two(1.5 * mine + near + 0.25 * far), axis=1))
        p = BETA * nn(jnp.concatenate(ps, axis=0), once)
        q = GAMMA * nn(jnp.concatenate(qs, axis=0), twice)
        for n, a in enumerate(layers):
            for b in range(CY):
                at = (n * CY + b) * MC
                pp[c, a, b] = p[at : at + MC]
                qq[c, a, b] = q[at : at + MC]

    y_right = [sub_copy(ysr.at[c], yl.at[c], y_send.at[c, 0], y_recv.at[c, 0], me + 1) for c in range(CHUNKS)]
    y_left = [sub_copy(ysl.at[c], yr.at[c], y_send.at[c, 1], y_recv.at[c, 1], me - 1) for c in range(CHUNKS)]
    for c in range(CHUNKS):
        filters(c, (2, 3, 4, 5))
        x_right[c].wait_recv()
        x_left[c].wait_recv()
        filters(c, (0, 1, 6, 7))

        for a in range(CX):
            ysr[c, 0, a] = 0.5 * pp[c, a, 7] + 0.25 * qq[c, a, 6] + qq[c, a, 7]
            ysr[c, 1, a] = 0.25 * qq[c, a, 7]
            ysl[c, 0, a] = 0.5 * pp[c, a, 0] + 0.25 * qq[c, a, 1] + qq[c, a, 0]
            ysl[c, 1, a] = 0.25 * qq[c, a, 0]
        pl.when(has_right)(y_right[c].start)
        pl.when(has_left)(y_left[c].start)
        departures.append(lambda c=c: pl.when(has_right)(y_right[c].wait_send))
        departures.append(lambda c=c: pl.when(has_left)(y_left[c].wait_send))

    end_left = jnp.where(has_left, 1.5, 1.25).astype(F32)
    end_right = jnp.where(has_right, 1.5, 1.25).astype(F32)

    def press(c):
        def step(a, carry):
            p = [pp[c, a, b] for b in range(CY)]
            q = [qq[c, a, b] for b in range(CY)]
            for b in range(CY):
                near_p = [p[k] for k in (b - 1, b + 1) if 0 <= k < CY]
                near_q = [q[k] for k in (b - 1, b + 1) if 0 <= k < CY]
                far_q = [q[k] for k in (b - 2, b + 2) if 0 <= k < CY]
                centre = end_left if b == 0 else end_right if b == CY - 1 else 1.5
                total = ALPHA * s[c, a, b] + p[b] + 0.5 * sum(near_p) + centre * q[b] + sum(near_q) + 0.25 * sum(far_q)
                if b < 2:
                    total = total + yl[c, b, a]
                if b >= CY - 2:
                    total = total + yr[c, CY - 1 - b, a]
                high, low = two(total)
                fp[2 * a + b // 4, :, (b % 4) * 128 : (b % 4 + 1) * 128] = high
                fp[2 * a + b // 4, :, 512 + (b % 4) * 128 : 512 + (b % 4 + 1) * 128] = low
            return carry

        lax.fori_loop(0, CX, step, 0)

    def give(c):
        fields = fp[...].reshape(16 * MC, 1024)
        for times in (range(chips // 2), range(chips // 2, chips)):
            one_hot = jnp.concatenate([rhot[chip_to(t)] for t in times], axis=1)
            row = jnp.concatenate([rowf[chip_to(t), 0:1, :] for t in times], axis=1)
            product = nn(fields, jnp.concatenate([one_hot, one_hot], axis=0))
            total = jnp.where(row == 0, product[0:MC], 0.0)
            for k in range(1, 16):
                total = jnp.where(row == k, product[k * MC : (k + 1) * MC], total)
            for n, t in enumerate(times):
                for core in range(2):
                    at = (2 * n + core) * 128
                    ret[c, 2 * chip_to(t) + core] = total[:, at : at + 128]
            for t in times:
                each_source(chip_to(t), lambda j: back_copy(c, j, me).start())
        back[c, me] = ret[c, me]

    for c in range(CHUNKS):
        pl.when(has_left)(y_right[c].wait_recv)
        pl.when(has_right)(y_left[c].wait_recv)
        press(c)
        give(c)
        departures.append(lambda c=c: each_sub(lambda peer: back_copy(c, peer, me).wait_send()))

    def forces(c):
        each_sub(lambda peer: back_copy(c, peer, peer).wait_recv())
        force = jnp.concatenate([back[c, k] * weight_row(k) for k in range(n_sub)], axis=1)
        product = nt(jnp.concatenate(three(force), axis=0), jnp.concatenate([n2[k] for k in range(chips)], axis=1))
        product = product[0:MC] + product[MC : 2 * MC] + product[2 * MC :]
        return mass_ref[...] * v[c * MC : (c + 1) * MC] + product

    massed = jnp.concatenate([forces(c) for c in range(CHUNKS)], axis=0)
    win_w[2] = massed[:, :128]
    win_w[3] = massed[:, 128:]
    w_start()
    departures.append(w_sent)
    w_arrive()
    image_massed = apply(win_w, massed)

    x_high, x_low = two(jnp.concatenate([v, image, massed], axis=0))
    z_high, z_low = two(
        jnp.concatenate([image, massed, image_image, image_massed, v, jnp.zeros((96, NSD), F32)], axis=0)
    )
    x_both = jnp.concatenate([x_high, x_low], axis=0)
    product = nt(x_both, z_high) + nt(x_both, z_low)
    product = product[:96] + product[96:]
    third = jnp.where(lane < M, product[0:32, 128:], product[64:96, :128])
    whole[0:64, :] = product[0:64, :128]
    whole[64:96, :] = third
    whole[96:128, :] = jnp.zeros((32, 128), F32)
    for g in range(n_sub):
        gbuf[g, 0:rows, :] = whole[g * rows : (g + 1) * rows, :]
    each_sub(lambda peer: gram_copy(peer, me).start())
    departures.append(lambda: each_sub(lambda peer: gram_copy(peer, me).wait_send()))
    grecv[me, 0:rows] = gbuf[me, 0:rows]
    each_sub(lambda peer: gram_copy(peer, peer).wait_recv())
    part[0, 0:rows] = sum(grecv[g, 0:rows] for g in range(n_sub))
    each_passage(lambda peer: part_copy(peer, myp).start())
    departures.append(lambda: each_passage(lambda peer: part_copy(peer, myp).wait_send()))
    precv[myp, 0:rows] = part[0, 0:rows]
    each_passage(lambda peer: part_copy(peer, peer).wait_recv())
    part[1, 0:rows] = sum(precv[g, 0:rows] for g in range(n_passage))
    each_sub(lambda peer: full_copy(peer, me).start())
    departures.append(lambda: each_sub(lambda peer: full_copy(peer, me).wait_send()))
    gfull[me, 0:rows] = part[1, 0:rows]
    each_sub(lambda peer: full_copy(peer, peer).wait_recv())

    for g in range(n_sub):
        whole[g * rows : (g + 1) * rows, :] = gfull[g, 0:rows, :]
    turned = whole[...].T
    scale = 1.0 / (NSD * n_sub * n_passage)
    row_of = iota((M, 128), 0)

    def moved(x, blocks):
        return pltpu.roll(x, (128 - 32 * blocks) % 128, 1)

    top, mid, bottom = whole[0:32], whole[32:64], whole[64:96]
    numer = jnp.where(lane == row_of, top, 0.0)
    denom = jnp.where(lane == row_of, moved(top, 1), 0.0)
    theta = jnp.sum(numer, axis=1, keepdims=True) / jnp.sum(denom, axis=1, keepdims=True)
    theta_row = jnp.sum(jnp.where(lane == row_of, theta, 0.0), axis=0, keepdims=True)
    resid_ref[...] = image - theta * massed
    mass_stiff = moved(turned[32:64], 1)
    plain_vr = top - moved(top, 1) * theta_row
    plain_rv = turned[0:32] - theta * turned[32:64]
    stiff_rs = mid - theta * mass_stiff
    plain_rr = stiff_rs - moved(mid, 1) * theta_row + theta * theta_row * moved(bottom, 1)
    stiff_vr = moved(top, 2) - moved(top, 3) * theta_row
    stiff_rr = (
        moved(mid, 2) - theta * moved(bottom, 2) - moved(mid, 3) * theta_row + theta * theta_row * moved(bottom, 3)
    )

    def side(first, second):
        return (jnp.where(lane < M, first, pltpu.roll(second, 32, 1)) * scale)[:, : 2 * M]

    gs_ref[0:M, :] = side(top, stiff_vr)
    gs_ref[M:, :] = side(stiff_rs, stiff_rr)
    gp_ref[0:M, :] = side(bottom, plain_vr)
    gp_ref[M:, :] = side(plain_rv, plain_rr)

    for sent in departures:
        sent()


def body(
    n_passage,
    n_sub,
    block_vectors,
    stiffness,
    mass_diag,
    kblocks,
    block_cols,
    slot_node,
    slot_owner,
    slot_cell,
    slot_weight,
    live_slots,
):
    nc = slot_node.shape[0] // 128
    chips = n_sub // 2
    rows = -(-3 * M // n_sub // 8) * 8
    shapes = (
        jax.ShapeDtypeStruct((M, NSD), F32),
        jax.ShapeDtypeStruct((2 * M, 2 * M), F32),
        jax.ShapeDtypeStruct((2 * M, 2 * M), F32),
    )
    vmem = pl.BlockSpec(memory_space=pltpu.VMEM)
    hbm = pl.BlockSpec(memory_space=pltpu.HBM)
    dma = pltpu.SemaphoreType.DMA
    layers = pltpu.VMEM((CHUNKS, 2, CY, MC, CZ), F32)
    cells = pltpu.VMEM((CHUNKS, CX, CY, MC, CZ), F32)
    return pl.pallas_call(
        functools.partial(kernel, n_passage, n_sub),
        out_shape=shapes,
        in_specs=[hbm] * 10,
        out_specs=(vmem, vmem, vmem),
        scratch_shapes=[
            pltpu.VMEM((M, NSD), F32),
            pltpu.VMEM((1, NSD), F32),
            pltpu.VMEM((1, NSD), F32),
            pltpu.VMEM((2, 512, 128), F32),
            pltpu.SMEM((2, 4), I32),
            pltpu.VMEM((nc, 128), I32),
            pltpu.VMEM((nc, 128), I32),
            pltpu.VMEM((nc, 128), I32),
            pltpu.VMEM((nc, 128), F32),
            pltpu.SMEM((1,), I32),
            dma((10,)),
            pltpu.VMEM((6, M, 128), F32),
            pltpu.VMEM((6, M, 128), F32),
            pltpu.VMEM((6, M, 128), F32),
            pltpu.VMEM((2, 512, 128), BF16),
            pltpu.VMEM((2, 512, 128), BF16),
            pltpu.VMEM((n_sub, 8, 128), F32),
            pltpu.VMEM((chips, NSD, 256), BF16),
            pltpu.VMEM((CHUNKS, n_sub, MC + 8, CAP), F32),
            pltpu.VMEM((CHUNKS, n_sub, MC + 8, CAP), F32),
            pltpu.VMEM((chips, 512, 256), BF16),
            pltpu.VMEM((chips, 8, 256), I32),
            cells,
            layers,
            layers,
            cells,
            cells,
            layers,
            layers,
            layers,
            layers,
            pltpu.VMEM((16, MC, 1024), BF16),
            pltpu.VMEM((CHUNKS, n_sub, MC, CAP), F32),
            pltpu.VMEM((CHUNKS, n_sub, MC, CAP), F32),
            pltpu.VMEM((n_sub, rows, 128), F32),
            pltpu.VMEM((n_sub, rows, 128), F32),
            pltpu.VMEM((2, rows, 128), F32),
            pltpu.VMEM((n_passage, rows, 128), F32),
            pltpu.VMEM((n_sub, rows, 128), F32),
            pltpu.VMEM((128, 128), F32),
            dma((3, 2)),
            dma((3, 2)),
            dma((CHUNKS, n_sub)),
            dma((CHUNKS, n_sub)),
            dma((CHUNKS, 2)),
            dma((CHUNKS, 2)),
            dma((CHUNKS, 2)),
            dma((CHUNKS, 2)),
            dma((CHUNKS, n_sub)),
            dma((CHUNKS, n_sub)),
            dma((n_sub,)),
            dma((n_sub,)),
            dma((n_passage,)),
            dma((n_passage,)),
            dma((n_sub,)),
            dma((n_sub,)),
        ],
        compiler_params=pltpu.CompilerParams(
            collective_id=0, has_side_effects=True, vmem_limit_bytes=60 * 1024 * 1024
        ),
    )(
        block_vectors,
        stiffness.reshape(1, NSD),
        mass_diag.reshape(1, NSD),
        kblocks.reshape(2, 512, 128),
        block_cols,
        slot_node.reshape(nc, 128),
        slot_owner.reshape(nc, 128),
        slot_cell.reshape(nc, 128),
        slot_weight.reshape(nc, 128),
        live_slots,
    )


def solution(mesh):
    return jax.shard_map(
        functools.partial(body, mesh.shape["passage"], mesh.shape["sub"]),
        mesh=mesh,
        in_specs=(
            P(None, ("passage", "sub")),
            P(("passage", "sub")),
            P(("passage", "sub")),
            P(("passage", "sub"), None, None, None),
            P(("passage", "sub"), None),
            P(("passage", "sub")),
            P(("passage", "sub"), None),
            P(("passage", "sub")),
            P(("passage", "sub")),
            P(("passage", "sub")),
        ),
        out_specs=(P(None, ("passage", "sub")), P(), P()),
        check_vma=False,
    )
```

```python
import functools

import jax
import jax.numpy as jnp
from jax import lax
from jax.experimental import pallas as pl
from jax.experimental.pallas import tpu as pltpu
from jax.sharding import PartitionSpec as P

MESH = pl.DeviceIdType.MESH
F32 = jnp.float32
BF16 = jnp.bfloat16
I32 = jnp.int32

M = 32
CX = 8
CY = 8
CZ = 128
CAP = 128
NSD = 256
CHUNKS = 2
MC = M // CHUNKS

center_weight = 15.0
lower_bound = 1.0 / 15.0
upper_bound = 17.0 / 15.0
middle = (upper_bound + lower_bound) / 2.0
radius = (upper_bound - lower_bound) / 2.0
sigma_ratio = middle / radius
first_rho = 1.0 / sigma_ratio
second_rho = 1.0 / (2.0 * sigma_ratio - first_rho)
third_rho = 1.0 / (2.0 * sigma_ratio - second_rho)
FIRST = 1.0 / (center_weight * middle)
GAIN_TWO = 2.0 * second_rho / radius / center_weight
GAIN_THREE = 2.0 * third_rho / radius / center_weight
STEP_ONE = second_rho * first_rho * FIRST + GAIN_TWO * (1.0 - 17.0 * FIRST)
STEP_T = GAIN_TWO * 2.0 * FIRST
ALPHA = FIRST + STEP_ONE + third_rho * second_rho * STEP_ONE + GAIN_THREE * (1.0 - 17.0 * (FIRST + STEP_ONE))
BETA = STEP_T + third_rho * second_rho * STEP_T + GAIN_THREE * (2.0 * (FIRST + STEP_ONE) - 17.0 * STEP_T)
GAMMA = GAIN_THREE * 2.0 * STEP_T


def iota(shape, dim):
    return lax.broadcasted_iota(I32, shape, dim)


def nn(left, right):
    return jnp.dot(left, right, preferred_element_type=F32)


def nt(left, right):
    return lax.dot_general(left, right, (((1,), (1,)), ((), ())), preferred_element_type=F32)


def two(x):
    high = x.astype(BF16)
    return high, (x - high.astype(F32)).astype(BF16)


def three(x):
    high, rest = x.astype(BF16), None
    rest = x - high.astype(F32)
    middle_part = rest.astype(BF16)
    return high, middle_part, (rest - middle_part.astype(F32)).astype(BF16)


def kernel(
    n_passage,
    n_sub,
    v_hbm,
    stiff_hbm,
    mass_hbm,
    kb_hbm,
    cols_hbm,
    node_hbm,
    owner_hbm,
    cell_hbm,
    weight_hbm,
    live_hbm,
    resid_ref,
    gs_ref,
    gp_ref,
    v_ref,
    stiff_ref,
    mass_ref,
    kb_ref,
    cols_ref,
    node_ref,
    owner_ref,
    cell_ref,
    weight_ref,
    live_ref,
    in_sem,
    win_v,
    win_s,
    win_w,
    kbh,
    kbl,
    mt,
    n2,
    out,
    inc,
    rhot,
    rowf,
    s,
    xl,
    xr,
    pp,
    qq,
    ysl,
    ysr,
    yl,
    yr,
    fp,
    ret,
    back,
    gbuf,
    grecv,
    part,
    precv,
    gfull,
    whole,
    nb_send,
    nb_recv,
    a_send,
    a_recv,
    x_send,
    x_recv,
    y_send,
    y_recv,
    b_send,
    b_recv,
    g_send,
    g_recv,
    p_send,
    p_recv,
    f_send,
    f_recv,
):
    chips = n_sub // 2
    ni = node_ref.shape[0] * 128
    nc = node_ref.shape[0]
    rows = 3 * M // n_sub
    myp = lax.axis_index("passage")
    me = lax.axis_index("sub")
    chip = me // 2
    left_p = lax.rem(myp + n_passage - 1, n_passage)
    right_p = lax.rem(myp + 1, n_passage)
    has_left = me > 0
    has_right = me < n_sub - 1

    def sub_copy(src, dst, send, recv, peer):
        return pltpu.make_async_remote_copy(
            src_ref=src, dst_ref=dst, send_sem=send, recv_sem=recv,
            device_id={"sub": peer}, device_id_type=MESH,
        )

    def passage_copy(src, dst, send, recv, peer):
        return pltpu.make_async_remote_copy(
            src_ref=src, dst_ref=dst, send_sem=send, recv_sem=recv,
            device_id={"passage": peer}, device_id_type=MESH,
        )

    arguments = (
        (node_hbm, node_ref),
        (owner_hbm, owner_ref),
        (cell_hbm, cell_ref),
        (weight_hbm, weight_ref),
        (live_hbm, live_ref),
        (v_hbm, v_ref),
        (kb_hbm, kb_ref),
        (stiff_hbm, stiff_ref),
        (mass_hbm, mass_ref),
        (cols_hbm, cols_ref),
    )
    loads = [pltpu.make_async_copy(src, dst, in_sem.at[k]) for k, (src, dst) in enumerate(arguments)]
    for load in loads:
        load.start()

    for win in (win_v, win_s, win_w):
        win[0:2] = jnp.zeros((2, M, 128), F32)
        win[4:6] = jnp.zeros((2, M, 128), F32)

    @pl.when(jnp.logical_not(has_left))
    def _():
        yl[...] = jnp.zeros_like(yl)

    @pl.when(jnp.logical_not(has_right))
    def _():
        yr[...] = jnp.zeros_like(yr)

    barrier = pltpu.get_barrier_semaphore()

    def greet_sub(i, carry):
        pl.semaphore_signal(barrier, inc=1, device_id={"sub": lax.rem(me + i, n_sub)}, device_id_type=MESH)
        return carry

    def greet_passage(i, carry):
        pl.semaphore_signal(barrier, inc=1, device_id={"passage": lax.rem(myp + i, n_passage)}, device_id_type=MESH)
        return carry

    lax.fori_loop(1, n_sub, greet_sub, 0)
    lax.fori_loop(1, n_passage, greet_passage, 0)

    for load in loads[:5]:
        load.wait()

    owner = owner_ref[...]
    lane_of_slot = iota((1, ni), 1)

    def flat(x):
        return jnp.concatenate([x[c : c + 1, :] for c in range(nc)], axis=1)

    group = iota((n_sub, 128), 0)
    hot = [(owner[c : c + 1, :] == group).astype(F32) for c in range(nc)]
    upper = (iota((128, 128), 0) < iota((128, 128), 1)).astype(F32).astype(BF16)
    before = nn(jnp.concatenate(hot, axis=0).astype(BF16), upper)
    ahead = jnp.zeros((n_sub, 1), F32)
    ranks = []
    for c in range(nc):
        ranks.append(jnp.sum(hot[c] * (before[c * n_sub : (c + 1) * n_sub] + ahead), axis=0, keepdims=True))
        ahead = ahead + jnp.sum(hot[c], axis=1, keepdims=True)
    rank = jnp.concatenate(ranks, axis=1).astype(I32)
    rank_hot = (iota((CAP, ni), 0) == rank).astype(F32).astype(BF16)
    node = flat(node_ref[...]).astype(F32)
    cell = flat(cell_ref[...])
    weight = jnp.where(lane_of_slot < live_ref[0], flat(weight_ref[...]), 0.0)
    w0, w1, w2 = three(weight)
    which = iota((8, ni), 0)
    meta = jnp.zeros((8, ni), F32)
    for row, values in enumerate(
        (((cell >> 7) << 7).astype(F32), (cell & 127).astype(F32), node, w0.astype(F32), w1.astype(F32), w2.astype(F32))
    ):
        meta = jnp.where(which == row, values, meta)
    owner_row = flat(owner)
    lhs = jnp.concatenate([jnp.where(owner_row == g, meta, 0.0) for g in range(n_sub)], axis=0).astype(BF16)
    placed = nt(lhs, rank_hot)
    for g in range(n_sub):
        mt[g] = placed[g * 8 : (g + 1) * 8]
    for load in loads[5:]:
        load.wait()
    v = v_ref[...]
    win_v[2] = v[:, :128]
    win_v[3] = v[:, 128:]

    pl.semaphore_wait(barrier, n_sub - 1 + n_passage - 1)

    def exchange(win, k):
        to_right = sub_copy(win.at[pl.ds(2, 2)], win.at[pl.ds(0, 2)], nb_send.at[k, 0], nb_recv.at[k, 0], me + 1)
        to_left = sub_copy(win.at[pl.ds(2, 2)], win.at[pl.ds(4, 2)], nb_send.at[k, 1], nb_recv.at[k, 1], me - 1)

        def start():
            pl.when(has_right)(to_right.start)
            pl.when(has_left)(to_left.start)

        def arrive():
            pl.when(has_left)(to_right.wait_recv)
            pl.when(has_right)(to_left.wait_recv)

        def sent():
            pl.when(has_right)(to_right.wait_send)
            pl.when(has_left)(to_left.wait_send)

        return start, arrive, sent

    v_start, v_arrive, v_sent = exchange(win_v, 0)
    s_start, s_arrive, s_sent = exchange(win_s, 1)
    w_start, w_arrive, w_sent = exchange(win_w, 2)

    def out_copy(c, peer, slot):
        sent_rows = pl.ds(0, MC + 2 if c == 0 else MC)
        return sub_copy(
            out.at[c, peer, sent_rows], inc.at[c, slot, sent_rows], a_send.at[c, peer], a_recv.at[c, slot], peer
        )

    def back_copy(c, peer, slot):
        return sub_copy(ret.at[c, peer], back.at[c, slot], b_send.at[c, peer], b_recv.at[c, slot], peer)

    kept = pl.ds(0, rows)

    def gram_copy(peer, slot):
        return sub_copy(gbuf.at[peer, kept], grecv.at[slot, kept], g_send.at[peer], g_recv.at[slot], peer)

    def full_copy(peer, slot):
        return sub_copy(part.at[1, kept], gfull.at[slot, kept], f_send.at[peer], f_recv.at[slot], peer)

    def part_copy(peer, slot):
        return passage_copy(part.at[0, kept], precv.at[slot, kept], p_send.at[peer], p_recv.at[slot], peer)

    def far_first(k, count):
        half = (k + 1) // 2
        if isinstance(k, int):
            return count // 2 + (-half if k % 2 else half)
        return count // 2 + jnp.where(lax.rem(k, 2) == 1, -half, half)

    def each_sub(act):
        def step(k, carry):
            act(lax.rem(me + far_first(k, n_sub), n_sub))
            return carry

        for k in range(n_sub - 1):
            step(k, 0)

    def each_passage(act):
        def step(k, carry):
            act(lax.rem(myp + far_first(k, n_passage), n_passage))
            return carry

        for k in range(n_passage - 1):
            step(k, 0)

    def chip_to(t):
        return lax.rem(chip + far_first(t, chips), chips)

    v_start()
    departures = [v_sent]

    v3 = jnp.concatenate(three(v), axis=0)
    node_of = iota((NSD, 128), 0)

    def weight_row(g):
        return mt[g, 3:4, :] + mt[g, 4:5, :] + mt[g, 5:6, :]

    def send_step(t, carry):
        there = chip_to(t)
        parts = [(node_of == mt[2 * there + core, 2:3, :].astype(I32)).astype(F32) for core in range(2)]
        one_hot = jnp.concatenate(parts, axis=1).astype(BF16)
        n2[there] = one_hot
        picked = nn(v3, one_hot)
        picked = picked[0:M] + picked[M : 2 * M] + picked[2 * M :]
        for core in range(2):
            g = 2 * there + core
            values = picked[:, core * 128 : (core + 1) * 128] * weight_row(g)
            for c in range(CHUNKS):
                out[c, g, 0:MC, :] = values[c * MC : (c + 1) * MC]
            out[0, g, MC : MC + 2, :] = mt[g, 0:2, :]
            pl.when(g != me)(out_copy(0, g, me).start)
        return carry

    lax.fori_loop(0, chips, send_step, 0)
    inc[0, me, 0 : MC + 2] = out[0, me, 0 : MC + 2]

    for r in range(2):
        kb = kb_ref[r]
        high, low = two(kb)
        kbh[r] = high
        kbl[r] = low

    stiff = stiff_ref[...]

    def apply(win, own):
        mixed = []
        for r in range(2):
            blocks = jnp.concatenate([win[cols_ref[r, n]] for n in range(4)], axis=1)
            high, low = two(blocks)
            both = nn(jnp.concatenate([high, low], axis=0), kbh[r])
            mixed.append(both[:M] + both[M:] + nn(high, kbl[r]))
        return stiff * own + jnp.concatenate(mixed, axis=1)

    v_arrive()
    image = apply(win_v, v)
    win_s[2] = image[:, :128]
    win_s[3] = image[:, 128:]
    s_start()
    departures.append(s_sent)
    for c in range(1, CHUNKS):
        each_sub(lambda peer: out_copy(c - 1, peer, me).wait_send())
        each_sub(lambda peer: out_copy(c, peer, me).start())
        inc[c, me, 0:MC] = out[c, me, 0:MC]
    departures.append(lambda: each_sub(lambda peer: out_copy(CHUNKS - 1, peer, me).wait_send()))

    place = iota((512, 256), 0)

    def rows_of(there):
        high = jnp.concatenate([inc[0, 2 * there + k, MC : MC + 1, :] for k in range(2)], axis=1).astype(I32)
        low = jnp.concatenate([inc[0, 2 * there + k, MC + 1 : MC + 2, :] for k in range(2)], axis=1).astype(I32)
        return high >> 9, (high & 511) + low

    def each_source(there, act):
        for core in range(2):
            j = 2 * there + core
            pl.when(j != me)(functools.partial(act, j))

    def take(c):
        each_sub(lambda peer: out_copy(c, peer, peer).wait_recv())
        if c == 0:

            def mark(there, carry):
                row, column = rows_of(there)
                rhot[there] = (place == column).astype(F32).astype(BF16)
                rowf[there] = jnp.broadcast_to(row, (8, 256))
                return carry

            lax.fori_loop(0, chips, mark, 0)
        one_hot = jnp.concatenate([rhot[k] for k in range(chips)], axis=1)
        row = jnp.concatenate([rowf[k, 0:1, :] for k in range(chips)], axis=1)
        high, low = two(jnp.concatenate([inc[c, k, 0:MC, :] for k in range(n_sub)], axis=1))
        highs, lows = [], []
        for k in range(16):
            mask = jnp.broadcast_to((row == k).astype(F32), (MC, n_sub * CAP)).astype(BF16)
            highs.append(high * mask)
            lows.append(low * mask)
        terms = jnp.concatenate([jnp.concatenate(highs, axis=0), jnp.concatenate(lows, axis=0)], axis=1)
        product = nt(terms, jnp.concatenate([one_hot, one_hot], axis=1))
        for k in range(16):
            for q in range(4):
                s[c, k // 2, (k % 2) * 4 + q] = product[k * MC : (k + 1) * MC, q * 128 : (q + 1) * 128]

    x_right = [
        passage_copy(s.at[c, pl.ds(6, 2)], xl.at[c], x_send.at[c, 0], x_recv.at[c, 0], right_p) for c in range(CHUNKS)
    ]
    x_left = [
        passage_copy(s.at[c, pl.ds(0, 2)], xr.at[c], x_send.at[c, 1], x_recv.at[c, 1], left_p) for c in range(CHUNKS)
    ]
    for c in range(CHUNKS):
        take(c)
        x_right[c].start()
        x_left[c].start()
        departures += [x_right[c].wait_send, x_left[c].wait_send]

    s_arrive()
    image_image = apply(win_s, image)

    lane = iota((M, 128), 1)
    apart = jnp.abs(iota((128, 128), 0) - iota((128, 128), 1))
    at_end = (iota((128, 128), 0) == 0) | (iota((128, 128), 0) == 127)
    once = jnp.where(apart == 0, 1.0, jnp.where(apart == 1, 0.5, 0.0))
    middle_weight = jnp.where(at_end, 1.25, 1.5)
    twice = jnp.where(apart == 0, middle_weight, jnp.where(apart == 1, 1.0, jnp.where(apart == 2, 0.25, 0.0)))
    once = jnp.concatenate([once, once], axis=0).astype(BF16)
    twice = jnp.concatenate([twice, twice], axis=0).astype(BF16)

    def filters(c, layers):
        def layer(a, b):
            if a < 0:
                return xl[c, a + 2, b]
            if a >= CX:
                return xr[c, a - CX, b]
            return s[c, a, b]

        ps, qs = [], []
        for a in layers:
            for b in range(CY):
                near = layer(a - 1, b) + layer(a + 1, b)
                mine = layer(a, b)
                far = layer(a - 2, b) + layer(a + 2, b)
                ps.append(jnp.concatenate(two(mine + 0.5 * near), axis=1))
                qs.append(jnp.concatenate(two(1.5 * mine + near + 0.25 * far), axis=1))
        p = BETA * nn(jnp.concatenate(ps, axis=0), once)
        q = GAMMA * nn(jnp.concatenate(qs, axis=0), twice)
        for n, a in enumerate(layers):
            for b in range(CY):
                at = (n * CY + b) * MC
                pp[c, a, b] = p[at : at + MC]
                qq[c, a, b] = q[at : at + MC]

    y_right = [sub_copy(ysr.at[c], yl.at[c], y_send.at[c, 0], y_recv.at[c, 0], me + 1) for c in range(CHUNKS)]
    y_left = [sub_copy(ysl.at[c], yr.at[c], y_send.at[c, 1], y_recv.at[c, 1], me - 1) for c in range(CHUNKS)]
    for c in range(CHUNKS):
        filters(c, (2, 3, 4, 5))
        x_right[c].wait_recv()
        x_left[c].wait_recv()
        filters(c, (0, 1, 6, 7))

        for a in range(CX):
            ysr[c, 0, a] = 0.5 * pp[c, a, 7] + 0.25 * qq[c, a, 6] + qq[c, a, 7]
            ysr[c, 1, a] = 0.25 * qq[c, a, 7]
            ysl[c, 0, a] = 0.5 * pp[c, a, 0] + 0.25 * qq[c, a, 1] + qq[c, a, 0]
            ysl[c, 1, a] = 0.25 * qq[c, a, 0]
        pl.when(has_right)(y_right[c].start)
        pl.when(has_left)(y_left[c].start)
        departures.append(lambda c=c: pl.when(has_right)(y_right[c].wait_send))
        departures.append(lambda c=c: pl.when(has_left)(y_left[c].wait_send))

    end_left = jnp.where(has_left, 1.5, 1.25).astype(F32)
    end_right = jnp.where(has_right, 1.5, 1.25).astype(F32)

    def press(c):
        def step(a, carry):
            p = [pp[c, a, b] for b in range(CY)]
            q = [qq[c, a, b] for b in range(CY)]
            for b in range(CY):
                near_p = [p[k] for k in (b - 1, b + 1) if 0 <= k < CY]
                near_q = [q[k] for k in (b - 1, b + 1) if 0 <= k < CY]
                far_q = [q[k] for k in (b - 2, b + 2) if 0 <= k < CY]
                centre = end_left if b == 0 else end_right if b == CY - 1 else 1.5
                total = ALPHA * s[c, a, b] + p[b] + 0.5 * sum(near_p) + centre * q[b] + sum(near_q) + 0.25 * sum(far_q)
                if b < 2:
                    total = total + yl[c, b, a]
                if b >= CY - 2:
                    total = total + yr[c, CY - 1 - b, a]
                high, low = two(total)
                fp[2 * a + b // 4, :, (b % 4) * 128 : (b % 4 + 1) * 128] = high
                fp[2 * a + b // 4, :, 512 + (b % 4) * 128 : 512 + (b % 4 + 1) * 128] = low
            return carry

        lax.fori_loop(0, CX, step, 0)

    def give(c):
        fields = fp[...].reshape(16 * MC, 1024)
        for times in (range(chips // 2), range(chips // 2, chips)):
            one_hot = jnp.concatenate([rhot[chip_to(t)] for t in times], axis=1)
            row = jnp.concatenate([rowf[chip_to(t), 0:1, :] for t in times], axis=1)
            product = nn(fields, jnp.concatenate([one_hot, one_hot], axis=0))
            total = jnp.where(row == 0, product[0:MC], 0.0)
            for k in range(1, 16):
                total = jnp.where(row == k, product[k * MC : (k + 1) * MC], total)
            for n, t in enumerate(times):
                for core in range(2):
                    at = (2 * n + core) * 128
                    ret[c, 2 * chip_to(t) + core] = total[:, at : at + 128]
            for t in times:
                each_source(chip_to(t), lambda j: back_copy(c, j, me).start())
        back[c, me] = ret[c, me]

    for c in range(CHUNKS):
        pl.when(has_left)(y_right[c].wait_recv)
        pl.when(has_right)(y_left[c].wait_recv)
        press(c)
        give(c)
        departures.append(lambda c=c: each_sub(lambda peer: back_copy(c, peer, me).wait_send()))

    def forces(c):
        each_sub(lambda peer: back_copy(c, peer, peer).wait_recv())
        force = jnp.concatenate([back[c, k] * weight_row(k) for k in range(n_sub)], axis=1)
        product = nt(jnp.concatenate(three(force), axis=0), jnp.concatenate([n2[k] for k in range(chips)], axis=1))
        product = product[0:MC] + product[MC : 2 * MC] + product[2 * MC :]
        return mass_ref[...] * v[c * MC : (c + 1) * MC] + product

    massed = jnp.concatenate([forces(c) for c in range(CHUNKS)], axis=0)
    win_w[2] = massed[:, :128]
    win_w[3] = massed[:, 128:]
    w_start()
    departures.append(w_sent)
    w_arrive()
    image_massed = apply(win_w, massed)

    x_high, x_low = two(jnp.concatenate([v, image, massed], axis=0))
    z_high, z_low = two(
        jnp.concatenate([image, massed, image_image, image_massed, v, jnp.zeros((96, NSD), F32)], axis=0)
    )
    x_both = jnp.concatenate([x_high, x_low], axis=0)
    product = nt(x_both, z_high) + nt(x_both, z_low)
    product = product[:96] + product[96:]
    third = jnp.where(lane < M, product[0:32, 128:], product[64:96, :128])
    whole[0:64, :] = product[0:64, :128]
    whole[64:96, :] = third
    whole[96:128, :] = jnp.zeros((32, 128), F32)
    for g in range(n_sub):
        gbuf[g, 0:rows, :] = whole[g * rows : (g + 1) * rows, :]
    each_sub(lambda peer: gram_copy(peer, me).start())
    departures.append(lambda: each_sub(lambda peer: gram_copy(peer, me).wait_send()))
    grecv[me, 0:rows] = gbuf[me, 0:rows]
    each_sub(lambda peer: gram_copy(peer, peer).wait_recv())
    part[0, 0:rows] = sum(grecv[g, 0:rows] for g in range(n_sub))
    each_passage(lambda peer: part_copy(peer, myp).start())
    departures.append(lambda: each_passage(lambda peer: part_copy(peer, myp).wait_send()))
    precv[myp, 0:rows] = part[0, 0:rows]
    each_passage(lambda peer: part_copy(peer, peer).wait_recv())
    part[1, 0:rows] = sum(precv[g, 0:rows] for g in range(n_passage))
    each_sub(lambda peer: full_copy(peer, me).start())
    departures.append(lambda: each_sub(lambda peer: full_copy(peer, me).wait_send()))
    gfull[me, 0:rows] = part[1, 0:rows]
    each_sub(lambda peer: full_copy(peer, peer).wait_recv())

    for g in range(n_sub):
        whole[g * rows : (g + 1) * rows, :] = gfull[g, 0:rows, :]
    turned = whole[...].T
    scale = 1.0 / (NSD * n_sub * n_passage)
    row_of = iota((M, 128), 0)

    def moved(x, blocks):
        return pltpu.roll(x, (128 - 32 * blocks) % 128, 1)

    top, mid, bottom = whole[0:32], whole[32:64], whole[64:96]
    numer = jnp.where(lane == row_of, top, 0.0)
    denom = jnp.where(lane == row_of, moved(top, 1), 0.0)
    theta = jnp.sum(numer, axis=1, keepdims=True) / jnp.sum(denom, axis=1, keepdims=True)
    theta_row = jnp.sum(jnp.where(lane == row_of, theta, 0.0), axis=0, keepdims=True)
    resid_ref[...] = image - theta * massed
    mass_stiff = moved(turned[32:64], 1)
    plain_vr = top - moved(top, 1) * theta_row
    plain_rv = turned[0:32] - theta * turned[32:64]
    stiff_rs = mid - theta * mass_stiff
    plain_rr = stiff_rs - moved(mid, 1) * theta_row + theta * theta_row * moved(bottom, 1)
    stiff_vr = moved(top, 2) - moved(top, 3) * theta_row
    stiff_rr = (
        moved(mid, 2) - theta * moved(bottom, 2) - moved(mid, 3) * theta_row + theta * theta_row * moved(bottom, 3)
    )

    def side(first, second):
        return (jnp.where(lane < M, first, pltpu.roll(second, 32, 1)) * scale)[:, : 2 * M]

    gs_ref[0:M, :] = side(top, stiff_vr)
    gs_ref[M:, :] = side(stiff_rs, stiff_rr)
    gp_ref[0:M, :] = side(bottom, plain_vr)
    gp_ref[M:, :] = side(plain_rv, plain_rr)

    for sent in departures:
        sent()


def body(
    n_passage,
    n_sub,
    block_vectors,
    stiffness,
    mass_diag,
    kblocks,
    block_cols,
    slot_node,
    slot_owner,
    slot_cell,
    slot_weight,
    live_slots,
):
    nc = slot_node.shape[0] // 128
    chips = n_sub // 2
    rows = -(-3 * M // n_sub // 8) * 8
    shapes = (
        jax.ShapeDtypeStruct((M, NSD), F32),
        jax.ShapeDtypeStruct((2 * M, 2 * M), F32),
        jax.ShapeDtypeStruct((2 * M, 2 * M), F32),
    )
    vmem = pl.BlockSpec(memory_space=pltpu.VMEM)
    hbm = pl.BlockSpec(memory_space=pltpu.HBM)
    dma = pltpu.SemaphoreType.DMA
    layers = pltpu.VMEM((CHUNKS, 2, CY, MC, CZ), F32)
    cells = pltpu.VMEM((CHUNKS, CX, CY, MC, CZ), F32)
    return pl.pallas_call(
        functools.partial(kernel, n_passage, n_sub),
        out_shape=shapes,
        in_specs=[hbm] * 10,
        out_specs=(vmem, vmem, vmem),
        scratch_shapes=[
            pltpu.VMEM((M, NSD), F32),
            pltpu.VMEM((1, NSD), F32),
            pltpu.VMEM((1, NSD), F32),
            pltpu.VMEM((2, 512, 128), F32),
            pltpu.SMEM((2, 4), I32),
            pltpu.VMEM((nc, 128), I32),
            pltpu.VMEM((nc, 128), I32),
            pltpu.VMEM((nc, 128), I32),
            pltpu.VMEM((nc, 128), F32),
            pltpu.SMEM((1,), I32),
            dma((10,)),
            pltpu.VMEM((6, M, 128), F32),
            pltpu.VMEM((6, M, 128), F32),
            pltpu.VMEM((6, M, 128), F32),
            pltpu.VMEM((2, 512, 128), BF16),
            pltpu.VMEM((2, 512, 128), BF16),
            pltpu.VMEM((n_sub, 8, 128), F32),
            pltpu.VMEM((chips, NSD, 256), BF16),
            pltpu.VMEM((CHUNKS, n_sub, MC + 8, CAP), F32),
            pltpu.VMEM((CHUNKS, n_sub, MC + 8, CAP), F32),
            pltpu.VMEM((chips, 512, 256), BF16),
            pltpu.VMEM((chips, 8, 256), I32),
            cells,
            layers,
            layers,
            cells,
            cells,
            layers,
            layers,
            layers,
            layers,
            pltpu.VMEM((16, MC, 1024), BF16),
            pltpu.VMEM((CHUNKS, n_sub, MC, CAP), F32),
            pltpu.VMEM((CHUNKS, n_sub, MC, CAP), F32),
            pltpu.VMEM((n_sub, rows, 128), F32),
            pltpu.VMEM((n_sub, rows, 128), F32),
            pltpu.VMEM((2, rows, 128), F32),
            pltpu.VMEM((n_passage, rows, 128), F32),
            pltpu.VMEM((n_sub, rows, 128), F32),
            pltpu.VMEM((128, 128), F32),
            dma((3, 2)),
            dma((3, 2)),
            dma((CHUNKS, n_sub)),
            dma((CHUNKS, n_sub)),
            dma((CHUNKS, 2)),
            dma((CHUNKS, 2)),
            dma((CHUNKS, 2)),
            dma((CHUNKS, 2)),
            dma((CHUNKS, n_sub)),
            dma((CHUNKS, n_sub)),
            dma((n_sub,)),
            dma((n_sub,)),
            dma((n_passage,)),
            dma((n_passage,)),
            dma((n_sub,)),
            dma((n_sub,)),
        ],
        compiler_params=pltpu.CompilerParams(
            collective_id=0, has_side_effects=True, vmem_limit_bytes=60 * 1024 * 1024
        ),
    )(
        block_vectors,
        stiffness.reshape(1, NSD),
        mass_diag.reshape(1, NSD),
        kblocks.reshape(2, 512, 128),
        block_cols,
        slot_node.reshape(nc, 128),
        slot_owner.reshape(nc, 128),
        slot_cell.reshape(nc, 128),
        slot_weight.reshape(nc, 128),
        live_slots,
    )


def solution(mesh):
    return jax.shard_map(
        functools.partial(body, mesh.shape["passage"], mesh.shape["sub"]),
        mesh=mesh,
        in_specs=(
            P(None, ("passage", "sub")),
            P(("passage", "sub")),
            P(("passage", "sub")),
            P(("passage", "sub"), None, None, None),
            P(("passage", "sub"), None),
            P(("passage", "sub")),
            P(("passage", "sub"), None),
            P(("passage", "sub")),
            P(("passage", "sub")),
            P(("passage", "sub")),
        ),
        out_specs=(P(None, ("passage", "sub")), P(), P()),
        check_vma=False,
    )
```

```python
import functools

import jax
import jax.numpy as jnp
from jax import lax
from jax.experimental import pallas as pl
from jax.experimental.pallas import tpu as pltpu
from jax.sharding import PartitionSpec as P

MESH = pl.DeviceIdType.MESH
F32 = jnp.float32
BF16 = jnp.bfloat16
I32 = jnp.int32

M = 32
CX = 8
CY = 8
CZ = 128
CAP = 128
NSD = 256
CHUNKS = 2
MC = M // CHUNKS

center_weight = 15.0
lower_bound = 1.0 / 15.0
upper_bound = 17.0 / 15.0
middle = (upper_bound + lower_bound) / 2.0
radius = (upper_bound - lower_bound) / 2.0
sigma_ratio = middle / radius
first_rho = 1.0 / sigma_ratio
second_rho = 1.0 / (2.0 * sigma_ratio - first_rho)
third_rho = 1.0 / (2.0 * sigma_ratio - second_rho)
FIRST = 1.0 / (center_weight * middle)
GAIN_TWO = 2.0 * second_rho / radius / center_weight
GAIN_THREE = 2.0 * third_rho / radius / center_weight
STEP_ONE = second_rho * first_rho * FIRST + GAIN_TWO * (1.0 - 17.0 * FIRST)
STEP_T = GAIN_TWO * 2.0 * FIRST
ALPHA = FIRST + STEP_ONE + third_rho * second_rho * STEP_ONE + GAIN_THREE * (1.0 - 17.0 * (FIRST + STEP_ONE))
BETA = STEP_T + third_rho * second_rho * STEP_T + GAIN_THREE * (2.0 * (FIRST + STEP_ONE) - 17.0 * STEP_T)
GAMMA = GAIN_THREE * 2.0 * STEP_T


def iota(shape, dim):
    return lax.broadcasted_iota(I32, shape, dim)


def nn(left, right):
    return jnp.dot(left, right, preferred_element_type=F32)


def nt(left, right):
    return lax.dot_general(left, right, (((1,), (1,)), ((), ())), preferred_element_type=F32)


def two(x):
    high = x.astype(BF16)
    return high, (x - high.astype(F32)).astype(BF16)


def three(x):
    high, rest = x.astype(BF16), None
    rest = x - high.astype(F32)
    middle_part = rest.astype(BF16)
    return high, middle_part, (rest - middle_part.astype(F32)).astype(BF16)


def kernel(
    n_passage,
    n_sub,
    v_hbm,
    stiff_hbm,
    mass_hbm,
    kb_hbm,
    cols_hbm,
    node_hbm,
    owner_hbm,
    cell_hbm,
    weight_hbm,
    live_hbm,
    resid_ref,
    gs_ref,
    gp_ref,
    v_ref,
    stiff_ref,
    mass_ref,
    kb_ref,
    cols_ref,
    node_ref,
    owner_ref,
    cell_ref,
    weight_ref,
    live_ref,
    in_sem,
    win_v,
    win_s,
    win_w,
    kbh,
    kbl,
    mt,
    n2,
    out,
    inc,
    rhot,
    rowf,
    s,
    xl,
    xr,
    pp,
    qq,
    ysl,
    ysr,
    yl,
    yr,
    fp,
    ret,
    back,
    gbuf,
    grecv,
    part,
    precv,
    gfull,
    whole,
    nb_send,
    nb_recv,
    a_send,
    a_recv,
    x_send,
    x_recv,
    y_send,
    y_recv,
    b_send,
    b_recv,
    g_send,
    g_recv,
    p_send,
    p_recv,
    f_send,
    f_recv,
):
    chips = n_sub // 2
    ni = node_ref.shape[0] * 128
    nc = node_ref.shape[0]
    rows = 3 * M // n_sub
    myp = lax.axis_index("passage")
    me = lax.axis_index("sub")
    chip = me // 2
    left_p = lax.rem(myp + n_passage - 1, n_passage)
    right_p = lax.rem(myp + 1, n_passage)
    has_left = me > 0
    has_right = me < n_sub - 1

    def sub_copy(src, dst, send, recv, peer):
        return pltpu.make_async_remote_copy(
            src_ref=src, dst_ref=dst, send_sem=send, recv_sem=recv,
            device_id={"sub": peer}, device_id_type=MESH,
        )

    def passage_copy(src, dst, send, recv, peer):
        return pltpu.make_async_remote_copy(
            src_ref=src, dst_ref=dst, send_sem=send, recv_sem=recv,
            device_id={"passage": peer}, device_id_type=MESH,
        )

    arguments = (
        (node_hbm, node_ref),
        (owner_hbm, owner_ref),
        (cell_hbm, cell_ref),
        (weight_hbm, weight_ref),
        (live_hbm, live_ref),
        (v_hbm, v_ref),
        (kb_hbm, kb_ref),
        (stiff_hbm, stiff_ref),
        (mass_hbm, mass_ref),
        (cols_hbm, cols_ref),
    )
    loads = [pltpu.make_async_copy(src, dst, in_sem.at[k]) for k, (src, dst) in enumerate(arguments)]
    for load in loads:
        load.start()

    for win in (win_v, win_s, win_w):
        win[0:2] = jnp.zeros((2, M, 128), F32)
        win[4:6] = jnp.zeros((2, M, 128), F32)

    @pl.when(jnp.logical_not(has_left))
    def _():
        yl[...] = jnp.zeros_like(yl)

    @pl.when(jnp.logical_not(has_right))
    def _():
        yr[...] = jnp.zeros_like(yr)

    barrier = pltpu.get_barrier_semaphore()

    def greet_sub(i, carry):
        pl.semaphore_signal(barrier, inc=1, device_id={"sub": lax.rem(me + i, n_sub)}, device_id_type=MESH)
        return carry

    def greet_passage(i, carry):
        pl.semaphore_signal(barrier, inc=1, device_id={"passage": lax.rem(myp + i, n_passage)}, device_id_type=MESH)
        return carry

    lax.fori_loop(1, n_sub, greet_sub, 0)
    lax.fori_loop(1, n_passage, greet_passage, 0)

    for load in loads[:5]:
        load.wait()

    owner = owner_ref[...]
    lane_of_slot = iota((1, ni), 1)

    def flat(x):
        return jnp.concatenate([x[c : c + 1, :] for c in range(nc)], axis=1)

    group = iota((n_sub, 128), 0)
    hot = [(owner[c : c + 1, :] == group).astype(F32) for c in range(nc)]
    upper = (iota((128, 128), 0) < iota((128, 128), 1)).astype(F32).astype(BF16)
    before = nn(jnp.concatenate(hot, axis=0).astype(BF16), upper)
    ahead = jnp.zeros((n_sub, 1), F32)
    ranks = []
    for c in range(nc):
        ranks.append(jnp.sum(hot[c] * (before[c * n_sub : (c + 1) * n_sub] + ahead), axis=0, keepdims=True))
        ahead = ahead + jnp.sum(hot[c], axis=1, keepdims=True)
    rank = jnp.concatenate(ranks, axis=1).astype(I32)
    rank_hot = (iota((CAP, ni), 0) == rank).astype(F32).astype(BF16)
    node = flat(node_ref[...]).astype(F32)
    cell = flat(cell_ref[...])
    weight = jnp.where(lane_of_slot < live_ref[0], flat(weight_ref[...]), 0.0)
    w0, w1, w2 = three(weight)
    which = iota((8, ni), 0)
    meta = jnp.zeros((8, ni), F32)
    for row, values in enumerate(
        (((cell >> 7) << 7).astype(F32), (cell & 127).astype(F32), node, w0.astype(F32), w1.astype(F32), w2.astype(F32))
    ):
        meta = jnp.where(which == row, values, meta)
    owner_row = flat(owner)
    lhs = jnp.concatenate([jnp.where(owner_row == g, meta, 0.0) for g in range(n_sub)], axis=0).astype(BF16)
    placed = nt(lhs, rank_hot)
    for g in range(n_sub):
        mt[g] = placed[g * 8 : (g + 1) * 8]
    for load in loads[5:]:
        load.wait()
    v = v_ref[...]
    win_v[2] = v[:, :128]
    win_v[3] = v[:, 128:]

    pl.semaphore_wait(barrier, n_sub - 1 + n_passage - 1)

    def exchange(win, k):
        to_right = sub_copy(win.at[pl.ds(2, 2)], win.at[pl.ds(0, 2)], nb_send.at[k, 0], nb_recv.at[k, 0], me + 1)
        to_left = sub_copy(win.at[pl.ds(2, 2)], win.at[pl.ds(4, 2)], nb_send.at[k, 1], nb_recv.at[k, 1], me - 1)

        def start():
            pl.when(has_right)(to_right.start)
            pl.when(has_left)(to_left.start)

        def arrive():
            pl.when(has_left)(to_right.wait_recv)
            pl.when(has_right)(to_left.wait_recv)

        def sent():
            pl.when(has_right)(to_right.wait_send)
            pl.when(has_left)(to_left.wait_send)

        return start, arrive, sent

    v_start, v_arrive, v_sent = exchange(win_v, 0)
    s_start, s_arrive, s_sent = exchange(win_s, 1)
    w_start, w_arrive, w_sent = exchange(win_w, 2)

    def out_copy(c, peer, slot):
        sent_rows = pl.ds(0, MC + 2 if c == 0 else MC)
        return sub_copy(
            out.at[c, peer, sent_rows], inc.at[c, slot, sent_rows], a_send.at[c, peer], a_recv.at[c, slot], peer
        )

    def back_copy(c, peer, slot):
        return sub_copy(ret.at[c, peer], back.at[c, slot], b_send.at[c, peer], b_recv.at[c, slot], peer)

    kept = pl.ds(0, rows)

    def gram_copy(peer, slot):
        return sub_copy(gbuf.at[peer, kept], grecv.at[slot, kept], g_send.at[peer], g_recv.at[slot], peer)

    def full_copy(peer, slot):
        return sub_copy(part.at[1, kept], gfull.at[slot, kept], f_send.at[peer], f_recv.at[slot], peer)

    def part_copy(peer, slot):
        return passage_copy(part.at[0, kept], precv.at[slot, kept], p_send.at[peer], p_recv.at[slot], peer)

    def far_first(k, count):
        half = (k + 1) // 2
        if isinstance(k, int):
            return count // 2 + (-half if k % 2 else half)
        return count // 2 + jnp.where(lax.rem(k, 2) == 1, -half, half)

    def each_sub(act):
        def step(k, carry):
            act(lax.rem(me + far_first(k, n_sub), n_sub))
            return carry

        for k in range(n_sub - 1):
            step(k, 0)

    def each_passage(act):
        def hops(i):
            return min(i // 8, 4 - i // 8) + min(i % 8, 8 - i % 8)

        for i in sorted(range(1, n_passage), key=hops, reverse=True):
            act(lax.rem(myp + i, n_passage))

    def chip_to(t):
        return lax.rem(chip + far_first(t, chips), chips)

    v_start()
    departures = [v_sent]

    v3 = jnp.concatenate(three(v), axis=0)
    node_of = iota((NSD, 128), 0)

    def weight_row(g):
        return mt[g, 3:4, :] + mt[g, 4:5, :] + mt[g, 5:6, :]

    def send_step(t, carry):
        there = chip_to(t)
        parts = [(node_of == mt[2 * there + core, 2:3, :].astype(I32)).astype(F32) for core in range(2)]
        one_hot = jnp.concatenate(parts, axis=1).astype(BF16)
        n2[there] = one_hot
        picked = nn(v3, one_hot)
        picked = picked[0:M] + picked[M : 2 * M] + picked[2 * M :]
        for core in range(2):
            g = 2 * there + core
            values = picked[:, core * 128 : (core + 1) * 128] * weight_row(g)
            for c in range(CHUNKS):
                out[c, g, 0:MC, :] = values[c * MC : (c + 1) * MC]
            out[0, g, MC : MC + 2, :] = mt[g, 0:2, :]
            pl.when(g != me)(out_copy(0, g, me).start)
        return carry

    lax.fori_loop(0, chips, send_step, 0)
    inc[0, me, 0 : MC + 2] = out[0, me, 0 : MC + 2]

    for r in range(2):
        kb = kb_ref[r]
        high, low = two(kb)
        kbh[r] = high
        kbl[r] = low

    stiff = stiff_ref[...]

    def apply(win, own):
        mixed = []
        for r in range(2):
            blocks = jnp.concatenate([win[cols_ref[r, n]] for n in range(4)], axis=1)
            high, low = two(blocks)
            both = nn(jnp.concatenate([high, low], axis=0), kbh[r])
            mixed.append(both[:M] + both[M:] + nn(high, kbl[r]))
        return stiff * own + jnp.concatenate(mixed, axis=1)

    v_arrive()
    image = apply(win_v, v)
    win_s[2] = image[:, :128]
    win_s[3] = image[:, 128:]
    s_start()
    departures.append(s_sent)
    for c in range(1, CHUNKS):
        each_sub(lambda peer: out_copy(c - 1, peer, me).wait_send())
        each_sub(lambda peer: out_copy(c, peer, me).start())
        inc[c, me, 0:MC] = out[c, me, 0:MC]
    departures.append(lambda: each_sub(lambda peer: out_copy(CHUNKS - 1, peer, me).wait_send()))

    place = iota((512, 256), 0)

    def rows_of(there):
        high = jnp.concatenate([inc[0, 2 * there + k, MC : MC + 1, :] for k in range(2)], axis=1).astype(I32)
        low = jnp.concatenate([inc[0, 2 * there + k, MC + 1 : MC + 2, :] for k in range(2)], axis=1).astype(I32)
        return high >> 9, (high & 511) + low

    def each_source(there, act):
        for core in range(2):
            j = 2 * there + core
            pl.when(j != me)(functools.partial(act, j))

    def take(c):
        each_sub(lambda peer: out_copy(c, peer, peer).wait_recv())
        if c == 0:

            def mark(there, carry):
                row, column = rows_of(there)
                rhot[there] = (place == column).astype(F32).astype(BF16)
                rowf[there] = jnp.broadcast_to(row, (8, 256))
                return carry

            lax.fori_loop(0, chips, mark, 0)
        one_hot = jnp.concatenate([rhot[k] for k in range(chips)], axis=1)
        row = jnp.concatenate([rowf[k, 0:1, :] for k in range(chips)], axis=1)
        high, low = two(jnp.concatenate([inc[c, k, 0:MC, :] for k in range(n_sub)], axis=1))
        highs, lows = [], []
        for k in range(16):
            mask = jnp.broadcast_to((row == k).astype(F32), (MC, n_sub * CAP)).astype(BF16)
            highs.append(high * mask)
            lows.append(low * mask)
        terms = jnp.concatenate([jnp.concatenate(highs, axis=0), jnp.concatenate(lows, axis=0)], axis=1)
        product = nt(terms, jnp.concatenate([one_hot, one_hot], axis=1))
        for k in range(16):
            for q in range(4):
                s[c, k // 2, (k % 2) * 4 + q] = product[k * MC : (k + 1) * MC, q * 128 : (q + 1) * 128]

    x_right = [
        passage_copy(s.at[c, pl.ds(6, 2)], xl.at[c], x_send.at[c, 0], x_recv.at[c, 0], right_p) for c in range(CHUNKS)
    ]
    x_left = [
        passage_copy(s.at[c, pl.ds(0, 2)], xr.at[c], x_send.at[c, 1], x_recv.at[c, 1], left_p) for c in range(CHUNKS)
    ]
    for c in range(CHUNKS):
        take(c)
        x_right[c].start()
        x_left[c].start()
        departures += [x_right[c].wait_send, x_left[c].wait_send]

    s_arrive()
    image_image = apply(win_s, image)

    lane = iota((M, 128), 1)
    apart = jnp.abs(iota((128, 128), 0) - iota((128, 128), 1))
    at_end = (iota((128, 128), 0) == 0) | (iota((128, 128), 0) == 127)
    once = jnp.where(apart == 0, 1.0, jnp.where(apart == 1, 0.5, 0.0))
    middle_weight = jnp.where(at_end, 1.25, 1.5)
    twice = jnp.where(apart == 0, middle_weight, jnp.where(apart == 1, 1.0, jnp.where(apart == 2, 0.25, 0.0)))
    once = jnp.concatenate([once, once], axis=0).astype(BF16)
    twice = jnp.concatenate([twice, twice], axis=0).astype(BF16)

    def filters(c, layers):
        def layer(a, b):
            if a < 0:
                return xl[c, a + 2, b]
            if a >= CX:
                return xr[c, a - CX, b]
            return s[c, a, b]

        ps, qs = [], []
        for a in layers:
            for b in range(CY):
                near = layer(a - 1, b) + layer(a + 1, b)
                mine = layer(a, b)
                far = layer(a - 2, b) + layer(a + 2, b)
                ps.append(jnp.concatenate(two(mine + 0.5 * near), axis=1))
                qs.append(jnp.concatenate(two(1.5 * mine + near + 0.25 * far), axis=1))
        p = BETA * nn(jnp.concatenate(ps, axis=0), once)
        q = GAMMA * nn(jnp.concatenate(qs, axis=0), twice)
        for n, a in enumerate(layers):
            for b in range(CY):
                at = (n * CY + b) * MC
                pp[c, a, b] = p[at : at + MC]
                qq[c, a, b] = q[at : at + MC]

    y_right = [sub_copy(ysr.at[c], yl.at[c], y_send.at[c, 0], y_recv.at[c, 0], me + 1) for c in range(CHUNKS)]
    y_left = [sub_copy(ysl.at[c], yr.at[c], y_send.at[c, 1], y_recv.at[c, 1], me - 1) for c in range(CHUNKS)]
    for c in range(CHUNKS):
        filters(c, (2, 3, 4, 5))
        x_right[c].wait_recv()
        x_left[c].wait_recv()
        filters(c, (0, 1, 6, 7))

        for a in range(CX):
            ysr[c, 0, a] = 0.5 * pp[c, a, 7] + 0.25 * qq[c, a, 6] + qq[c, a, 7]
            ysr[c, 1, a] = 0.25 * qq[c, a, 7]
            ysl[c, 0, a] = 0.5 * pp[c, a, 0] + 0.25 * qq[c, a, 1] + qq[c, a, 0]
            ysl[c, 1, a] = 0.25 * qq[c, a, 0]
        pl.when(has_right)(y_right[c].start)
        pl.when(has_left)(y_left[c].start)
        departures.append(lambda c=c: pl.when(has_right)(y_right[c].wait_send))
        departures.append(lambda c=c: pl.when(has_left)(y_left[c].wait_send))

    end_left = jnp.where(has_left, 1.5, 1.25).astype(F32)
    end_right = jnp.where(has_right, 1.5, 1.25).astype(F32)

    def press(c):
        def step(a, carry):
            p = [pp[c, a, b] for b in range(CY)]
            q = [qq[c, a, b] for b in range(CY)]
            for b in range(CY):
                near_p = [p[k] for k in (b - 1, b + 1) if 0 <= k < CY]
                near_q = [q[k] for k in (b - 1, b + 1) if 0 <= k < CY]
                far_q = [q[k] for k in (b - 2, b + 2) if 0 <= k < CY]
                centre = end_left if b == 0 else end_right if b == CY - 1 else 1.5
                total = ALPHA * s[c, a, b] + p[b] + 0.5 * sum(near_p) + centre * q[b] + sum(near_q) + 0.25 * sum(far_q)
                if b < 2:
                    total = total + yl[c, b, a]
                if b >= CY - 2:
                    total = total + yr[c, CY - 1 - b, a]
                high, low = two(total)
                fp[2 * a + b // 4, :, (b % 4) * 128 : (b % 4 + 1) * 128] = high
                fp[2 * a + b // 4, :, 512 + (b % 4) * 128 : 512 + (b % 4 + 1) * 128] = low
            return carry

        lax.fori_loop(0, CX, step, 0)

    def give(c):
        fields = fp[...].reshape(16 * MC, 1024)
        for times in (range(chips // 2), range(chips // 2, chips)):
            one_hot = jnp.concatenate([rhot[chip_to(t)] for t in times], axis=1)
            row = jnp.concatenate([rowf[chip_to(t), 0:1, :] for t in times], axis=1)
            product = nn(fields, jnp.concatenate([one_hot, one_hot], axis=0))
            total = jnp.where(row == 0, product[0:MC], 0.0)
            for k in range(1, 16):
                total = jnp.where(row == k, product[k * MC : (k + 1) * MC], total)
            for n, t in enumerate(times):
                for core in range(2):
                    at = (2 * n + core) * 128
                    ret[c, 2 * chip_to(t) + core] = total[:, at : at + 128]
            for t in times:
                each_source(chip_to(t), lambda j: back_copy(c, j, me).start())
        back[c, me] = ret[c, me]

    for c in range(CHUNKS):
        pl.when(has_left)(y_right[c].wait_recv)
        pl.when(has_right)(y_left[c].wait_recv)
        press(c)
        give(c)
        departures.append(lambda c=c: each_sub(lambda peer: back_copy(c, peer, me).wait_send()))

    def forces(c):
        each_sub(lambda peer: back_copy(c, peer, peer).wait_recv())
        force = jnp.concatenate([back[c, k] * weight_row(k) for k in range(n_sub)], axis=1)
        product = nt(jnp.concatenate(three(force), axis=0), jnp.concatenate([n2[k] for k in range(chips)], axis=1))
        product = product[0:MC] + product[MC : 2 * MC] + product[2 * MC :]
        return mass_ref[...] * v[c * MC : (c + 1) * MC] + product

    massed = jnp.concatenate([forces(c) for c in range(CHUNKS)], axis=0)
    win_w[2] = massed[:, :128]
    win_w[3] = massed[:, 128:]
    w_start()
    departures.append(w_sent)
    w_arrive()
    image_massed = apply(win_w, massed)

    x_high, x_low = two(jnp.concatenate([v, image, massed], axis=0))
    z_high, z_low = two(
        jnp.concatenate([image, massed, image_image, image_massed, v, jnp.zeros((96, NSD), F32)], axis=0)
    )
    x_both = jnp.concatenate([x_high, x_low], axis=0)
    product = nt(x_both, z_high) + nt(x_both, z_low)
    product = product[:96] + product[96:]
    third = jnp.where(lane < M, product[0:32, 128:], product[64:96, :128])
    whole[0:64, :] = product[0:64, :128]
    whole[64:96, :] = third
    whole[96:128, :] = jnp.zeros((32, 128), F32)
    for g in range(n_sub):
        gbuf[g, 0:rows, :] = whole[g * rows : (g + 1) * rows, :]
    each_sub(lambda peer: gram_copy(peer, me).start())
    for sent in departures:
        sent()
    departures = [lambda: each_sub(lambda peer: gram_copy(peer, me).wait_send())]
    grecv[me, 0:rows] = gbuf[me, 0:rows]
    each_sub(lambda peer: gram_copy(peer, peer).wait_recv())
    part[0, 0:rows] = sum(grecv[g, 0:rows] for g in range(n_sub))
    each_passage(lambda peer: part_copy(peer, myp).start())
    for sent in departures:
        sent()
    departures = [lambda: each_passage(lambda peer: part_copy(peer, myp).wait_send())]
    precv[myp, 0:rows] = part[0, 0:rows]
    each_passage(lambda peer: part_copy(peer, peer).wait_recv())
    part[1, 0:rows] = sum(precv[g, 0:rows] for g in range(n_passage))
    each_sub(lambda peer: full_copy(peer, me).start())
    for sent in departures:
        sent()
    departures = [lambda: each_sub(lambda peer: full_copy(peer, me).wait_send())]
    gfull[me, 0:rows] = part[1, 0:rows]
    each_sub(lambda peer: full_copy(peer, peer).wait_recv())

    for g in range(n_sub):
        whole[g * rows : (g + 1) * rows, :] = gfull[g, 0:rows, :]
    turned = whole[...].T
    scale = 1.0 / (NSD * n_sub * n_passage)
    row_of = iota((M, 128), 0)

    def moved(x, blocks):
        return pltpu.roll(x, (128 - 32 * blocks) % 128, 1)

    top, mid, bottom = whole[0:32], whole[32:64], whole[64:96]
    numer = jnp.where(lane == row_of, top, 0.0)
    denom = jnp.where(lane == row_of, moved(top, 1), 0.0)
    theta = jnp.sum(numer, axis=1, keepdims=True) / jnp.sum(denom, axis=1, keepdims=True)
    theta_row = jnp.sum(jnp.where(lane == row_of, theta, 0.0), axis=0, keepdims=True)
    resid_ref[...] = image - theta * massed
    mass_stiff = moved(turned[32:64], 1)
    plain_vr = top - moved(top, 1) * theta_row
    plain_rv = turned[0:32] - theta * turned[32:64]
    stiff_rs = mid - theta * mass_stiff
    plain_rr = stiff_rs - moved(mid, 1) * theta_row + theta * theta_row * moved(bottom, 1)
    stiff_vr = moved(top, 2) - moved(top, 3) * theta_row
    stiff_rr = (
        moved(mid, 2) - theta * moved(bottom, 2) - moved(mid, 3) * theta_row + theta * theta_row * moved(bottom, 3)
    )

    def side(first, second):
        return (jnp.where(lane < M, first, pltpu.roll(second, 32, 1)) * scale)[:, : 2 * M]

    gs_ref[0:M, :] = side(top, stiff_vr)
    gs_ref[M:, :] = side(stiff_rs, stiff_rr)
    gp_ref[0:M, :] = side(bottom, plain_vr)
    gp_ref[M:, :] = side(plain_rv, plain_rr)

    for sent in departures:
        sent()


def body(
    n_passage,
    n_sub,
    block_vectors,
    stiffness,
    mass_diag,
    kblocks,
    block_cols,
    slot_node,
    slot_owner,
    slot_cell,
    slot_weight,
    live_slots,
):
    nc = slot_node.shape[0] // 128
    chips = n_sub // 2
    rows = -(-3 * M // n_sub // 8) * 8
    shapes = (
        jax.ShapeDtypeStruct((M, NSD), F32),
        jax.ShapeDtypeStruct((2 * M, 2 * M), F32),
        jax.ShapeDtypeStruct((2 * M, 2 * M), F32),
    )
    vmem = pl.BlockSpec(memory_space=pltpu.VMEM)
    hbm = pl.BlockSpec(memory_space=pltpu.HBM)
    dma = pltpu.SemaphoreType.DMA
    layers = pltpu.VMEM((CHUNKS, 2, CY, MC, CZ), F32)
    cells = pltpu.VMEM((CHUNKS, CX, CY, MC, CZ), F32)
    return pl.pallas_call(
        functools.partial(kernel, n_passage, n_sub),
        out_shape=shapes,
        in_specs=[hbm] * 10,
        out_specs=(vmem, vmem, vmem),
        scratch_shapes=[
            pltpu.VMEM((M, NSD), F32),
            pltpu.VMEM((1, NSD), F32),
            pltpu.VMEM((1, NSD), F32),
            pltpu.VMEM((2, 512, 128), F32),
            pltpu.SMEM((2, 4), I32),
            pltpu.VMEM((nc, 128), I32),
            pltpu.VMEM((nc, 128), I32),
            pltpu.VMEM((nc, 128), I32),
            pltpu.VMEM((nc, 128), F32),
            pltpu.SMEM((1,), I32),
            dma((10,)),
            pltpu.VMEM((6, M, 128), F32),
            pltpu.VMEM((6, M, 128), F32),
            pltpu.VMEM((6, M, 128), F32),
            pltpu.VMEM((2, 512, 128), BF16),
            pltpu.VMEM((2, 512, 128), BF16),
            pltpu.VMEM((n_sub, 8, 128), F32),
            pltpu.VMEM((chips, NSD, 256), BF16),
            pltpu.VMEM((CHUNKS, n_sub, MC + 8, CAP), F32),
            pltpu.VMEM((CHUNKS, n_sub, MC + 8, CAP), F32),
            pltpu.VMEM((chips, 512, 256), BF16),
            pltpu.VMEM((chips, 8, 256), I32),
            cells,
            layers,
            layers,
            cells,
            cells,
            layers,
            layers,
            layers,
            layers,
            pltpu.VMEM((16, MC, 1024), BF16),
            pltpu.VMEM((CHUNKS, n_sub, MC, CAP), F32),
            pltpu.VMEM((CHUNKS, n_sub, MC, CAP), F32),
            pltpu.VMEM((n_sub, rows, 128), F32),
            pltpu.VMEM((n_sub, rows, 128), F32),
            pltpu.VMEM((2, rows, 128), F32),
            pltpu.VMEM((n_passage, rows, 128), F32),
            pltpu.VMEM((n_sub, rows, 128), F32),
            pltpu.VMEM((128, 128), F32),
            dma((3, 2)),
            dma((3, 2)),
            dma((CHUNKS, n_sub)),
            dma((CHUNKS, n_sub)),
            dma((CHUNKS, 2)),
            dma((CHUNKS, 2)),
            dma((CHUNKS, 2)),
            dma((CHUNKS, 2)),
            dma((CHUNKS, n_sub)),
            dma((CHUNKS, n_sub)),
            dma((n_sub,)),
            dma((n_sub,)),
            dma((n_passage,)),
            dma((n_passage,)),
            dma((n_sub,)),
            dma((n_sub,)),
        ],
        compiler_params=pltpu.CompilerParams(
            collective_id=0, has_side_effects=True, vmem_limit_bytes=60 * 1024 * 1024
        ),
    )(
        block_vectors,
        stiffness.reshape(1, NSD),
        mass_diag.reshape(1, NSD),
        kblocks.reshape(2, 512, 128),
        block_cols,
        slot_node.reshape(nc, 128),
        slot_owner.reshape(nc, 128),
        slot_cell.reshape(nc, 128),
        slot_weight.reshape(nc, 128),
        live_slots,
    )


def solution(mesh):
    return jax.shard_map(
        functools.partial(body, mesh.shape["passage"], mesh.shape["sub"]),
        mesh=mesh,
        in_specs=(
            P(None, ("passage", "sub")),
            P(("passage", "sub")),
            P(("passage", "sub")),
            P(("passage", "sub"), None, None, None),
            P(("passage", "sub"), None),
            P(("passage", "sub")),
            P(("passage", "sub"), None),
            P(("passage", "sub")),
            P(("passage", "sub")),
            P(("passage", "sub")),
        ),
        out_specs=(P(None, ("passage", "sub")), P(), P()),
        check_vma=False,
    )
```
